32 devices in a mesh: groups: 2 (over x), gx: 4 (over z), gy: 4 (over y, core).
Axes of the slice: x: 2, y: 2, z: 4, core: 2. Of those that a mesh axis runs over, the one named last changes fastest.
Arguments:
- tokens: bfloat16 [16, 4, 2, 9216], P('groups', 'gx', None, 'gy'), parts along dimension 0, may hold values from -6 to 6
- gain: float32 [9216], P('gy'), may hold values from 0.1 to 1.9
- w_query: bfloat16 [9216, 6144], P('gy', 'gx'), may hold values from -0.15625 to 0.15625
- w_keyval: bfloat16 [9216, 512], P('gy', 'gx'), may hold values from -0.0625 to 0.0625
- w_gate: bfloat16 [9216, 36864], P('gy', 'gx'), may hold values from -0.0625 to 0.0625
- w_up: bfloat16 [9216, 36864], P('gy', 'gx'), may hold values from -0.0625 to 0.0625
- cache: bfloat16 [16, 4, 1024, 512], P(('groups', 'gy'), 'gx'), parts along dimension 0, may hold values from -40 to 40
- lengths: int32 [16, 4], P(('groups', 'gy'), 'gx'), parts along dimension 0, may hold values from 1 to 1024, as said below
Outputs:
- context: bfloat16 [16, 4, 2, 6144], P(('groups', 'gy'), 'gx'), parts along dimension 0
- hidden: bfloat16 [16, 4, 2, 36864], P(('groups', 'gy'), None, None, 'gx'), parts along dimension 0
The draws below stay inside these ranges and needn't reach their ends.
There are 2 independent parts, one for each index of `groups`. The reference program is written for one: setup_inputs(seed, part) draws one part's arguments, and reference() takes and returns one part's arrays. A program takes and returns all parts, laid end to end along the dimension named above; an argument that names none is the same for every part. Nothing has to cross between parts.
Inputs may be any that keep to these rules, and one draw needn't show every extreme that they name: `lengths`: the largest of each draw is exactly 1024.
All inputs are finite; a program needn't handle non-finite values.
Results may differ from the reference program's by a relative error of at most 0.012.
The reference program's roundings to bfloat16 on the way count: a program that leaves them out, or rounds other values in their place, can miss the bound.
Values may be sent and summed in bfloat16 or wider, within the bound.
No kernel may reach another device: no remote copies, remote signals or barrier semaphores. Data moves between devices by JAX's collectives and lax.ppermute only.
A program may use at most 192 MiB of HBM per device.

```python
import jax
import jax.numpy as jnp
from jax import lax

D = 9216
HEADS = 24
HD = 256
FF = 36864
CACHE_POSITIONS = 1024
STEPS = 2
SEQUENCES_WIDE = 4
SEQUENCES_TALL = 8


def draw_w_query(key, part):
    key = jax.random.fold_in(key, 7)
    values = jnp.clip(jax.random.normal(key, (D, HEADS * HD), jnp.float32), -6.0, 6.0) * D ** (-0.5)
    return values.astype(jnp.bfloat16)


def draw_cache(key, part):
    key = jax.random.fold_in(key, 11)
    random_root_key = jax.random.fold_in(key, 0)
    values = jax.random.normal(random_root_key, (SEQUENCES_TALL, SEQUENCES_WIDE, CACHE_POSITIONS, 2 * HD), jnp.float32)
    values = jnp.clip(values, -6.0, 6.0)
    return values.astype(jnp.bfloat16)


def draw_lengths(key, part):
    key = jax.random.fold_in(key, 23)
    length_key, choose_key = jax.random.split(key)
    drawn = jax.random.randint(length_key, (SEQUENCES_TALL * SEQUENCES_WIDE,), 1, CACHE_POSITIONS + 1, jnp.int32)
    longest = jax.random.randint(choose_key, (), 0, SEQUENCES_TALL * SEQUENCES_WIDE, jnp.int32)
    drawn = jnp.where(jnp.arange(SEQUENCES_TALL * SEQUENCES_WIDE, dtype=jnp.int32) == longest, CACHE_POSITIONS, drawn)
    return drawn.reshape(SEQUENCES_TALL, SEQUENCES_WIDE)


def steps_of(key, shape, cuts, smallest, high):
    def one(dim, parts):
        draws = jax.random.uniform(jax.random.fold_in(jax.random.fold_in(key, 6), dim), (parts,), jnp.float32, smallest / len(cuts), high / len(cuts))
        return jnp.repeat(jnp.exp(draws), shape[dim] // parts).reshape((-1,) + (1,) * (len(shape) - dim - 1))

    level = one(*cuts[0])
    for cut in cuts[1:]:
        level = level * one(*cut)
    return level


def normal_values(rng, dims, deviation, reach, pieces=(), kind=jnp.bfloat16):
    values = jax.random.normal(rng, dims, jnp.float32) * deviation
    if len(pieces) > 0:
        values = steps_of(rng, dims, pieces, -0.22, 0.18) * values
    return jnp.clip(values, min=-reach, max=reach).astype(kind)


def setup_inputs(seed: int = 0, part: int = 0) -> dict:
    splits = jax.random.split(jax.random.key(seed), 9)
    part_keys = jax.random.split(jax.random.fold_in(splits[8], part), 9)
    tokens = normal_values(part_keys[0], (SEQUENCES_TALL, SEQUENCES_WIDE, STEPS, D), 1.0, 6.0, ((1, 4), (3, 4)))
    gain = jnp.clip(1.0 + 0.18 * jax.random.normal(splits[1], (D,), jnp.float32), 0.1, 1.9)
    w_query = draw_w_query(jax.random.fold_in(splits[8], 71), part)
    w_keyval = normal_values(splits[3], (D, 2 * HD), D ** -0.5, 0.0625, ((0, 4), (1, 4)))
    w_gate = normal_values(splits[4], (D, FF), D ** -0.5, 0.0625, ((0, 4), (1, 4)))
    w_up = normal_values(splits[5], (D, FF), D ** -0.5, 0.0625, ((0, 4), (1, 4)))
    cache = draw_cache(jax.random.fold_in(jax.random.fold_in(splits[8], part), 71), part)
    lengths = draw_lengths(jax.random.fold_in(jax.random.fold_in(splits[8], part), 71), part)
    return {"tokens": tokens, "gain": gain, "w_query": w_query, "w_keyval": w_keyval, "w_gate": w_gate, "w_up": w_up, "cache": cache, "lengths": lengths}


EPSILON = 1e-05
MASKED = -1e+30

def normalize_rows(tokens, gain):
    floats = tokens.astype(jnp.float32)
    average = lax.optimization_barrier(jnp.sum(floats, axis=-1)) / D
    squares = lax.optimization_barrier(jnp.sum(floats * floats, axis=-1)) / D
    inverse_std = lax.rsqrt(squares - average * average + EPSILON)
    return ((floats - average[..., None]) * inverse_std[..., None] * gain).astype(jnp.bfloat16)

def attend(queries, new_pairs, cache, lengths):
    batch = queries.shape[0]
    steps = queries.shape[1]
    every_head = queries.reshape(batch, steps * HEADS, HD).astype(jnp.float32)
    stored_key_cache = cache[..., :HD].astype(jnp.float32)
    stored_value_cache = cache[..., HD:].astype(jnp.float32)
    appended_keys = new_pairs[..., :HD].astype(jnp.float32)
    appended_values = new_pairs[..., HD:].astype(jnp.float32)
    rescale_factor = HD ** (-0.5)
    cache_scores = jnp.einsum('eaf,eif->eai', every_head, stored_key_cache) * rescale_factor
    positions = jnp.arange(cache.shape[1], dtype=jnp.int32)
    visible = positions[None, None, :] < lengths[:, None, None]
    cache_scores = jnp.where(visible, cache_scores, MASKED)
    new_token_scores = jnp.einsum('izr,igr->izg', every_head, appended_keys) * rescale_factor
    owner_step = jnp.arange(steps * HEADS, dtype=jnp.int32) // HEADS
    causal = jnp.arange(steps, dtype=jnp.int32)[None, :] <= owner_step[:, None]
    new_token_scores = jnp.where(causal[None], new_token_scores, MASKED)
    highest = jnp.maximum(lax.optimization_barrier(jnp.max(cache_scores, axis=-1)), lax.optimization_barrier(jnp.max(new_token_scores, axis=-1)))
    exp_cached = jnp.exp(cache_scores - highest[..., None])
    exp_fresh = jnp.exp(new_token_scores - highest[..., None])
    totals = lax.optimization_barrier(jnp.sum(exp_cached, axis=-1)) + lax.optimization_barrier(jnp.sum(exp_fresh, axis=-1))
    cache_part_weight = (exp_cached / totals[..., None]).astype(jnp.bfloat16).astype(jnp.float32)
    new_part_weight = (exp_fresh / totals[..., None]).astype(jnp.bfloat16).astype(jnp.float32)
    context = jnp.einsum('wyi,wit->wyt', cache_part_weight, stored_value_cache)
    context = context + jnp.einsum('nga,nax->ngx', new_part_weight, appended_values)
    return context.astype(jnp.bfloat16).reshape(batch, steps, HEADS * HD)

def reference(tokens, gain, w_query, w_keyval, w_gate, w_up, cache, lengths):
    normed = normalize_rows(tokens, gain)
    row_block = normed.reshape(-1, D)
    queries = jnp.dot(row_block, w_query, preferred_element_type=jnp.float32).astype(jnp.bfloat16)
    pairs = jnp.dot(row_block, w_keyval, preferred_element_type=jnp.float32).astype(jnp.bfloat16)
    gate_part = jnp.dot(row_block, w_gate, preferred_element_type=jnp.float32)
    up_part = jnp.dot(row_block, w_up, preferred_element_type=jnp.float32)
    hidden = (jax.nn.silu(gate_part) * up_part).astype(jnp.bfloat16)
    hidden = hidden.reshape(SEQUENCES_TALL, SEQUENCES_WIDE, STEPS, FF)
    batch = SEQUENCES_TALL * SEQUENCES_WIDE
    context = attend(queries.reshape(batch, STEPS, HEADS * HD), pairs.reshape(batch, STEPS, 2 * HD), cache.reshape(batch, CACHE_POSITIONS, 2 * HD), lengths.reshape(batch))
    return (context.reshape(SEQUENCES_TALL, SEQUENCES_WIDE, STEPS, HEADS * HD), hidden)
```

```python
import functools

import jax
import jax.numpy as jnp
from jax import lax
from jax.experimental import pallas as pl
from jax.experimental.pallas import tpu as pltpu
from jax.sharding import PartitionSpec as P

D = 9216
HEADS = 24
HD = 256
EPSILON = 1e-05
MASKED = -1e30
MIB = 1024 * 1024
F32 = jnp.float32
BF16 = jnp.bfloat16


def whole(memory_space=pltpu.VMEM):
    return pl.BlockSpec(memory_space=memory_space)


def params(mib):
    return pltpu.CompilerParams(vmem_limit_bytes=mib * MIB)


def tile_of(cols, most):
    best = cols
    for tile in range(128, min(cols, most) + 1, 128):
        if cols % tile == 0:
            best = tile
    return best


def stats_kernel(tokens_ref, out_ref):
    floats = tokens_ref[...].astype(F32)
    sums = jnp.sum(floats, axis=-1, keepdims=True)
    squares = jnp.sum(floats * floats, axis=-1, keepdims=True)
    lane = lax.broadcasted_iota(jnp.int32, out_ref.shape, 1)
    out_ref[...] = jnp.where(lane < 64, sums, squares)


def partial_stats(tokens):
    return pl.pallas_call(
        stats_kernel,
        out_shape=jax.ShapeDtypeStruct((tokens.shape[0], 128), F32),
        in_specs=[whole()],
        out_specs=whole(),
    )(tokens)


def norm_kernel(count, source_ref, gain_ref, *refs):
    token_refs, stat_refs, out_ref = refs[:count], refs[count : 2 * count], refs[2 * count]
    gain = gain_ref[...]
    parts = []
    for token_ref, stat_ref in zip(token_refs, stat_refs):
        stats = stat_ref[...]
        average = stats[:, 0:1] / D
        inverse_std = lax.rsqrt(stats[:, 64:65] / D - average * average + EPSILON)
        floats = token_ref[...].astype(F32)
        parts.append(((floats - average) * inverse_std * gain).astype(BF16))
    normed = jnp.concatenate(parts, axis=0)
    rows = normed.shape[0]
    place = lax.broadcasted_iota(jnp.int32, (rows, rows), 1) == source_ref[...]
    out_ref[...] = jnp.dot(
        jnp.where(place, 1.0, 0.0).astype(BF16), normed, preferred_element_type=F32
    ).astype(BF16)


def normed_rows(source, gain, tokens, stats):
    rows = sum(t.shape[0] for t in tokens)
    features = gain.shape[0]
    return pl.pallas_call(
        functools.partial(norm_kernel, len(tokens)),
        out_shape=jax.ShapeDtypeStruct((rows, features), BF16),
        in_specs=[whole()] * (2 + 2 * len(tokens)),
        out_specs=whole(),
        compiler_params=params(16),
    )(source, gain.reshape(1, features), *tokens, *stats)


def small_kernel(x_ref, wq_ref, wkv_ref, send_ref, keep_ref):
    x = x_ref[...]
    half = x.shape[0] // 2
    cols = wq_ref.shape[1]
    q = jnp.dot(x, wq_ref[...], preferred_element_type=F32)
    send_ref[:, :cols] = q[:half]
    keep_ref[:, :cols] = q[half:]
    kv = jnp.dot(x, wkv_ref[...], preferred_element_type=F32)
    send_ref[:, cols:] = kv[:half]
    keep_ref[:, cols:] = kv[half:]


def query_sums(x, w_query, w_keyval):
    rows, features = x.shape
    cols = w_query.shape[1] + w_keyval.shape[1]
    out = jax.ShapeDtypeStruct((rows // 2, cols), F32)
    return pl.pallas_call(
        small_kernel,
        out_shape=(out, out),
        in_specs=[whole()] * 3,
        out_specs=(whole(), whole()),
        compiler_params=params(24),
        cost_estimate=pl.CostEstimate(
            flops=2 * rows * features * cols,
            bytes_accessed=2 * features * cols,
            transcendentals=0,
        ),
    )(x, w_query, w_keyval)


def wide_kernel(x_ref, wg_ref, wu_ref, send_ref, keep_ref):
    x = x_ref[...]
    half = x.shape[0] // 2
    for index, ref in enumerate((wg_ref, wu_ref)):
        part = jnp.dot(x, ref[...], preferred_element_type=F32)
        send_ref[index] = part[:half].astype(BF16)
        keep_ref[index] = part[half:]


def wide_sums(x, w_gate, w_up, start, cols):
    rows, features = x.shape
    tile = tile_of(cols, 384)
    first = start // tile
    weight = pl.BlockSpec((features, tile), lambda j: (0, first + j))
    out = pl.BlockSpec((2, rows // 2, tile), lambda j: (0, 0, j))
    return pl.pallas_call(
        wide_kernel,
        grid=(cols // tile,),
        out_shape=(
            jax.ShapeDtypeStruct((2, rows // 2, cols), BF16),
            jax.ShapeDtypeStruct((2, rows // 2, cols), F32),
        ),
        in_specs=[pl.BlockSpec((rows, features), lambda j: (0, 0)), weight, weight],
        out_specs=(out, out),
        compiler_params=params(32),
        cost_estimate=pl.CostEstimate(
            flops=4 * rows * features * cols,
            bytes_accessed=4 * features * cols,
            transcendentals=0,
        ),
    )(x, w_gate, w_up)


def query_rows_kernel(source_ref, *refs):
    out_ref = refs[-1]
    total = refs[0][...]
    for ref in refs[1:-1]:
        total = total + ref[...]
    rows = total.shape[0]
    place = lax.broadcasted_iota(jnp.int32, (rows, rows), 1) == source_ref[...]
    out_ref[...] = jnp.dot(
        jnp.where(place, 1.0, 0.0).astype(BF16), total.astype(BF16), preferred_element_type=F32
    ).astype(BF16)


def query_rows(source, terms):
    return pl.pallas_call(
        query_rows_kernel,
        out_shape=jax.ShapeDtypeStruct(terms[0].shape, BF16),
        in_specs=[whole()] * (1 + len(terms)),
        out_specs=whole(),
    )(source, *terms)


def attend_kernel(count, steps, query_cols, slot_ref, lengths_ref, cache_ref, *refs):
    part_refs, (out_ref, held, fresh) = refs[:count], refs[count:]
    for index, ref in enumerate(part_refs):
        held[slot_ref[index]] = ref[...].astype(F32)
    pair_cols = held.shape[2] - query_cols
    heads = query_cols // HD
    scale = HD ** (-0.5)
    batch, positions = cache_ref.shape[0], cache_ref.shape[1]
    fresh[...] = jnp.zeros_like(fresh)
    for b in range(batch):
        rows = pl.ds(b * steps, steps)
        for c in range(count):
            fresh[b, :steps, c * pair_cols : (c + 1) * pair_cols] = held[c, rows, query_cols:]
        queries = jnp.concatenate(
            [held[c, rows, h * HD : (h + 1) * HD] for c in range(count) for h in range(heads)],
            axis=0,
        ).astype(BF16)
        pairs = fresh[b].astype(BF16)
        dims = (((1,), (1,)), ((), ()))
        old = lax.dot_general(
            queries, cache_ref[b, :, :HD], dims, preferred_element_type=F32
        ) * scale
        position = lax.broadcasted_iota(jnp.int32, old.shape, 1)
        old = jnp.where(position < lengths_ref[b], old, MASKED)
        new = lax.dot_general(queries, pairs[:, :HD], dims, preferred_element_type=F32) * scale
        step = lax.broadcasted_iota(jnp.int32, new.shape, 0) % steps
        new = jnp.where(lax.broadcasted_iota(jnp.int32, new.shape, 1) <= step, new, MASKED)
        highest = jnp.maximum(
            jnp.max(old, axis=-1, keepdims=True), jnp.max(new, axis=-1, keepdims=True)
        )
        old = jnp.exp(old - highest)
        new = jnp.exp(new - highest)
        total = jnp.sum(old, axis=-1, keepdims=True) + jnp.sum(new, axis=-1, keepdims=True)
        context = jnp.dot(
            (old / total).astype(BF16), cache_ref[b, :, HD:], preferred_element_type=F32
        ) + jnp.dot((new / total).astype(BF16), pairs[:, HD:], preferred_element_type=F32)
        for h in range(HEADS):
            out_ref[rows, h * HD : (h + 1) * HD] = context[h * steps : (h + 1) * steps].astype(BF16)


def attend(slots, lengths, cache, parts, steps, query_cols):
    batch = cache.shape[0]
    count = len(parts)
    rows, cols = parts[0].shape
    return pl.pallas_call(
        functools.partial(attend_kernel, count, steps, query_cols),
        out_shape=jax.ShapeDtypeStruct((rows, HEADS * HD), BF16),
        in_specs=[whole(pltpu.SMEM), whole(pltpu.SMEM)] + [whole()] * (1 + count),
        out_specs=whole(),
        scratch_shapes=[
            pltpu.VMEM((count, rows, cols), F32),
            pltpu.VMEM((batch, 8, 2 * HD), F32),
        ],
        compiler_params=params(16),
        cost_estimate=pl.CostEstimate(
            flops=4 * batch * steps * HEADS * HD * cache.shape[1],
            bytes_accessed=2 * cache.size,
            transcendentals=batch * steps * HEADS * cache.shape[1],
        ),
    )(slots, lengths, cache, *parts)


def on_device(tokens, gain, w_query, w_keyval, w_gate, w_up, cache, lengths):
    size_x, size_y = lax.axis_size("gx"), lax.axis_size("gy")
    chips = size_y // 2
    me_x, me_y = lax.axis_index("gx"), lax.axis_index("gy")
    tall, _, steps, features = tokens.shape
    local = cache.shape[0]
    block = local * size_x * steps

    def shift_x(value, by):
        return lax.ppermute(value, "gx", [(i, (i + by) % size_x) for i in range(size_x)])

    def shift_y(value, by):
        return lax.ppermute(value, "gy", [(i, (i + by) % size_y) for i in range(size_y)])

    def swap(value):
        return lax.ppermute(value, "gy", [(i, i ^ 1) for i in range(size_y)])

    mine = tokens.reshape(tall * steps, features)
    gathered = [mine] + [shift_x(mine, by) for by in range(1, size_x)]
    stats = partial_stats(mine)
    stats = sum([shift_y(stats, by) for by in range(1, size_y)], stats)
    every_stat = [stats] + [shift_x(stats, by) for by in range(1, size_x)]

    row = jnp.arange(2 * chips * block, dtype=jnp.int32)
    core = jnp.where(row < chips * block, 1 - me_y % 2, me_y % 2)
    chip = (me_y // 2 + 1 + row // block % chips) % chips
    sequence = (chip * 2 + core) * local + row % block // (size_x * steps)
    column = row // steps % size_x
    source = (me_x - column) % size_x * (tall * steps) + sequence * steps + row % steps
    x = normed_rows(source[:, None], gain, gathered, every_stat)

    send, keep = query_sums(x, w_query, w_keyval)
    total = keep + swap(send)
    terms = [total[(chips - 1) * block :]] + [
        shift_y(total[(by - 1) * block : by * block], 2 * by) for by in range(1, chips)
    ]
    row = jnp.arange(block, dtype=jnp.int32)
    to = (me_x + row // (local * steps)) % size_x
    order = row // steps % local * (size_x * steps) + to * steps + row % steps
    ready = query_rows(order[:, None], terms)
    per = local * steps
    parts = [ready[:per]] + [
        shift_x(ready[by * per : (by + 1) * per], by) for by in range(1, size_x)
    ]
    slots = (me_x - jnp.arange(size_x, dtype=jnp.int32)) % size_x

    hidden_cols = w_gate.shape[1]
    chunks = 4
    cols = hidden_cols // chunks
    pieces = []
    for chunk in range(chunks):
        send, keep = wide_sums(x, w_gate, w_up, chunk * cols, cols)
        total = keep + swap(send).astype(F32)
        whole_sum = total[:, (chips - 1) * block :]
        for by in range(1, chips):
            part = total[:, (by - 1) * block : by * block].astype(BF16)
            whole_sum = whole_sum + shift_y(part, 2 * by).astype(F32)
        pieces.append((jax.nn.silu(whole_sum[0]) * whole_sum[1]).astype(BF16))
    hidden = jnp.concatenate(pieces, axis=1).reshape(local, size_x, steps, hidden_cols)

    context = attend(
        slots,
        lengths.reshape(local),
        cache.reshape(local, cache.shape[2], cache.shape[3]),
        parts,
        steps,
        w_query.shape[1],
    )
    return (context.reshape(local, 1, steps, HEADS * HD), hidden)


def solution(mesh):
    return jax.shard_map(
        on_device,
        mesh=mesh,
        in_specs=(
            P("groups", "gx", None, "gy"),
            P("gy"),
            P("gy", "gx"),
            P("gy", "gx"),
            P("gy", "gx"),
            P("gy", "gx"),
            P(("groups", "gy"), "gx", None, None),
            P(("groups", "gy"), "gx"),
        ),
        out_specs=(P(("groups", "gy"), "gx", None, None), P(("groups", "gy"), None, None, "gx")),
        check_vma=False,
    )
```

```python
import functools

import jax
import jax.numpy as jnp
from jax import lax
from jax.experimental import pallas as pl
from jax.experimental.pallas import tpu as pltpu
from jax.sharding import PartitionSpec as P

D = 9216
HEADS = 24
HD = 256
EPSILON = 1e-05
MASKED = -1e30
MIB = 1024 * 1024
TILE = 256
DEPTH = 4
F32 = jnp.float32
BF16 = jnp.bfloat16


def whole(memory_space=pltpu.VMEM):
    return pl.BlockSpec(memory_space=memory_space)


def params():
    return pltpu.CompilerParams(vmem_limit_bytes=11 * MIB)


def stats_kernel(*refs):
    out_ref = refs[-1]
    rows = refs[0].shape[0]
    for index, ref in enumerate(refs[:-2]):
        floats = ref[...].astype(F32)
        sums = jnp.sum(floats, axis=-1, keepdims=True)
        squares = jnp.sum(floats * floats, axis=-1, keepdims=True)
        lane = lax.broadcasted_iota(jnp.int32, (rows, 128), 1)
        out_ref[index * rows : (index + 1) * rows] = jnp.where(lane < 64, sums, squares)


def partial_stats(tokens, after):
    return pl.pallas_call(
        stats_kernel,
        out_shape=jax.ShapeDtypeStruct((len(tokens) * tokens[0].shape[0], 128), F32),
        in_specs=[whole()] * len(tokens) + [whole(pl.ANY)],
        out_specs=whole(),
        compiler_params=params(),
    )(*tokens, after)


def norm_kernel(count, source_ref, gain_ref, *refs):
    token_refs, stat_refs, out_ref = refs[:count], refs[count:-2], refs[-1]
    gain = gain_ref[...]
    stats = stat_refs[0][...]
    for ref in stat_refs[1:]:
        stats = stats + ref[...]
    parts = []
    for index, token_ref in enumerate(token_refs):
        rows = token_ref.shape[0]
        mine = stats[index * rows : (index + 1) * rows]
        average = mine[:, 0:1] / D
        inverse_std = lax.rsqrt(mine[:, 64:65] / D - average * average + EPSILON)
        floats = token_ref[...].astype(F32)
        parts.append(((floats - average) * inverse_std * gain).astype(BF16))
    normed = jnp.concatenate(parts, axis=0)
    rows = normed.shape[0]
    place = lax.broadcasted_iota(jnp.int32, (rows, rows), 1) == source_ref[...]
    out_ref[...] = jnp.dot(
        jnp.where(place, 1.0, 0.0).astype(BF16), normed, preferred_element_type=F32
    ).astype(BF16)


def normed_rows(source, gain, tokens, stats, after):
    rows = sum(t.shape[0] for t in tokens)
    features = gain.shape[0]
    return pl.pallas_call(
        functools.partial(norm_kernel, len(tokens)),
        out_shape=jax.ShapeDtypeStruct((rows, features), BF16),
        in_specs=[whole()] * (2 + len(tokens) + len(stats)) + [whole(pl.ANY)],
        out_specs=whole(),
        compiler_params=params(),
    )(source, gain.reshape(1, features), *tokens, *stats, after)


def in_hbm(arrays):
    return [pltpu.with_memory_space_constraint(a, pltpu.HBM) for a in arrays]


def tile_copies(w_refs, tile, place, sems):
    columns = pl.ds(pl.multiple_of(tile * TILE, TILE), TILE)
    return [
        pltpu.make_async_copy(ref.at[:, columns], place.at[index], sems.at[index])
        for index, ref in enumerate(w_refs)
    ]


def load_kernel(first, small, w_refs, out_refs, sems):
    copies = [
        pltpu.make_async_copy(w_refs[2 + index], out_refs[1 + index], sems.at[0, index])
        for index in range(small)
    ]
    for copy in copies:
        copy.start()
    tiles = out_refs[0].shape[0]
    for tile in range(tiles):
        for copy in tile_copies(w_refs[:2], first + tile, out_refs[0].at[tile], sems.at[1 + tile]):
            copy.start()
    for tile in range(tiles):
        for copy in tile_copies(w_refs[:2], first + tile, out_refs[0].at[tile], sems.at[1 + tile]):
            copy.wait()
    for copy in copies:
        copy.wait()


def load(weights, smalls, first, tiles, after=()):
    features = weights[0].shape[0]

    def kernel(*refs):
        w_refs = refs[: 2 + len(smalls)]
        out_refs = refs[2 + len(smalls) + len(after) : -1]
        load_kernel(first, len(smalls), w_refs, out_refs, refs[-1])

    return pl.pallas_call(
        kernel,
        out_shape=[pltpu.VMEM((tiles, 2, features, TILE), BF16)]
        + [pltpu.VMEM(small.shape, small.dtype) for small in smalls],
        in_specs=[whole(pltpu.HBM)] * (2 + len(smalls)) + [whole(pl.ANY)] * len(after),
        out_specs=[whole()] * (1 + len(smalls)),
        scratch_shapes=[pltpu.SemaphoreType.DMA((1 + tiles, 2))],
        compiler_params=params(),
        cost_estimate=pl.CostEstimate(
            flops=0,
            bytes_accessed=4 * features * TILE * tiles + 2 * sum(s.size for s in smalls),
            transcendentals=0,
        ),
    )(*in_hbm(weights), *in_hbm(smalls), *after)


def small_kernel(x_ref, wq_ref, wkv_ref, send_ref, keep_ref):
    x = x_ref[...]
    half = x.shape[0] // 2
    cols = wq_ref.shape[1]
    q = jnp.dot(x, wq_ref[...], preferred_element_type=F32)
    send_ref[:, :cols] = q[:half]
    keep_ref[:, :cols] = q[half:]
    kv = jnp.dot(x, wkv_ref[...], preferred_element_type=F32)
    send_ref[:, cols:] = kv[:half]
    keep_ref[:, cols:] = kv[half:]


def query_sums(x, w_query, w_keyval):
    rows, features = x.shape
    cols = w_query.shape[1] + w_keyval.shape[1]
    out = pltpu.VMEM((rows // 2, cols), F32)
    return pl.pallas_call(
        small_kernel,
        out_shape=(out, out),
        in_specs=[whole()] * 3,
        out_specs=(whole(), whole()),
        compiler_params=params(),
        cost_estimate=pl.CostEstimate(
            flops=2 * rows * features * cols,
            bytes_accessed=2 * features * cols,
            transcendentals=0,
        ),
    )(
        x,
        pltpu.with_memory_space_constraint(w_query, pltpu.VMEM),
        pltpu.with_memory_space_constraint(w_keyval, pltpu.VMEM),
    )


def wide_kernel(first, tiles, x_ref, w_refs, pre_refs, send_ref, keep_ref, next_ref, ring, ring_sems, next_sems):
    held = sum(ref.shape[0] for ref in pre_refs)
    streamed = tiles - held
    depth = ring.shape[0]
    following = 0 if next_ref is None else next_ref.shape[0]
    half = x_ref.shape[0] // 2

    def fetch(index):
        return tile_copies(w_refs, first + held + index, ring.at[lax.rem(index, depth)], ring_sems.at[lax.rem(index, depth)])

    def fetch_next(index):
        return tile_copies(w_refs, first + tiles + index, next_ref.at[index], next_sems.at[index])

    def start(copies):
        for copy in copies:
            copy.start()

    def multiply(tile, place):
        columns = pl.ds(pl.multiple_of(tile * TILE, TILE), TILE)
        for index in range(2):
            part = jnp.dot(x_ref[...], place[index], preferred_element_type=F32)
            send_ref[index, :, columns] = part[:half].astype(BF16)
            keep_ref[index, :, columns] = part[half:]

    early = min(depth, streamed)
    for index in range(early):
        start(fetch(index))
    early_next = min(following, max(DEPTH - early, 0)) if streamed else following
    for index in range(early_next):
        start(fetch_next(index))
    done = 0
    for ref in pre_refs:

        def from_held(index, carry, ref=ref, done=done):
            multiply(done + index, ref.at[index])
            return carry

        lax.fori_loop(0, ref.shape[0], from_held, 0)
        done += ref.shape[0]

    def from_ring(index, carry):
        for copy in fetch(index):
            copy.wait()
        multiply(held + index, ring.at[lax.rem(index, depth)])

        @pl.when(index + depth < streamed)
        def _():
            start(fetch(index + depth))

        if following > early_next:
            later = index + early_next + depth - streamed

            @pl.when((later >= early_next) & (later < following))
            def _():
                start(fetch_next(later))

        return carry

    lax.fori_loop(0, streamed, from_ring, 0)
    for index in range(following):
        for copy in fetch_next(index):
            copy.wait()


def wide_sums(x, weights, held, first, tiles, following, after=()):
    rows, features = x.shape
    cols = tiles * TILE
    streamed = tiles - sum(h.shape[0] for h in held)
    depth = min(DEPTH, max(streamed, 1))

    def kernel(x_ref, wg_ref, wu_ref, *refs):
        pre_refs = refs[: len(held)]
        refs = refs[len(held) + len(after) :]
        send_ref, keep_ref = refs[:2]
        next_ref = refs[2] if following else None
        ring, ring_sems, next_sems = refs[-3:]
        wide_kernel(
            first, tiles, x_ref, (wg_ref, wu_ref), pre_refs, send_ref, keep_ref, next_ref, ring, ring_sems, next_sems
        )

    out_shape = [
        pltpu.VMEM((2, rows // 2, cols), BF16),
        pltpu.VMEM((2, rows // 2, cols), F32),
    ]
    if following:
        out_shape.append(pltpu.VMEM((following, 2, features, TILE), BF16))
    return pl.pallas_call(
        kernel,
        out_shape=out_shape,
        in_specs=[whole(), whole(pltpu.HBM), whole(pltpu.HBM)]
        + [whole()] * len(held)
        + [whole(pl.ANY)] * len(after),
        out_specs=[whole()] * len(out_shape),
        scratch_shapes=[
            pltpu.VMEM((depth, 2, features, TILE), BF16),
            pltpu.SemaphoreType.DMA((depth, 2)),
            pltpu.SemaphoreType.DMA((max(following, 1), 2)),
        ],
        compiler_params=params(),
        cost_estimate=pl.CostEstimate(
            flops=4 * rows * features * cols,
            bytes_accessed=4 * features * TILE * (streamed + following),
            transcendentals=0,
        ),
    )(x, *in_hbm(weights), *[pltpu.with_memory_space_constraint(h, pltpu.VMEM) for h in held], *after)


def attend_kernel(count, steps, query_cols, slot_ref, lengths_ref, cache_ref, *refs):
    part_refs, (out_ref, held, fresh) = refs[:count], refs[count:]
    for index, ref in enumerate(part_refs):
        for b in range(ref.shape[0]):
            held[slot_ref[index], b, :steps] = ref[b].astype(F32)
    pair_cols = held.shape[3] - query_cols
    heads = query_cols // HD
    scale = HD ** (-0.5)
    batch, positions = cache_ref.shape[0], cache_ref.shape[1]
    fresh[...] = jnp.zeros_like(fresh)
    for b in range(batch):
        rows = pl.ds(b * steps, steps)
        for c in range(count):
            fresh[b, :steps, c * pair_cols : (c + 1) * pair_cols] = held[c, b, :steps, query_cols:]
        queries = jnp.concatenate(
            [held[c, b, :steps, h * HD : (h + 1) * HD] for c in range(count) for h in range(heads)],
            axis=0,
        ).astype(BF16)
        pairs = fresh[b].astype(BF16)
        dims = (((1,), (1,)), ((), ()))
        old = lax.dot_general(
            queries, cache_ref[b, :, :HD], dims, preferred_element_type=F32
        ) * scale
        position = lax.broadcasted_iota(jnp.int32, old.shape, 1)
        old = jnp.where(position < lengths_ref[b], old, MASKED)
        new = lax.dot_general(queries, pairs[:, :HD], dims, preferred_element_type=F32) * scale
        step = lax.broadcasted_iota(jnp.int32, new.shape, 0) % steps
        new = jnp.where(lax.broadcasted_iota(jnp.int32, new.shape, 1) <= step, new, MASKED)
        highest = jnp.maximum(
            jnp.max(old, axis=-1, keepdims=True), jnp.max(new, axis=-1, keepdims=True)
        )
        old = jnp.exp(old - highest)
        new = jnp.exp(new - highest)
        total = jnp.sum(old, axis=-1, keepdims=True) + jnp.sum(new, axis=-1, keepdims=True)
        context = jnp.dot(
            (old / total).astype(BF16), cache_ref[b, :, HD:], preferred_element_type=F32
        ) + jnp.dot((new / total).astype(BF16), pairs[:, HD:], preferred_element_type=F32)
        for h in range(HEADS):
            out_ref[rows, h * HD : (h + 1) * HD] = context[h * steps : (h + 1) * steps].astype(BF16)


def attend(slots, lengths, cache, parts, steps, query_cols):
    batch = cache.shape[0]
    count = len(parts)
    rows, cols = batch * steps, parts[0].shape[2]
    return pl.pallas_call(
        functools.partial(attend_kernel, count, steps, query_cols),
        out_shape=jax.ShapeDtypeStruct((rows, HEADS * HD), BF16),
        in_specs=[whole(pltpu.SMEM), whole(pltpu.SMEM)] + [whole()] * (1 + count),
        out_specs=whole(),
        scratch_shapes=[
            pltpu.VMEM((count, batch, 8, cols), F32),
            pltpu.VMEM((batch, 8, 2 * HD), F32),
        ],
        compiler_params=params(),
        cost_estimate=pl.CostEstimate(
            flops=4 * batch * steps * HEADS * HD * cache.shape[1],
            bytes_accessed=2 * cache.size,
            transcendentals=batch * steps * HEADS * cache.shape[1],
        ),
    )(slots, lengths, cache, *parts)


def on_device(tokens, gain, w_query, w_keyval, w_gate, w_up, cache, lengths):
    size_x, size_y = lax.axis_size("gx"), lax.axis_size("gy")
    chips = size_y // 2
    me_x, me_y = lax.axis_index("gx"), lax.axis_index("gy")
    tall, _, steps, features = tokens.shape
    local = cache.shape[0]
    block = local * size_x * steps

    def shift_x(value, by):
        return lax.ppermute(value, "gx", [(i, (i + by) % size_x) for i in range(size_x)])

    def shift_y(value, by):
        return lax.ppermute(value, "gy", [(i, (i + by) % size_y) for i in range(size_y)])

    def swap(value):
        return lax.ppermute(value, "gy", [(i, i ^ 1) for i in range(size_y)])

    weights = (w_gate, w_up)
    tiles = w_gate.shape[1] // TILE
    bounds = [tiles * share // 36 for share in (0, 8, 19, 32, 36)]
    before = [tiles * share // 36 for share in (4, 4)]
    ahead = [max(1, tiles * share // 36) for share in (4, 4, 3)] + [0]
    gathered = [tokens] + [shift_x(tokens, by) for by in range(1, size_x)]
    gathered = [t.reshape(tall * steps, features) for t in gathered]
    first_tiles, w_query, w_keyval = load(weights, (w_query, w_keyval), 0, before[0])
    stats = partial_stats(gathered, first_tiles)
    every_stat = [stats] + [shift_y(stats, by) for by in range(1, size_y)]
    (second_tiles,) = load(weights, (), before[0], before[1], after=(stats,))

    row = jnp.arange(2 * chips * block, dtype=jnp.int32)
    core = jnp.where(row < chips * block, 1 - me_y % 2, me_y % 2)
    chip = (me_y // 2 + 1 + row // block % chips) % chips
    sequence = (chip * 2 + core) * local + row % block // (size_x * steps)
    column = row // steps % size_x
    source = (me_x - column) % size_x * (tall * steps) + sequence * steps + row % steps
    x = normed_rows(source[:, None], gain, gathered, every_stat, second_tiles)

    def across_chips(total, kind):
        whole_sum = total[..., (chips - 1) * block :, :]
        for by in range(1, chips):
            part = total[..., (by - 1) * block : by * block, :].astype(kind)
            whole_sum = whole_sum + shift_y(part, 2 * by).astype(F32)
        return whole_sum

    def gated(whole_sum):
        return (jax.nn.silu(whole_sum[0]) * whole_sum[1]).astype(BF16)

    def chunk_sums(chunk, held, after):
        return wide_sums(
            x, weights, held, bounds[chunk], bounds[chunk + 1] - bounds[chunk], ahead[chunk], after
        )

    query_cols = w_query.shape[1]
    send_q, keep_q = query_sums(x, w_query, w_keyval)
    send, keep, held = chunk_sums(0, (first_tiles, second_tiles), (send_q,))
    total_q = keep_q + swap(send_q)

    send_1, keep_1, held = chunk_sums(1, (held,), (total_q, send))
    total_0 = keep + swap(send).astype(F32)
    ready = across_chips(total_q, F32).astype(BF16).reshape(local, size_x, steps, -1)
    turned = [
        lax.dynamic_slice_in_dim(ready, (me_x + by) % size_x, 1, 1)[:, 0] for by in range(size_x)
    ]

    send_2, keep_2, held = chunk_sums(2, (held,), (total_0, turned[0], send_1))
    total_1 = keep_1 + swap(send_1).astype(F32)
    parts = [turned[0]] + [shift_x(turned[by], by) for by in range(1, size_x)]
    sum_0 = across_chips(total_0, BF16)

    send_3, keep_3 = chunk_sums(3, (held,), (total_1, parts[-1], sum_0, send_2))
    total_2 = keep_2 + swap(send_2).astype(F32)
    sum_1 = across_chips(total_1, BF16)
    total_3 = keep_3 + swap(send_3).astype(F32)
    sum_2 = across_chips(total_2, BF16)
    sum_3 = across_chips(total_3, BF16)
    pieces = [gated(s) for s in (sum_0, sum_1, sum_2, sum_3)]
    hidden = jnp.concatenate(pieces, axis=1).reshape(local, size_x, steps, -1)
    slots = (me_x - jnp.arange(size_x, dtype=jnp.int32)) % size_x

    context = attend(
        slots,
        lengths.reshape(local),
        cache.reshape(local, cache.shape[2], cache.shape[3]),
        parts,
        steps,
        query_cols,
    )
    return (context.reshape(local, 1, steps, HEADS * HD), hidden)


def solution(mesh):
    return jax.shard_map(
        on_device,
        mesh=mesh,
        in_specs=(
            P("groups", "gx", None, "gy"),
            P("gy"),
            P("gy", "gx"),
            P("gy", "gx"),
            P("gy", "gx"),
            P("gy", "gx"),
            P(("groups", "gy"), "gx", None, None),
            P(("groups", "gy"), "gx"),
        ),
        out_specs=(P(("groups", "gy"), "gx", None, None), P(("groups", "gy"), None, None, "gx")),
        check_vma=False,
    )
```

```python
import functools

import jax
import jax.numpy as jnp
from jax import lax
from jax.experimental import pallas as pl
from jax.experimental.pallas import tpu as pltpu
from jax.sharding import PartitionSpec as P

D = 9216
HEADS = 24
HD = 256
EPSILON = 1e-05
MASKED = -1e30
MIB = 1024 * 1024
TILE = 256
DEPTH = 3
F32 = jnp.float32
BF16 = jnp.bfloat16


def whole(memory_space=pltpu.VMEM):
    return pl.BlockSpec(memory_space=memory_space)


def params():
    return pltpu.CompilerParams(vmem_limit_bytes=9 * MIB)


def stats_kernel(count, *refs):
    token_refs, (rows_ref, out_ref) = refs[:count], refs[-2:]
    tall, _, steps, features = token_refs[0].shape
    for index, ref in enumerate(token_refs):
        for t in range(tall):
            first = (index * tall + t) * steps
            rows_ref[first : first + steps] = ref[t, 0].astype(F32)
    floats = rows_ref[...]
    sums = jnp.sum(floats, axis=-1, keepdims=True)
    squares = jnp.sum(floats * floats, axis=-1, keepdims=True)
    lane = lax.broadcasted_iota(jnp.int32, out_ref.shape, 1)
    out_ref[...] = jnp.where(lane < 64, sums, squares)


def partial_stats(tokens, after):
    tall, _, steps, features = tokens[0].shape
    rows = len(tokens) * tall * steps
    return pl.pallas_call(
        functools.partial(stats_kernel, len(tokens)),
        out_shape=(pltpu.VMEM((rows, features), F32), pltpu.VMEM((rows, 128), F32)),
        in_specs=[whole()] * len(tokens) + [whole(pl.ANY)],
        out_specs=(whole(), whole()),
        compiler_params=params(),
    )(*tokens, after)


def norm_kernel(source_ref, gain_ref, rows_ref, *refs):
    stat_refs, out_ref = refs[:-2], refs[-1]
    stats = stat_refs[0][...]
    for ref in stat_refs[1:]:
        stats = stats + ref[...]
    average = stats[:, 0:1] / D
    inverse_std = lax.rsqrt(stats[:, 64:65] / D - average * average + EPSILON)
    normed = ((rows_ref[...] - average) * inverse_std * gain_ref[...]).astype(BF16)
    rows = normed.shape[0]
    place = lax.broadcasted_iota(jnp.int32, (rows, rows), 1) == source_ref[...]
    out_ref[...] = jnp.dot(
        jnp.where(place, 1.0, 0.0).astype(BF16), normed, preferred_element_type=F32
    ).astype(BF16)


def normed_rows(source, gain, rows, stats, after):
    return pl.pallas_call(
        norm_kernel,
        out_shape=pltpu.VMEM(rows.shape, BF16),
        in_specs=[whole()] * (3 + len(stats)) + [whole(pl.ANY)],
        out_specs=whole(),
        compiler_params=params(),
    )(source, gain, rows, *stats, after)


def combine_kernel(keep_ref, sent_ref, *out_refs):
    total = keep_ref[...] + sent_ref[...].astype(F32)
    block = out_refs[0].shape[-2]
    for index, ref in enumerate(out_refs):
        ref[...] = total[..., index * block : (index + 1) * block, :].astype(ref.dtype)


def combine(keep, sent, chips):
    shape = keep.shape[:-2] + (keep.shape[-2] // chips, keep.shape[-1])
    return pl.pallas_call(
        combine_kernel,
        out_shape=[pltpu.VMEM(shape, sent.dtype)] * (chips - 1) + [pltpu.VMEM(shape, F32)],
        in_specs=[whole()] * 2,
        out_specs=[whole()] * chips,
        compiler_params=params(),
    )(keep, sent)


def query_rows_kernel(count, source_ref, *refs):
    term_refs, out_refs = refs[:-count], refs[-count:]
    total = term_refs[0][...]
    for ref in term_refs[1:]:
        total = total + ref[...]
    rows = total.shape[0]
    place = lax.broadcasted_iota(jnp.int32, (rows, rows), 1) == source_ref[...]
    turned = jnp.dot(
        jnp.where(place, 1.0, 0.0).astype(BF16), total.astype(BF16), preferred_element_type=F32
    )
    each = rows // count
    for index, ref in enumerate(out_refs):
        ref[...] = turned[index * each : (index + 1) * each].astype(BF16)


def query_rows(source, terms, count):
    rows, cols = terms[0].shape
    return pl.pallas_call(
        functools.partial(query_rows_kernel, count),
        out_shape=[pltpu.VMEM((rows // count, cols), BF16)] * count,
        in_specs=[whole()] * (1 + len(terms)),
        out_specs=[whole()] * count,
        compiler_params=params(),
    )(source, *terms)


def gated_kernel(counts, *refs):
    out_ref = refs[-1]
    local, wide, steps, _ = out_ref.shape
    taken, first = 0, 0
    for count in counts:
        total = refs[taken][...]
        for ref in refs[taken + 1 : taken + count]:
            total = total + ref[...].astype(F32)
        taken += count
        gate, up = total[0], total[1]
        hidden = gate / (1.0 + jnp.exp(-gate)) * up
        cols = hidden.shape[1]
        for row in range(local * wide):
            piece = hidden[row * steps : (row + 1) * steps].astype(BF16)
            out_ref[row // wide, row % wide, :, first : first + cols] = piece
        first += cols


def gated(chunks, shape):
    terms = [term for chunk in chunks for term in chunk]
    return pl.pallas_call(
        functools.partial(gated_kernel, [len(chunk) for chunk in chunks]),
        out_shape=jax.ShapeDtypeStruct(shape, BF16),
        in_specs=[whole()] * len(terms),
        out_specs=whole(),
        compiler_params=params(),
    )(*terms)


def in_hbm(arrays):
    return [pltpu.with_memory_space_constraint(a, pltpu.HBM) for a in arrays]


def tile_copies(w_refs, tile, place, sems):
    columns = pl.ds(pl.multiple_of(tile * TILE, TILE), TILE)
    return [
        pltpu.make_async_copy(ref.at[:, columns], place.at[index], sems.at[index])
        for index, ref in enumerate(w_refs)
    ]


def load_kernel(first, small, w_refs, out_refs, sems):
    copies = [
        pltpu.make_async_copy(w_refs[2 + index], out_refs[1 + index], sems.at[0, index])
        for index in range(small)
    ]
    for copy in copies:
        copy.start()
    tiles = out_refs[0].shape[0]
    for tile in range(tiles):
        for copy in tile_copies(w_refs[:2], first + tile, out_refs[0].at[tile], sems.at[1 + tile]):
            copy.start()
    for tile in range(tiles):
        for copy in tile_copies(w_refs[:2], first + tile, out_refs[0].at[tile], sems.at[1 + tile]):
            copy.wait()
    for copy in copies:
        copy.wait()


def load(weights, smalls, first, tiles, after=()):
    features = weights[0].shape[0]

    def kernel(*refs):
        w_refs = refs[: 2 + len(smalls)]
        out_refs = refs[2 + len(smalls) + len(after) : -1]
        load_kernel(first, len(smalls), w_refs, out_refs, refs[-1])

    return pl.pallas_call(
        kernel,
        out_shape=[pltpu.VMEM((tiles, 2, features, TILE), BF16)]
        + [pltpu.VMEM(small.shape, small.dtype) for small in smalls],
        in_specs=[whole(pltpu.HBM)] * (2 + len(smalls)) + [whole(pl.ANY)] * len(after),
        out_specs=[whole()] * (1 + len(smalls)),
        scratch_shapes=[pltpu.SemaphoreType.DMA((1 + tiles, 2))],
        compiler_params=params(),
        cost_estimate=pl.CostEstimate(
            flops=0,
            bytes_accessed=4 * features * TILE * tiles + 2 * sum(s.size for s in smalls),
            transcendentals=0,
        ),
    )(*in_hbm(weights), *in_hbm(smalls), *after)


def small_kernel(x_ref, wq_ref, wkv_ref, send_ref, keep_ref):
    x = x_ref[...]
    half = x.shape[0] // 2
    cols = wq_ref.shape[1]
    q = jnp.dot(x, wq_ref[...], preferred_element_type=F32)
    send_ref[:, :cols] = q[:half]
    keep_ref[:, :cols] = q[half:]
    kv = jnp.dot(x, wkv_ref[...], preferred_element_type=F32)
    send_ref[:, cols:] = kv[:half]
    keep_ref[:, cols:] = kv[half:]


def query_sums(x, w_query, w_keyval):
    rows, features = x.shape
    cols = w_query.shape[1] + w_keyval.shape[1]
    out = pltpu.VMEM((rows // 2, cols), F32)
    return pl.pallas_call(
        small_kernel,
        out_shape=(out, out),
        in_specs=[whole()] * 3,
        out_specs=(whole(), whole()),
        compiler_params=params(),
        cost_estimate=pl.CostEstimate(
            flops=2 * rows * features * cols,
            bytes_accessed=2 * features * cols,
            transcendentals=0,
        ),
    )(
        x,
        pltpu.with_memory_space_constraint(w_query, pltpu.VMEM),
        pltpu.with_memory_space_constraint(w_keyval, pltpu.VMEM),
    )


def wide_kernel(first, tiles, x_ref, w_refs, pre_refs, out_refs, next_ref, ring, ring_sems, next_sems):
    held = sum(ref.shape[0] for ref in pre_refs)
    streamed = tiles - held
    depth = ring.shape[0]
    following = 0 if next_ref is None else next_ref.shape[0]

    def fetch(index):
        slot = lax.rem(index, depth)
        return tile_copies(w_refs, first + held + index, ring.at[slot], ring_sems.at[slot])

    def fetch_next(index):
        return tile_copies(w_refs, first + tiles + index, next_ref.at[index], next_sems.at[index])

    def start(copies):
        for copy in copies:
            copy.start()

    def multiply(tile, place):
        columns = pl.ds(pl.multiple_of(tile * TILE, TILE), TILE)
        for index in range(2):
            part = jnp.dot(x_ref[...], place[index], preferred_element_type=F32)
            row = 0
            for ref in out_refs:
                rows = ref.shape[1]
                ref[index, :, columns] = part[row : row + rows].astype(ref.dtype)
                row += rows

    early = min(depth, streamed)
    for index in range(early):
        start(fetch(index))
    early_next = min(following, max(DEPTH - early, 0)) if streamed else following
    for index in range(early_next):
        start(fetch_next(index))
    done = 0
    for ref in pre_refs:

        def from_held(index, carry, ref=ref, done=done):
            multiply(done + index, ref.at[index])
            return carry

        lax.fori_loop(0, ref.shape[0], from_held, 0)
        done += ref.shape[0]

    def from_ring(index, carry):
        for copy in fetch(index):
            copy.wait()
        multiply(held + index, ring.at[lax.rem(index, depth)])

        @pl.when(index + depth < streamed)
        def _():
            start(fetch(index + depth))

        if following > early_next:
            later = index + early_next + depth - streamed

            @pl.when((later >= early_next) & (later < following))
            def _():
                start(fetch_next(later))

        return carry

    lax.fori_loop(0, streamed, from_ring, 0)
    for index in range(following):
        for copy in fetch_next(index):
            copy.wait()


def wide_sums(x, weights, held, first, tiles, following, blocks, after=()):
    rows, features = x.shape
    cols = tiles * TILE
    streamed = tiles - sum(h.shape[0] for h in held)
    depth = min(DEPTH, max(streamed, 1))
    outs = len(blocks)

    def kernel(x_ref, wg_ref, wu_ref, *refs):
        pre_refs = refs[: len(held)]
        refs = refs[len(held) + len(after) :]
        next_ref = refs[outs] if following else None
        wide_kernel(first, tiles, x_ref, (wg_ref, wu_ref), pre_refs, refs[:outs], next_ref, *refs[-3:])

    out_shape = [pltpu.VMEM((2, block, cols), BF16) for block in blocks[:-1]]
    out_shape.append(pltpu.VMEM((2, blocks[-1], cols), F32))
    if following:
        out_shape.append(pltpu.VMEM((following, 2, features, TILE), BF16))
    return pl.pallas_call(
        kernel,
        out_shape=out_shape,
        in_specs=[whole(), whole(pltpu.HBM), whole(pltpu.HBM)]
        + [whole()] * len(held)
        + [whole(pl.ANY)] * len(after),
        out_specs=[whole()] * len(out_shape),
        scratch_shapes=[
            pltpu.VMEM((depth, 2, features, TILE), BF16),
            pltpu.SemaphoreType.DMA((depth, 2)),
            pltpu.SemaphoreType.DMA((max(following, 1), 2)),
        ],
        compiler_params=params(),
        cost_estimate=pl.CostEstimate(
            flops=4 * rows * features * cols,
            bytes_accessed=4 * features * TILE * (streamed + following),
            transcendentals=0,
        ),
    )(x, *in_hbm(weights), *[pltpu.with_memory_space_constraint(h, pltpu.VMEM) for h in held], *after)


def attend_kernel(count, steps, query_cols, slot_ref, lengths_ref, cache_ref, *refs):
    part_refs, (out_ref, held, fresh) = refs[:count], refs[-3:]
    for index, ref in enumerate(part_refs):
        held[slot_ref[index]] = ref[...].astype(F32)
    pair_cols = held.shape[2] - query_cols
    heads = query_cols // HD
    scale = HD ** (-0.5)
    batch, positions = cache_ref.shape[0], cache_ref.shape[1]
    fresh[...] = jnp.zeros_like(fresh)
    for b in range(batch):
        rows = pl.ds(b * steps, steps)
        for c in range(count):
            fresh[b, :steps, c * pair_cols : (c + 1) * pair_cols] = held[c, rows, query_cols:]
        queries = jnp.concatenate(
            [held[c, rows, h * HD : (h + 1) * HD] for c in range(count) for h in range(heads)],
            axis=0,
        ).astype(BF16)
        pairs = fresh[b].astype(BF16)
        dims = (((1,), (1,)), ((), ()))
        old = lax.dot_general(
            queries, cache_ref[b, :, :HD], dims, preferred_element_type=F32
        ) * scale
        position = lax.broadcasted_iota(jnp.int32, old.shape, 1)
        old = jnp.where(position < lengths_ref[b], old, MASKED)
        new = lax.dot_general(queries, pairs[:, :HD], dims, preferred_element_type=F32) * scale
        step = lax.broadcasted_iota(jnp.int32, new.shape, 0) % steps
        new = jnp.where(lax.broadcasted_iota(jnp.int32, new.shape, 1) <= step, new, MASKED)
        highest = jnp.maximum(
            jnp.max(old, axis=-1, keepdims=True), jnp.max(new, axis=-1, keepdims=True)
        )
        old = jnp.exp(old - highest)
        new = jnp.exp(new - highest)
        total = jnp.sum(old, axis=-1, keepdims=True) + jnp.sum(new, axis=-1, keepdims=True)
        context = jnp.dot(
            (old / total).astype(BF16), cache_ref[b, :, HD:], preferred_element_type=F32
        ) + jnp.dot((new / total).astype(BF16), pairs[:, HD:], preferred_element_type=F32)
        for h in range(HEADS):
            piece = context[h * steps : (h + 1) * steps].astype(BF16)
            out_ref[b, 0, :, h * HD : (h + 1) * HD] = piece


def attend(slots, lengths, cache, parts, steps, query_cols, after):
    batch = cache.shape[0]
    count = len(parts)
    rows, cols = parts[0].shape
    return pl.pallas_call(
        functools.partial(attend_kernel, count, steps, query_cols),
        out_shape=jax.ShapeDtypeStruct((batch, 1, steps, HEADS * HD), BF16),
        in_specs=[whole(pltpu.SMEM), whole(pltpu.SMEM)] + [whole()] * (1 + count) + [whole(pl.ANY)] * len(after),
        out_specs=whole(),
        scratch_shapes=[
            pltpu.VMEM((count, rows, cols), F32),
            pltpu.VMEM((batch, 8, 2 * HD), F32),
        ],
        compiler_params=params(),
        cost_estimate=pl.CostEstimate(
            flops=4 * batch * steps * HEADS * HD * cache.shape[1],
            bytes_accessed=2 * cache.size,
            transcendentals=batch * steps * HEADS * cache.shape[1],
        ),
    )(slots, lengths, cache, *parts, *after)


def on_device(tokens, gain, w_query, w_keyval, w_gate, w_up, cache, lengths):
    size_x, size_y = lax.axis_size("gx"), lax.axis_size("gy")
    chips = size_y // 2
    me_x, me_y = lax.axis_index("gx"), lax.axis_index("gy")
    tall, _, steps, features = tokens.shape
    local = cache.shape[0]
    block = local * size_x * steps

    def shift_x(value, by):
        return lax.ppermute(value, "gx", [(i, (i + by) % size_x) for i in range(size_x)])

    def shift_y(value, by):
        return lax.ppermute(value, "gy", [(i, (i + by) % size_y) for i in range(size_y)])

    def swap(value):
        return lax.ppermute(value, "gy", [(i, i ^ 1) for i in range(size_y)])

    def across_core(value):
        pairs = []
        for i in range(size_y):
            pairs.append((i, (i // 2 + 1) % chips * 2 + (1 - i % 2)))
        return lax.ppermute(value, "gy", pairs)

    row = jnp.arange(2 * chips * block, dtype=jnp.int32)
    core = jnp.where(row < chips * block, 1 - me_y % 2, me_y % 2)
    chip = (me_y // 2 + 1 + row // block % chips) % chips
    sequence = (chip * 2 + core) * local + row % block // (size_x * steps)
    column = row // steps % size_x
    source = (me_x - column) % size_x * (tall * steps) + sequence * steps + row % steps
    source = source[:, None]
    row = jnp.arange(block, dtype=jnp.int32)
    to = (me_x + row // (local * steps)) % size_x
    order = row // steps % local * (size_x * steps) + to * steps + row % steps
    order = order[:, None]
    slots = (me_x - jnp.arange(size_x, dtype=jnp.int32)) % size_x
    lengths = lengths.reshape(local)
    gain = gain.reshape(1, features)

    weights = (w_gate, w_up)
    tiles = w_gate.shape[1] // TILE
    before = [tiles * share // 36 for share in (5, 5)]
    bounds = [0, sum(before)] + [tiles * share // 36 for share in (20, 28, 36)]
    ahead = [max(1, tiles * share // 36) for share in (3, 3, 3)] + [0]
    gathered = [tokens] + [shift_x(tokens, by) for by in range(1, size_x)]
    (first_tiles,) = load(weights, (), 0, before[0], after=(source, order, slots, lengths, gain))
    rows, stats = partial_stats(gathered, first_tiles)
    every_stat = [stats] + [shift_y(stats, by) for by in range(1, size_y)]
    (second_tiles,) = load(weights, (), before[0], before[1], after=(stats,))
    x = normed_rows(source, gain, rows, every_stat, second_tiles)

    halves = (chips * block, chips * block)
    direct = chips == 2

    def chunk_sums(chunk, held, after, blocks=halves):
        count = bounds[chunk + 1] - bounds[chunk]
        return wide_sums(x, weights, held, bounds[chunk], count, ahead[chunk], blocks, after)

    def across_chips(parts):
        return [parts[-1]] + [shift_y(part, 2 * by) for by, part in enumerate(parts[:-1], 1)]

    query_cols = w_query.shape[1]
    send_q, keep_q = query_sums(x, w_query, w_keyval)
    send_0, keep_0, held = chunk_sums(0, (first_tiles, second_tiles), (send_q,))
    parts_q = combine(keep_q, swap(send_q), chips)

    send_1, keep_1, held = chunk_sums(1, (held,), (parts_q[0], send_0))
    parts_0 = combine(keep_0, swap(send_0), chips)
    turned = query_rows(order, across_chips(parts_q), size_x)

    send_2, keep_2, held = chunk_sums(2, (held,), (parts_0[0], turned[0], send_1))
    parts_1 = combine(keep_1, swap(send_1), chips)
    new = [turned[0]] + [shift_x(turned[by], by) for by in range(1, size_x)]

    last = chunk_sums(3, (held,), (parts_1[0], send_2), (block,) * 4 if direct else halves)
    parts_2 = combine(keep_2, swap(send_2), chips)
    cache = cache.reshape(local, cache.shape[2], cache.shape[3])
    context = attend(slots, lengths, cache, new, steps, query_cols, (parts_2[0], last[0]))
    if direct:
        terms_3 = [last[3], across_core(last[0]), swap(last[1]), shift_y(last[2], 2)]
    else:
        terms_3 = across_chips(combine(last[1], swap(last[0]), chips))
    chunks = [across_chips(parts) for parts in (parts_0, parts_1, parts_2)] + [terms_3]
    return (context, gated(chunks, (local, size_x, steps, w_gate.shape[1])))


def solution(mesh):
    return jax.shard_map(
        on_device,
        mesh=mesh,
        in_specs=(
            P("groups", "gx", None, "gy"),
            P("gy"),
            P("gy", "gx"),
            P("gy", "gx"),
            P("gy", "gx"),
            P("gy", "gx"),
            P(("groups", "gy"), "gx", None, None),
            P(("groups", "gy"), "gx"),
        ),
        out_specs=(P(("groups", "gy"), "gx", None, None), P(("groups", "gy"), None, None, "gx")),
        check_vma=False,
    )
```

```python
import functools

import jax
import jax.numpy as jnp
from jax import lax
from jax.experimental import pallas as pl
from jax.experimental.pallas import tpu as pltpu
from jax.sharding import PartitionSpec as P

D = 9216
HEADS = 24
HD = 256
EPSILON = 1e-05
MASKED = -1e30
MIB = 1024 * 1024
TILE = 256
DEPTH = 3
F32 = jnp.float32
BF16 = jnp.bfloat16


def whole(memory_space=pltpu.VMEM):
    return pl.BlockSpec(memory_space=memory_space)


def cost_of(*arrays):
    size = sum(a.size for a in arrays)
    return pl.CostEstimate(flops=size, bytes_accessed=size // 16, transcendentals=0)


def params():
    return pltpu.CompilerParams(vmem_limit_bytes=9 * MIB)


def stats_kernel(count, *refs):
    token_refs, (rows_ref, out_ref) = refs[:count], refs[-2:]
    tall, _, steps, features = token_refs[0].shape
    for index, ref in enumerate(token_refs):
        for t in range(tall):
            first = (index * tall + t) * steps
            rows_ref[first : first + steps] = ref[t, 0].astype(F32)
    floats = rows_ref[...]
    sums = jnp.sum(floats, axis=-1, keepdims=True)
    squares = jnp.sum(floats * floats, axis=-1, keepdims=True)
    lane = lax.broadcasted_iota(jnp.int32, out_ref.shape, 1)
    out_ref[...] = jnp.where(lane < 64, sums, squares)


def partial_stats(tokens, after):
    tall, _, steps, features = tokens[0].shape
    rows = len(tokens) * tall * steps
    return pl.pallas_call(
        functools.partial(stats_kernel, len(tokens)),
        out_shape=(pltpu.VMEM((rows, features), F32), pltpu.VMEM((rows, 128), F32)),
        in_specs=[whole()] * len(tokens) + [whole(pl.ANY)],
        out_specs=(whole(), whole()),
        compiler_params=params(),
        cost_estimate=cost_of(*tokens),
    )(*tokens, after)


def norm_kernel(source_ref, gain_ref, rows_ref, *refs):
    stat_refs, out_ref = refs[:-2], refs[-1]
    stats = stat_refs[0][...]
    for ref in stat_refs[1:]:
        stats = stats + ref[...]
    average = stats[:, 0:1] / D
    inverse_std = lax.rsqrt(stats[:, 64:65] / D - average * average + EPSILON)
    normed = ((rows_ref[...] - average) * inverse_std * gain_ref[...][None, :]).astype(BF16)
    rows = normed.shape[0]
    place = lax.broadcasted_iota(jnp.int32, (rows, rows), 1) == source_ref[...]
    out_ref[...] = jnp.dot(
        jnp.where(place, 1.0, 0.0).astype(BF16), normed, preferred_element_type=F32
    ).astype(BF16)


def normed_rows(source, gain, rows, stats, after):
    return pl.pallas_call(
        norm_kernel,
        out_shape=pltpu.VMEM(rows.shape, BF16),
        in_specs=[whole()] * (3 + len(stats)) + [whole(pl.ANY)],
        out_specs=whole(),
        compiler_params=params(),
        cost_estimate=cost_of(rows),
    )(source, gain, rows, *stats, after)


def combine_kernel(chips, small, *refs):
    sent_ref, keep_ref = refs[:2]
    out_refs = refs[3 if small else 2 :]
    cols = keep_ref.shape[2]
    block = keep_ref.shape[1] // chips
    for index in range(chips):
        rows = slice(index * block, (index + 1) * block)
        total = keep_ref[:, rows] + sent_ref[:, rows, :cols].astype(F32)
        out_refs[index][:, :, :cols] = total.astype(out_refs[index].dtype)
        if small:
            sent = sent_ref[0, rows, cols:].astype(F32) + sent_ref[1, rows, cols:].astype(F32)
            total = refs[2][rows] + sent
            if index == chips - 1:
                out_refs[chips][...] = total
            else:
                store_split(out_refs[index], slice(cols, cols + small), total)


def combine(chips, sent, keep, keep_q=None):
    small = 0 if keep_q is None else keep_q.shape[1]
    block = keep.shape[1] // chips
    out_shape = [pltpu.VMEM((2, block, sent.shape[2]), BF16)] * (chips - 1)
    out_shape.append(pltpu.VMEM((2, block, keep.shape[2]), F32))
    if small:
        out_shape.append(pltpu.VMEM((block, small), F32))
    args = (sent, keep, keep_q) if small else (sent, keep)
    return pl.pallas_call(
        functools.partial(combine_kernel, chips, small),
        out_shape=out_shape,
        in_specs=[whole()] * len(args),
        out_specs=[whole()] * len(out_shape),
        compiler_params=params(),
        cost_estimate=cost_of(*args),
    )(*args)


def query_rows_kernel(count, source_ref, *refs):
    term_refs, out_refs = refs[:-count], refs[-count:]
    total = term_refs[0][...]
    rows, cols = total.shape
    for ref in term_refs[1:]:
        first = ref.shape[2] - cols
        total = total + (ref[0, :, first:].astype(F32) + ref[1, :, first:].astype(F32))
    place = lax.broadcasted_iota(jnp.int32, (rows, rows), 1) == source_ref[...]
    turned = jnp.dot(
        jnp.where(place, 1.0, 0.0).astype(BF16), total.astype(BF16), preferred_element_type=F32
    )
    each = rows // count
    for index, ref in enumerate(out_refs):
        ref[...] = turned[index * each : (index + 1) * each].astype(BF16)


def query_rows(source, terms, count):
    rows, cols = terms[0].shape
    return pl.pallas_call(
        functools.partial(query_rows_kernel, count),
        out_shape=[pltpu.VMEM((rows // count, cols), BF16)] * count,
        in_specs=[whole()] * (1 + len(terms)),
        out_specs=[whole()] * count,
        compiler_params=params(),
        cost_estimate=cost_of(*terms),
    )(source, *terms)


def gated_kernel(counts, ready, *refs):
    out_ref = refs[-1]
    local, wide, steps, _ = out_ref.shape
    taken, first = ready, 0
    for ref in refs[:ready]:
        out_ref[:, :, :, : ref.shape[3]] = ref[...]
        first = ref.shape[3]
    for count in counts:
        total = refs[taken][...]
        cols = total.shape[2]
        for ref in refs[taken + 1 : taken + count]:
            total = total + ref[:, :, :cols].astype(F32)
        taken += count
        gate, up = total[0], total[1]
        hidden = gate / (1.0 + jnp.exp(-gate)) * up
        for row in range(local * wide):
            piece = hidden[row * steps : (row + 1) * steps].astype(BF16)
            out_ref[row // wide, row % wide, :, first : first + cols] = piece
        first += cols


def gated(chunks, out_shape, ready=(), after=()):
    terms = [term for chunk in chunks for term in chunk]
    return pl.pallas_call(
        functools.partial(gated_kernel, [len(chunk) for chunk in chunks], len(ready)),
        out_shape=out_shape,
        in_specs=[whole()] * (len(ready) + len(terms)) + [whole(pl.ANY)] * len(after),
        out_specs=whole(),
        compiler_params=params(),
        cost_estimate=cost_of(*ready, *terms),
    )(*ready, *terms, *after)


def in_hbm(arrays):
    return [pltpu.with_memory_space_constraint(a, pltpu.HBM) for a in arrays]


def in_vmem(arrays):
    return [pltpu.with_memory_space_constraint(a, pltpu.VMEM) for a in arrays]


def tile_copies(w_refs, tile, place, sems):
    columns = pl.ds(pl.multiple_of(tile * TILE, TILE), TILE)
    return [
        pltpu.make_async_copy(
            ref.at[:, columns], place.at[:, index * TILE : (index + 1) * TILE], sems.at[index]
        )
        for index, ref in enumerate(w_refs)
    ]


def load_kernel(first, tiles, wg_ref, wu_ref, *refs):
    out_ref, sems = refs[-2:]

    def copies(tile):
        return tile_copies((wg_ref, wu_ref), first + tile, out_ref.at[tile], sems.at[tile])

    for tile in range(tiles):
        for copy in copies(tile):
            copy.start()
    for tile in range(tiles):
        for copy in copies(tile):
            copy.wait()


def load(weights, first, tiles, after):
    features = weights[0].shape[0]
    return pl.pallas_call(
        functools.partial(load_kernel, first, tiles),
        out_shape=pltpu.VMEM((tiles, features, 2 * TILE), BF16),
        in_specs=[whole(pltpu.HBM)] * 2 + [whole(pl.ANY)] * len(after),
        out_specs=whole(),
        scratch_shapes=[pltpu.SemaphoreType.DMA((tiles, 2))],
        compiler_params=params(),
        cost_estimate=pl.CostEstimate(
            flops=0, bytes_accessed=4 * features * TILE * tiles, transcendentals=0
        ),
    )(*in_hbm(weights), *after)


def store_split(ref, columns, value):
    high = value.astype(BF16)
    ref[0, :, columns] = high
    ref[1, :, columns] = (value - high.astype(F32)).astype(BF16)


def multiply(x_ref, place, tile, send_ref, keep_ref):
    part = jnp.dot(x_ref[...], place[...], preferred_element_type=F32)
    half = part.shape[0] // 2
    columns = pl.ds(pl.multiple_of(tile * TILE, TILE), TILE)
    for index in range(2):
        ref_columns = slice(index * TILE, (index + 1) * TILE)
        send_ref[index, :, columns] = part[:half, ref_columns].astype(BF16)
        keep_ref[index, :, columns] = part[half:, ref_columns]


def first_kernel(held, x_ref, wg_ref, wu_ref, wq_ref, wkv_ref, *refs):
    pre_refs = refs[:held]
    send_ref, keep_ref, keep_q_ref, next_ref, q_ref, kv_ref, small_sems, next_sems = refs[held:]
    tiles = sum(ref.shape[0] for ref in pre_refs)
    half = x_ref.shape[0] // 2
    smalls = [
        pltpu.make_async_copy(wq_ref, q_ref, small_sems.at[0]),
        pltpu.make_async_copy(wkv_ref, kv_ref, small_sems.at[1]),
    ]
    for copy in smalls:
        copy.start()

    def fetch_next(index):
        return tile_copies((wg_ref, wu_ref), tiles + index, next_ref.at[index], next_sems.at[index])

    for index in range(next_ref.shape[0]):
        for copy in fetch_next(index):
            copy.start()
    done = 0
    for ref in pre_refs:

        def from_held(index, carry, ref=ref, done=done):
            multiply(x_ref, ref.at[index], done + index, send_ref, keep_ref)
            return carry

        lax.fori_loop(0, ref.shape[0], from_held, 0)
        done += ref.shape[0]
    taken = 0
    for copy, ref in zip(smalls, (q_ref, kv_ref)):
        copy.wait()
        cols = ref.shape[1]
        part = jnp.dot(x_ref[...], ref[...], preferred_element_type=F32)
        store_split(send_ref, slice(tiles * TILE + taken, tiles * TILE + taken + cols), part[:half])
        keep_q_ref[:, taken : taken + cols] = part[half:]
        taken += cols
    for index in range(next_ref.shape[0]):
        for copy in fetch_next(index):
            copy.wait()


def first_sums(x, weights, w_query, w_keyval, held, following):
    rows, features = x.shape
    tiles = sum(h.shape[0] for h in held)
    cols, small = tiles * TILE, w_query.shape[1] + w_keyval.shape[1]
    return pl.pallas_call(
        functools.partial(first_kernel, len(held)),
        out_shape=[
            pltpu.VMEM((2, rows // 2, cols + small), BF16),
            pltpu.VMEM((2, rows // 2, cols), F32),
            pltpu.VMEM((rows // 2, small), F32),
            pltpu.VMEM((following, features, 2 * TILE), BF16),
        ],
        in_specs=[whole()] + [whole(pltpu.HBM)] * 4 + [whole()] * len(held),
        out_specs=[whole()] * 4,
        scratch_shapes=[
            pltpu.VMEM(w_query.shape, BF16),
            pltpu.VMEM(w_keyval.shape, BF16),
            pltpu.SemaphoreType.DMA((2,)),
            pltpu.SemaphoreType.DMA((following, 2)),
        ],
        compiler_params=params(),
        cost_estimate=pl.CostEstimate(
            flops=2 * rows * features * (2 * cols + small),
            bytes_accessed=4 * features * cols,
            transcendentals=0,
        ),
    )(x, *in_hbm((*weights, w_query, w_keyval)), *in_vmem(held))


def wide_kernel(first, tiles, following, after, x_ref, wg_ref, wu_ref, pre_ref, *refs):
    send_ref, keep_ref = refs[after : after + 2]
    next_ref = refs[after + 2] if following else None
    ring, ring_sems, next_sems = refs[-3:]
    held, depth = pre_ref.shape[0], ring.shape[0]
    streamed = tiles - held

    def fetch(index):
        slot = lax.rem(index, depth)
        return tile_copies((wg_ref, wu_ref), first + held + index, ring.at[slot], ring_sems.at[slot])

    def fetch_next(index):
        return tile_copies((wg_ref, wu_ref), first + tiles + index, next_ref.at[index], next_sems.at[index])

    def start(copies):
        for copy in copies:
            copy.start()

    early = min(depth, streamed)
    for index in range(early):
        start(fetch(index))
    early_next = min(following, depth - early)
    for index in range(early_next):
        start(fetch_next(index))

    def from_held(index, carry):
        multiply(x_ref, pre_ref.at[index], index, send_ref, keep_ref)
        return carry

    lax.fori_loop(0, held, from_held, 0)

    def from_ring(index, carry):
        for copy in fetch(index):
            copy.wait()
        multiply(x_ref, ring.at[lax.rem(index, depth)], held + index, send_ref, keep_ref)

        @pl.when(index + depth < streamed)
        def _():
            start(fetch(index + depth))

        if following > early_next:
            later = index + early_next + depth - streamed

            @pl.when((later >= early_next) & (later < following))
            def _():
                start(fetch_next(later))

        return carry

    lax.fori_loop(0, streamed, from_ring, 0)
    for index in range(following):
        for copy in fetch_next(index):
            copy.wait()


def wide_sums(x, weights, held, first, tiles, following, after):
    rows, features = x.shape
    cols = tiles * TILE
    streamed = tiles - held.shape[0]
    depth = min(DEPTH, max(streamed, 1))
    out_shape = [
        pltpu.VMEM((2, rows // 2, cols), BF16),
        pltpu.VMEM((2, rows // 2, cols), F32),
    ]
    if following:
        out_shape.append(pltpu.VMEM((following, features, 2 * TILE), BF16))
    return pl.pallas_call(
        functools.partial(wide_kernel, first, tiles, following, len(after)),
        out_shape=out_shape,
        in_specs=[whole(), whole(pltpu.HBM), whole(pltpu.HBM), whole()]
        + [whole(pl.ANY)] * len(after),
        out_specs=[whole()] * len(out_shape),
        scratch_shapes=[
            pltpu.VMEM((depth, features, 2 * TILE), BF16),
            pltpu.SemaphoreType.DMA((depth, 2)),
            pltpu.SemaphoreType.DMA((max(following, 1), 2)),
        ],
        compiler_params=params(),
        cost_estimate=pl.CostEstimate(
            flops=4 * rows * features * cols,
            bytes_accessed=4 * features * TILE * (streamed + following),
            transcendentals=0,
        ),
    )(x, *in_hbm(weights), *in_vmem((held,)), *after)


def attend_kernel(count, steps, query_cols, slot_ref, lengths_ref, cache_ref, *refs):
    part_refs, (out_ref, held, fresh) = refs[:count], refs[-3:]
    for index, ref in enumerate(part_refs):
        held[slot_ref[index]] = ref[...].astype(F32)
    pair_cols = held.shape[2] - query_cols
    heads = query_cols // HD
    scale = HD ** (-0.5)
    batch, positions = cache_ref.shape[0], cache_ref.shape[1]
    fresh[...] = jnp.zeros_like(fresh)
    for b in range(batch):
        rows = pl.ds(b * steps, steps)
        for c in range(count):
            fresh[b, :steps, c * pair_cols : (c + 1) * pair_cols] = held[c, rows, query_cols:]
        queries = jnp.concatenate(
            [held[c, rows, h * HD : (h + 1) * HD] for c in range(count) for h in range(heads)],
            axis=0,
        ).astype(BF16)
        pairs = fresh[b].astype(BF16)
        dims = (((1,), (1,)), ((), ()))
        old = lax.dot_general(
            queries, cache_ref[b, :, :HD], dims, preferred_element_type=F32
        ) * scale
        position = lax.broadcasted_iota(jnp.int32, old.shape, 1)
        old = jnp.where(position < lengths_ref[b, 0], old, MASKED)
        new = lax.dot_general(queries, pairs[:, :HD], dims, preferred_element_type=F32) * scale
        step = lax.broadcasted_iota(jnp.int32, new.shape, 0) % steps
        new = jnp.where(lax.broadcasted_iota(jnp.int32, new.shape, 1) <= step, new, MASKED)
        highest = jnp.maximum(
            jnp.max(old, axis=-1, keepdims=True), jnp.max(new, axis=-1, keepdims=True)
        )
        old = jnp.exp(old - highest)
        new = jnp.exp(new - highest)
        total = jnp.sum(old, axis=-1, keepdims=True) + jnp.sum(new, axis=-1, keepdims=True)
        context = jnp.dot(
            (old / total).astype(BF16), cache_ref[b, :, HD:], preferred_element_type=F32
        ) + jnp.dot((new / total).astype(BF16), pairs[:, HD:], preferred_element_type=F32)
        for h in range(HEADS):
            piece = context[h * steps : (h + 1) * steps].astype(BF16)
            out_ref[b, 0, :, h * HD : (h + 1) * HD] = piece


def attend(slots, lengths, cache, parts, steps, query_cols, after):
    batch = cache.shape[0]
    count = len(parts)
    rows, cols = parts[0].shape
    return pl.pallas_call(
        functools.partial(attend_kernel, count, steps, query_cols),
        out_shape=jax.ShapeDtypeStruct((batch, 1, steps, HEADS * HD), BF16),
        in_specs=[whole(pltpu.SMEM), whole(pltpu.SMEM)] + [whole()] * (1 + count) + [whole(pl.ANY)] * len(after),
        out_specs=whole(),
        scratch_shapes=[
            pltpu.VMEM((count, rows, cols), F32),
            pltpu.VMEM((batch, 8, 2 * HD), F32),
        ],
        compiler_params=params(),
        cost_estimate=pl.CostEstimate(
            flops=4 * batch * steps * HEADS * HD * cache.shape[1],
            bytes_accessed=2 * cache.size,
            transcendentals=batch * steps * HEADS * cache.shape[1],
        ),
    )(slots, lengths, cache, *parts, *after)


def on_device(tokens, gain, w_query, w_keyval, w_gate, w_up, cache, lengths):
    size_x, size_y = lax.axis_size("gx"), lax.axis_size("gy")
    chips = size_y // 2
    me_x, me_y = lax.axis_index("gx"), lax.axis_index("gy")
    tall, _, steps, features = tokens.shape
    local = cache.shape[0]
    block = local * size_x * steps

    def shift_x(value, by):
        return lax.ppermute(value, "gx", [(i, (i + by) % size_x) for i in range(size_x)])

    def shift_y(value, by):
        return lax.ppermute(value, "gy", [(i, (i + by) % size_y) for i in range(size_y)])

    def swap(value):
        return lax.ppermute(value, "gy", [(i, i ^ 1) for i in range(size_y)])

    row = jnp.arange(2 * chips * block, dtype=jnp.int32)
    core = jnp.where(row < chips * block, 1 - me_y % 2, me_y % 2)
    chip = (me_y // 2 + 1 + row // block % chips) % chips
    sequence = (chip * 2 + core) * local + row % block // (size_x * steps)
    column = row // steps % size_x
    source = (me_x - column) % size_x * (tall * steps) + sequence * steps + row % steps
    source = source[:, None]
    row = jnp.arange(block, dtype=jnp.int32)
    to = (me_x + row // (local * steps)) % size_x
    order = row // steps % local * (size_x * steps) + to * steps + row % steps
    order = order[:, None]
    slots = (me_x - jnp.arange(size_x, dtype=jnp.int32)) % size_x

    weights = (w_gate, w_up)
    tiles = w_gate.shape[1] // TILE
    before = [tiles * share // 36 for share in (4, 5)]
    bounds = [0, sum(before)] + [tiles * share // 36 for share in (23, 31, 36)]
    ahead = [max(1, tiles * share // 36) for share in (5, 3, 3)] + [0]
    gathered = [tokens] + [shift_x(tokens, by) for by in range(1, size_x)]
    first_tiles = load(weights, 0, before[0], (source, order, slots))
    rows, stats = partial_stats(gathered, first_tiles)
    every_stat = [stats] + [shift_y(stats, by) for by in range(1, size_y)]
    second_tiles = load(weights, before[0], before[1], (stats,))
    x = normed_rows(source, gain, rows, every_stat, second_tiles)

    def chunk_sums(chunk, held, after):
        count = bounds[chunk + 1] - bounds[chunk]
        return wide_sums(x, weights, held, bounds[chunk], count, ahead[chunk], after)

    def to_chips(parts):
        return [shift_y(part, 2 * by) for by, part in enumerate(parts[: chips - 1], 1)]

    send_0, keep_0, keep_q, held = first_sums(
        x, weights, w_query, w_keyval, (first_tiles, second_tiles), ahead[0]
    )
    send_1, keep_1, held = chunk_sums(1, held, (send_0,))
    parts_0 = combine(chips, swap(send_0), keep_0, keep_q)
    from_0 = to_chips(parts_0)

    send_2, keep_2, held = chunk_sums(2, held, (parts_0[0], send_1))
    parts_1 = combine(chips, swap(send_1), keep_1)
    from_1 = to_chips(parts_1)
    turned = query_rows(order, [parts_0[-1]] + from_0, size_x)
    new = [turned[0]] + [shift_x(turned[by], by) for by in range(1, size_x)]

    send_3, keep_3 = chunk_sums(3, held, (parts_1[0], turned[0], send_2))
    parts_2 = combine(chips, swap(send_2), keep_2)
    from_2 = to_chips(parts_2)
    context = attend(
        slots,
        lengths,
        cache.reshape(local, cache.shape[2], cache.shape[3]),
        new,
        steps,
        w_query.shape[1],
        (parts_2[0], send_3, from_1[0]),
    )
    parts_3 = combine(chips, swap(send_3), keep_3)
    from_3 = to_chips(parts_3)
    half_done = gated(
        [[parts_0[chips - 1]] + from_0, [parts_1[-1]] + from_1],
        pltpu.VMEM((local, size_x, steps, bounds[2] * TILE), BF16),
        (),
        (parts_3[0],),
    )
    hidden = gated(
        [[parts_2[-1]] + from_2, [parts_3[-1]] + from_3],
        jax.ShapeDtypeStruct((local, size_x, steps, w_gate.shape[1]), BF16),
        (half_done,),
    )
    return (context, hidden)


def solution(mesh):
    return jax.shard_map(
        on_device,
        mesh=mesh,
        in_specs=(
            P("groups", "gx", None, "gy"),
            P("gy"),
            P("gy", "gx"),
            P("gy", "gx"),
            P("gy", "gx"),
            P("gy", "gx"),
            P(("groups", "gy"), "gx", None, None),
            P(("groups", "gy"), "gx"),
        ),
        out_specs=(P(("groups", "gy"), "gx", None, None), P(("groups", "gy"), None, None, "gx")),
        check_vma=False,
    )
```

```python
import functools

import jax
import jax.numpy as jnp
from jax import lax
from jax.experimental import pallas as pl
from jax.experimental.pallas import tpu as pltpu
from jax.sharding import PartitionSpec as P

D = 9216
HEADS = 24
HD = 256
EPSILON = 1e-05
MASKED = -1e30
MIB = 1024 * 1024
TILE = 256
DEPTH = 6
WIDE = 15
F32 = jnp.float32
BF16 = jnp.bfloat16


def whole(memory_space=pltpu.VMEM):
    return pl.BlockSpec(memory_space=memory_space)


def cost_of(*arrays):
    size = sum(a.size for a in arrays)
    return pl.CostEstimate(flops=size, bytes_accessed=size // 16, transcendentals=0)


def params(mib=9):
    return pltpu.CompilerParams(vmem_limit_bytes=mib * MIB)


def stats_kernel(count, *refs):
    token_refs, (rows_ref, out_ref) = refs[:count], refs[-2:]
    tall, _, steps, features = token_refs[0].shape
    for index, ref in enumerate(token_refs):
        for t in range(tall):
            first = (index * tall + t) * steps
            rows_ref[first : first + steps] = ref[t, 0].astype(F32)
    floats = rows_ref[...]
    sums = jnp.sum(floats, axis=-1, keepdims=True)
    squares = jnp.sum(floats * floats, axis=-1, keepdims=True)
    lane = lax.broadcasted_iota(jnp.int32, out_ref.shape, 1)
    out_ref[...] = jnp.where(lane < 64, sums, squares)


def partial_stats(tokens, after):
    tall, _, steps, features = tokens[0].shape
    rows = len(tokens) * tall * steps
    return pl.pallas_call(
        functools.partial(stats_kernel, len(tokens)),
        out_shape=(pltpu.VMEM((rows, features), F32), pltpu.VMEM((rows, 128), F32)),
        in_specs=[whole()] * len(tokens) + [whole(pl.ANY)],
        out_specs=(whole(), whole()),
        compiler_params=params(),
        cost_estimate=cost_of(*tokens),
    )(*tokens, after)


def norm_kernel(source_ref, gain_ref, rows_ref, *refs):
    stat_refs, out_ref = refs[:-2], refs[-1]
    stats = stat_refs[0][...]
    for ref in stat_refs[1:]:
        stats = stats + ref[...]
    average = stats[:, 0:1] / D
    inverse_std = lax.rsqrt(stats[:, 64:65] / D - average * average + EPSILON)
    normed = ((rows_ref[...] - average) * inverse_std * gain_ref[...][None, :]).astype(BF16)
    rows = normed.shape[0]
    place = lax.broadcasted_iota(jnp.int32, (rows, rows), 1) == source_ref[...]
    out_ref[...] = jnp.dot(
        jnp.where(place, 1.0, 0.0).astype(BF16), normed, preferred_element_type=F32
    ).astype(BF16)


def normed_rows(source, gain, rows, stats, after):
    return pl.pallas_call(
        norm_kernel,
        out_shape=pltpu.VMEM(rows.shape, BF16),
        in_specs=[whole()] * (3 + len(stats)) + [whole(pl.ANY)],
        out_specs=whole(),
        compiler_params=params(),
        cost_estimate=cost_of(rows),
    )(source, gain, rows, *stats, after)


def combine_kernel(chips, small, skip, *refs):
    sent_ref, keep_ref = refs[:2]
    out_refs = refs[skip:]
    cols = keep_ref.shape[2]
    block = keep_ref.shape[1] // chips
    for index in range(chips):
        rows = slice(index * block, (index + 1) * block)
        total = keep_ref[:, rows] + sent_ref[:, rows, :cols].astype(F32)
        out_refs[index][:, :, :cols] = total.astype(out_refs[index].dtype)
        if small:
            sent = sent_ref[0, rows, cols:].astype(F32) + sent_ref[1, rows, cols:].astype(F32)
            total = refs[2][rows] + sent
            if index == chips - 1:
                out_refs[chips][...] = total
            else:
                store_split(out_refs[index], slice(cols, cols + small), total)


def combine(chips, sent, keep, keep_q=None, carry=None, after=()):
    small = 0 if keep_q is None else keep_q.shape[1]
    block = keep.shape[1] // chips
    out_shape = [pltpu.VMEM((2, block, sent.shape[2]), BF16)] * (chips - 1)
    out_shape.append(pltpu.VMEM((2, block, keep.shape[2]), F32))
    if small:
        out_shape.append(pltpu.VMEM((block, small), F32))
    args = (sent, keep, keep_q) if small else (sent, keep)
    extra = [*after] if carry is None else [*after, *in_vmem((carry,))]
    out_specs = [whole()] * len(out_shape)
    aliases = {}
    if carry is not None:
        aliases = {len(args) + len(after): len(out_shape)}
        out_shape.append(pltpu.VMEM(carry.shape, carry.dtype))
        out_specs.append(whole())
    return pl.pallas_call(
        functools.partial(combine_kernel, chips, small, len(args) + len(extra)),
        out_shape=out_shape,
        in_specs=[whole()] * len(args)
        + [whole(pl.ANY)] * len(after)
        + [whole()] * (len(extra) - len(after)),
        out_specs=out_specs,
        input_output_aliases=aliases,
        compiler_params=params(),
        cost_estimate=cost_of(*args),
    )(*args, *extra)


def query_rows_kernel(count, source_ref, *refs):
    term_refs, out_refs = refs[:-count], refs[-count:]
    total = term_refs[0][...]
    rows, cols = total.shape
    for ref in term_refs[1:]:
        first = ref.shape[2] - cols
        total = total + (ref[0, :, first:].astype(F32) + ref[1, :, first:].astype(F32))
    place = lax.broadcasted_iota(jnp.int32, (rows, rows), 1) == source_ref[...]
    turned = jnp.dot(
        jnp.where(place, 1.0, 0.0).astype(BF16), total.astype(BF16), preferred_element_type=F32
    )
    each = rows // count
    for index, ref in enumerate(out_refs):
        ref[...] = turned[index * each : (index + 1) * each].astype(BF16)


def query_rows(source, terms, count):
    rows, cols = terms[0].shape
    return pl.pallas_call(
        functools.partial(query_rows_kernel, count),
        out_shape=[pltpu.VMEM((rows // count, cols), BF16)] * count,
        in_specs=[whole()] * (1 + len(terms)),
        out_specs=[whole()] * count,
        compiler_params=params(),
        cost_estimate=cost_of(*terms),
    )(source, *terms)


def gated_kernel(counts, ready, *refs):
    out_ref = refs[-1]
    local, wide, steps, _ = out_ref.shape
    taken, first = ready, 0
    for ref in refs[:ready]:
        out_ref[:, :, :, : ref.shape[3]] = ref[...]
        first = ref.shape[3]
    for count in counts:
        total = refs[taken][...]
        cols = total.shape[2]
        for ref in refs[taken + 1 : taken + count]:
            total = total + ref[:, :, :cols].astype(F32)
        taken += count
        gate, up = total[0], total[1]
        hidden = gate / (1.0 + jnp.exp(-gate)) * up
        for row in range(local * wide):
            piece = hidden[row * steps : (row + 1) * steps].astype(BF16)
            out_ref[row // wide, row % wide, :, first : first + cols] = piece
        first += cols


def gated(chunks, out_shape, ready=(), after=()):
    terms = [term for chunk in chunks for term in chunk]
    return pl.pallas_call(
        functools.partial(gated_kernel, [len(chunk) for chunk in chunks], len(ready)),
        out_shape=out_shape,
        in_specs=[whole()] * (len(ready) + len(terms)) + [whole(pl.ANY)] * len(after),
        out_specs=whole(),
        compiler_params=params(),
        cost_estimate=cost_of(*ready, *terms),
    )(*ready, *terms, *after)


def in_hbm(arrays):
    return [pltpu.with_memory_space_constraint(a, pltpu.HBM) for a in arrays]


def in_vmem(arrays):
    return [pltpu.with_memory_space_constraint(a, pltpu.VMEM) for a in arrays]


def tile_copies(w_refs, tile, place, sems):
    columns = pl.ds(pl.multiple_of(tile * TILE, TILE), TILE)
    return [
        pltpu.make_async_copy(
            ref.at[:, columns], place.at[:, index * TILE : (index + 1) * TILE], sems.at[index]
        )
        for index, ref in enumerate(w_refs)
    ]


def load_kernel(first, tiles, wg_ref, wu_ref, *refs):
    out_ref, sems = refs[-2:]

    def copies(tile):
        return tile_copies((wg_ref, wu_ref), first + tile, out_ref.at[tile], sems.at[tile])

    for tile in range(tiles):
        for copy in copies(tile):
            copy.start()
    for tile in range(tiles):
        for copy in copies(tile):
            copy.wait()


def load(weights, first, tiles, after):
    features = weights[0].shape[0]
    return pl.pallas_call(
        functools.partial(load_kernel, first, tiles),
        out_shape=pltpu.VMEM((tiles, features, 2 * TILE), BF16),
        in_specs=[whole(pltpu.HBM)] * 2 + [whole(pl.ANY)] * len(after),
        out_specs=whole(),
        scratch_shapes=[pltpu.SemaphoreType.DMA((tiles, 2))],
        compiler_params=params(),
        cost_estimate=pl.CostEstimate(
            flops=0, bytes_accessed=4 * features * TILE * tiles, transcendentals=0
        ),
    )(*in_hbm(weights), *after)


def store_split(ref, columns, value):
    high = value.astype(BF16)
    ref[0, :, columns] = high
    ref[1, :, columns] = (value - high.astype(F32)).astype(BF16)


def multiply(x_ref, place, tile, send_ref, keep_ref):
    part = jnp.dot(x_ref[...], place[...], preferred_element_type=F32)
    half = part.shape[0] // 2
    columns = pl.ds(pl.multiple_of(tile * TILE, TILE), TILE)
    for index in range(2):
        ref_columns = slice(index * TILE, (index + 1) * TILE)
        send_ref[index, :, columns] = part[:half, ref_columns].astype(BF16)
        keep_ref[index, :, columns] = part[half:, ref_columns]


def first_kernel(held, x_ref, wg_ref, wu_ref, wq_ref, wkv_ref, *refs):
    pre_refs = refs[:held]
    send_ref, keep_ref, keep_q_ref, next_ref, q_ref, kv_ref, small_sems, next_sems = refs[held:]
    tiles = sum(ref.shape[0] for ref in pre_refs)
    half = x_ref.shape[0] // 2
    smalls = [
        pltpu.make_async_copy(wq_ref, q_ref, small_sems.at[0]),
        pltpu.make_async_copy(wkv_ref, kv_ref, small_sems.at[1]),
    ]
    for copy in smalls:
        copy.start()

    def fetch_next(index):
        return tile_copies((wg_ref, wu_ref), tiles + index, next_ref.at[index], next_sems.at[index])

    for index in range(next_ref.shape[0]):
        for copy in fetch_next(index):
            copy.start()
    done = 0
    for ref in pre_refs:
        for index in range(ref.shape[0]):
            multiply(x_ref, ref.at[index], done + index, send_ref, keep_ref)
        done += ref.shape[0]
    taken = 0
    for copy, ref in zip(smalls, (q_ref, kv_ref)):
        copy.wait()
        cols = ref.shape[1]
        part = jnp.dot(x_ref[...], ref[...], preferred_element_type=F32)
        store_split(send_ref, slice(tiles * TILE + taken, tiles * TILE + taken + cols), part[:half])
        keep_q_ref[:, taken : taken + cols] = part[half:]
        taken += cols
    for index in range(next_ref.shape[0]):
        for copy in fetch_next(index):
            copy.wait()


def first_sums(x, weights, w_query, w_keyval, held, following):
    rows, features = x.shape
    tiles = sum(h.shape[0] for h in held)
    cols, small = tiles * TILE, w_query.shape[1] + w_keyval.shape[1]
    return pl.pallas_call(
        functools.partial(first_kernel, len(held)),
        out_shape=[
            pltpu.VMEM((2, rows // 2, cols + small), BF16),
            pltpu.VMEM((2, rows // 2, cols), F32),
            pltpu.VMEM((rows // 2, small), F32),
            pltpu.VMEM((following, features, 2 * TILE), BF16),
        ],
        in_specs=[whole()] + [whole(pltpu.HBM)] * 4 + [whole()] * len(held),
        out_specs=[whole()] * 4,
        scratch_shapes=[
            pltpu.VMEM(w_query.shape, BF16),
            pltpu.VMEM(w_keyval.shape, BF16),
            pltpu.SemaphoreType.DMA((2,)),
            pltpu.SemaphoreType.DMA((following, 2)),
        ],
        compiler_params=params(),
        cost_estimate=pl.CostEstimate(
            flops=2 * rows * features * (2 * cols + small),
            bytes_accessed=4 * features * cols,
            transcendentals=0,
        ),
    )(x, *in_hbm((*weights, w_query, w_keyval)), *in_vmem(held))


def wide_kernel(first, tiles, following, after, x_ref, wg_ref, wu_ref, pre_ref, *refs):
    send_ref, keep_ref = refs[after : after + 2]
    next_ref = refs[after + 2] if following else None
    ring, ring_sems, next_sems = refs[-3:]
    held, depth = pre_ref.shape[0], ring.shape[0]
    streamed = tiles - held

    def fetch(index):
        slot = lax.rem(index, depth)
        return tile_copies((wg_ref, wu_ref), first + held + index, ring.at[slot], ring_sems.at[slot])

    def fetch_next(index):
        return tile_copies((wg_ref, wu_ref), first + tiles + index, next_ref.at[index], next_sems.at[index])

    def start(copies):
        for copy in copies:
            copy.start()

    early = min(depth, streamed)
    for index in range(early):
        start(fetch(index))
    early_next = min(following, DEPTH - early)
    for index in range(early_next):
        start(fetch_next(index))

    for index in range(held):
        multiply(x_ref, pre_ref.at[index], index, send_ref, keep_ref)

    def from_ring(index, carry):
        for copy in fetch(index):
            copy.wait()
        multiply(x_ref, ring.at[lax.rem(index, depth)], held + index, send_ref, keep_ref)

        @pl.when(index + depth < streamed)
        def _():
            start(fetch(index + depth))

        if following > early_next:
            later = index + early_next + depth - streamed

            @pl.when((later >= early_next) & (later < following))
            def _():
                start(fetch_next(later))

        return carry

    lax.fori_loop(0, streamed, from_ring, 0)
    for index in range(following):
        for copy in fetch_next(index):
            copy.wait()


def wide_sums(x, weights, held, first, tiles, following, after):
    rows, features = x.shape
    cols = tiles * TILE
    streamed = tiles - held.shape[0]
    depth = min(DEPTH, max(streamed, 1))
    out_shape = [
        pltpu.VMEM((2, rows // 2, cols), BF16),
        pltpu.VMEM((2, rows // 2, cols), F32),
    ]
    if following:
        out_shape.append(pltpu.VMEM((following, features, 2 * TILE), BF16))
    return pl.pallas_call(
        functools.partial(wide_kernel, first, tiles, following, len(after)),
        out_shape=out_shape,
        in_specs=[whole(), whole(pltpu.HBM), whole(pltpu.HBM), whole()]
        + [whole(pl.ANY)] * len(after),
        out_specs=[whole()] * len(out_shape),
        scratch_shapes=[
            pltpu.VMEM((depth, features, 2 * TILE), BF16),
            pltpu.SemaphoreType.DMA((depth, 2)),
            pltpu.SemaphoreType.DMA((max(following, 1), 2)),
        ],
        compiler_params=params(WIDE),
        cost_estimate=pl.CostEstimate(
            flops=4 * rows * features * cols,
            bytes_accessed=4 * features * TILE * (streamed + following),
            transcendentals=0,
        ),
    )(x, *in_hbm(weights), *in_vmem((held,)), *after)


def attend_kernel(count, steps, query_cols, slot_ref, lengths_ref, cache_ref, *refs):
    part_refs, (out_ref, held, fresh) = refs[:count], refs[-3:]
    for index, ref in enumerate(part_refs):
        held[slot_ref[index]] = ref[...].astype(F32)
    pair_cols = held.shape[2] - query_cols
    heads = query_cols // HD
    scale = HD ** (-0.5)
    batch, positions = cache_ref.shape[0], cache_ref.shape[1]
    fresh[...] = jnp.zeros_like(fresh)
    for b in range(batch):
        rows = pl.ds(b * steps, steps)
        for c in range(count):
            fresh[b, :steps, c * pair_cols : (c + 1) * pair_cols] = held[c, rows, query_cols:]
        queries = jnp.concatenate(
            [held[c, rows, h * HD : (h + 1) * HD] for c in range(count) for h in range(heads)],
            axis=0,
        ).astype(BF16)
        pairs = fresh[b].astype(BF16)
        dims = (((1,), (1,)), ((), ()))
        old = lax.dot_general(
            queries, cache_ref[b, :, :HD], dims, preferred_element_type=F32
        ) * scale
        position = lax.broadcasted_iota(jnp.int32, old.shape, 1)
        old = jnp.where(position < lengths_ref[b], old, MASKED)
        new = lax.dot_general(queries, pairs[:, :HD], dims, preferred_element_type=F32) * scale
        step = lax.broadcasted_iota(jnp.int32, new.shape, 0) % steps
        new = jnp.where(lax.broadcasted_iota(jnp.int32, new.shape, 1) <= step, new, MASKED)
        highest = jnp.maximum(
            jnp.max(old, axis=-1, keepdims=True), jnp.max(new, axis=-1, keepdims=True)
        )
        old = jnp.exp(old - highest)
        new = jnp.exp(new - highest)
        total = jnp.sum(old, axis=-1, keepdims=True) + jnp.sum(new, axis=-1, keepdims=True)
        context = jnp.dot(
            (old / total).astype(BF16), cache_ref[b, :, HD:], preferred_element_type=F32
        ) + jnp.dot((new / total).astype(BF16), pairs[:, HD:], preferred_element_type=F32)
        for h in range(HEADS):
            piece = context[h * steps : (h + 1) * steps].astype(BF16)
            out_ref[b, 0, :, h * HD : (h + 1) * HD] = piece


def attend(slots, lengths, cache, parts, steps, query_cols, after):
    batch = cache.shape[0]
    count = len(parts)
    rows, cols = parts[0].shape
    return pl.pallas_call(
        functools.partial(attend_kernel, count, steps, query_cols),
        out_shape=jax.ShapeDtypeStruct((batch, 1, steps, HEADS * HD), BF16),
        in_specs=[whole(pltpu.SMEM), whole(pltpu.SMEM)] + [whole()] * (1 + count) + [whole(pl.ANY)] * len(after),
        out_specs=whole(),
        scratch_shapes=[
            pltpu.VMEM((count, rows, cols), F32),
            pltpu.VMEM((batch, 8, 2 * HD), F32),
        ],
        compiler_params=params(),
        cost_estimate=pl.CostEstimate(
            flops=4 * batch * steps * HEADS * HD * cache.shape[1],
            bytes_accessed=2 * cache.size,
            transcendentals=batch * steps * HEADS * cache.shape[1],
        ),
    )(slots, lengths, cache, *parts, *after)


def on_device(tokens, gain, w_query, w_keyval, w_gate, w_up, cache, lengths):
    size_x, size_y = lax.axis_size("gx"), lax.axis_size("gy")
    chips = size_y // 2
    me_x, me_y = lax.axis_index("gx"), lax.axis_index("gy")
    tall, _, steps, features = tokens.shape
    local = cache.shape[0]
    block = local * size_x * steps

    def shift_x(value, by):
        return lax.ppermute(value, "gx", [(i, (i + by) % size_x) for i in range(size_x)])

    def shift_y(value, by):
        return lax.ppermute(value, "gy", [(i, (i + by) % size_y) for i in range(size_y)])

    def swap(value):
        return lax.ppermute(value, "gy", [(i, i ^ 1) for i in range(size_y)])

    row = jnp.arange(2 * chips * block, dtype=jnp.int32)
    core = jnp.where(row < chips * block, 1 - me_y % 2, me_y % 2)
    chip = (me_y // 2 + 1 + row // block % chips) % chips
    sequence = (chip * 2 + core) * local + row % block // (size_x * steps)
    column = row // steps % size_x
    source = (me_x - column) % size_x * (tall * steps) + sequence * steps + row % steps
    source = source[:, None]
    row = jnp.arange(block, dtype=jnp.int32)
    to = (me_x + row // (local * steps)) % size_x
    order = row // steps % local * (size_x * steps) + to * steps + row % steps
    order = order[:, None]
    slots = (me_x - jnp.arange(size_x, dtype=jnp.int32)) % size_x

    weights = (w_gate, w_up)
    tiles = w_gate.shape[1] // TILE
    before = [tiles * share // 36 for share in (4, 5)]
    bounds = [0, sum(before)] + [tiles * share // 36 for share in (21, 30, 36)]
    ahead = [max(1, tiles * share // 36) for share in (5, 4, 4)] + [0]
    gathered = [tokens] + [shift_x(tokens, by) for by in range(1, size_x)]
    first_tiles = load(weights, 0, before[0], (source, order, slots))
    rows, stats = partial_stats(gathered, first_tiles)
    every_stat = [stats] + [shift_y(stats, by) for by in range(1, size_y)]
    second_tiles = load(weights, before[0], before[1], (stats,))
    x = normed_rows(source, gain, rows, every_stat, second_tiles)

    def chunk_sums(chunk, held, after):
        count = bounds[chunk + 1] - bounds[chunk]
        return wide_sums(x, weights, held, bounds[chunk], count, ahead[chunk], after)

    def to_chips(parts):
        return [shift_y(part, 2 * by) for by, part in enumerate(parts[: chips - 1], 1)]

    send_0, keep_0, keep_q, held = first_sums(
        x, weights, w_query, w_keyval, (first_tiles, second_tiles), ahead[0]
    )
    send_1, keep_1, held = chunk_sums(1, held, (send_0,))
    parts_0 = combine(chips, swap(send_0), keep_0, keep_q)
    from_0 = to_chips(parts_0)

    send_2, keep_2, held = chunk_sums(2, held, (parts_0[0], send_1))
    parts_1 = combine(chips, swap(send_1), keep_1)
    from_1 = to_chips(parts_1)
    turned = query_rows(order, [parts_0[-1]] + from_0, size_x)
    new = [turned[0]] + [shift_x(turned[by], by) for by in range(1, size_x)]

    send_3, keep_3 = chunk_sums(3, held, (parts_1[0], turned[0], send_2))
    *parts_2, send_3 = combine(chips, swap(send_2), keep_2, None, send_3, (*new[1:], from_1[0]))
    from_2 = to_chips(parts_2)
    context = attend(
        slots,
        lengths.reshape(local),
        cache.reshape(local, cache.shape[2], cache.shape[3]),
        new,
        steps,
        w_query.shape[1],
        (parts_2[0], send_3),
    )
    parts_3 = combine(chips, swap(send_3), keep_3)
    from_3 = to_chips(parts_3)
    half_done = gated(
        [[parts_0[chips - 1]] + from_0, [parts_1[-1]] + from_1],
        pltpu.VMEM((local, size_x, steps, bounds[2] * TILE), BF16),
        (),
        (parts_3[0],),
    )
    hidden = gated(
        [[parts_2[-1]] + from_2, [parts_3[-1]] + from_3],
        jax.ShapeDtypeStruct((local, size_x, steps, w_gate.shape[1]), BF16),
        (half_done,),
    )
    return (context, hidden)


def solution(mesh):
    return jax.shard_map(
        on_device,
        mesh=mesh,
        in_specs=(
            P("groups", "gx", None, "gy"),
            P("gy"),
            P("gy", "gx"),
            P("gy", "gx"),
            P("gy", "gx"),
            P("gy", "gx"),
            P(("groups", "gy"), "gx", None, None),
            P(("groups", "gy"), "gx"),
        ),
        out_specs=(P(("groups", "gy"), "gx", None, None), P(("groups", "gy"), None, None, "gx")),
        check_vma=False,
    )
```

```python
import functools

import jax
import jax.numpy as jnp
from jax import lax
from jax.experimental import pallas as pl
from jax.experimental.pallas import tpu as pltpu
from jax.sharding import PartitionSpec as P

D = 9216
HEADS = 24
HD = 256
EPSILON = 1e-05
MASKED = -1e30
MIB = 1024 * 1024
TILE = 256
SLOTS = 10
F32 = jnp.float32
BF16 = jnp.bfloat16


def whole(memory_space=pltpu.VMEM):
    return pl.BlockSpec(memory_space=memory_space)


def cost_of(*arrays):
    size = sum(a.size for a in arrays)
    return pl.CostEstimate(flops=size, bytes_accessed=size // 16, transcendentals=0)


def params():
    return pltpu.CompilerParams(vmem_limit_bytes=9 * MIB)


def stats_kernel(count, *refs):
    token_refs, (rows_ref, out_ref) = refs[:count], refs[-2:]
    tall, _, steps, features = token_refs[0].shape
    for index, ref in enumerate(token_refs):
        for t in range(tall):
            first = (index * tall + t) * steps
            rows_ref[first : first + steps] = ref[t, 0].astype(F32)
    floats = rows_ref[...]
    sums = jnp.sum(floats, axis=-1, keepdims=True)
    squares = jnp.sum(floats * floats, axis=-1, keepdims=True)
    lane = lax.broadcasted_iota(jnp.int32, out_ref.shape, 1)
    out_ref[...] = jnp.where(lane < 64, sums, squares)


def partial_stats(tokens, after):
    tall, _, steps, features = tokens[0].shape
    rows = len(tokens) * tall * steps
    return pl.pallas_call(
        functools.partial(stats_kernel, len(tokens)),
        out_shape=(pltpu.VMEM((rows, features), F32), pltpu.VMEM((rows, 128), F32)),
        in_specs=[whole()] * len(tokens) + [whole(pl.ANY)],
        out_specs=(whole(), whole()),
        compiler_params=params(),
        cost_estimate=cost_of(*tokens),
    )(*tokens, after)


def norm_kernel(source_ref, gain_ref, rows_ref, *refs):
    stat_refs, out_ref = refs[:-2], refs[-1]
    stats = stat_refs[0][...]
    for ref in stat_refs[1:]:
        stats = stats + ref[...]
    average = stats[:, 0:1] / D
    inverse_std = lax.rsqrt(stats[:, 64:65] / D - average * average + EPSILON)
    normed = ((rows_ref[...] - average) * inverse_std * gain_ref[...][None, :]).astype(BF16)
    rows = normed.shape[0]
    place = lax.broadcasted_iota(jnp.int32, (rows, rows), 1) == source_ref[...]
    out_ref[...] = jnp.dot(
        jnp.where(place, 1.0, 0.0).astype(BF16), normed, preferred_element_type=F32
    ).astype(BF16)


def normed_rows(source, gain, rows, stats, after):
    return pl.pallas_call(
        norm_kernel,
        out_shape=pltpu.VMEM(rows.shape, BF16),
        in_specs=[whole()] * (3 + len(stats)) + [whole(pl.ANY)],
        out_specs=whole(),
        compiler_params=params(),
        cost_estimate=cost_of(rows),
    )(source, gain, rows, *stats, after)


def combine_kernel(chips, small, skip, *refs):
    sent_ref, keep_ref = refs[:2]
    out_refs = refs[skip:]
    cols = keep_ref.shape[2]
    block = keep_ref.shape[1] // chips
    for index in range(chips):
        rows = slice(index * block, (index + 1) * block)
        total = keep_ref[:, rows] + sent_ref[:, rows, :cols].astype(F32)
        out_refs[index][:, :, :cols] = total.astype(out_refs[index].dtype)
        if small:
            sent = sent_ref[0, rows, cols:].astype(F32) + sent_ref[1, rows, cols:].astype(F32)
            total = refs[2][rows] + sent
            if index == chips - 1:
                out_refs[chips][...] = total
            else:
                store_split(out_refs[index], slice(cols, cols + small), total)


def combine(chips, sent, keep, keep_q=None, carry=None, after=()):
    small = 0 if keep_q is None else keep_q.shape[1]
    block = keep.shape[1] // chips
    out_shape = [pltpu.VMEM((2, block, sent.shape[2]), BF16)] * (chips - 1)
    out_shape.append(pltpu.VMEM((2, block, keep.shape[2]), F32))
    if small:
        out_shape.append(pltpu.VMEM((block, small), F32))
    args = (sent, keep, keep_q) if small else (sent, keep)
    extra = [*after] if carry is None else [*after, *in_vmem((carry,))]
    out_specs = [whole()] * len(out_shape)
    aliases = {}
    if carry is not None:
        aliases = {len(args) + len(after): len(out_shape)}
        out_shape.append(pltpu.VMEM(carry.shape, carry.dtype))
        out_specs.append(whole())
    return pl.pallas_call(
        functools.partial(combine_kernel, chips, small, len(args) + len(extra)),
        out_shape=out_shape,
        in_specs=[whole()] * len(args)
        + [whole(pl.ANY)] * len(after)
        + [whole()] * (len(extra) - len(after)),
        out_specs=out_specs,
        input_output_aliases=aliases,
        compiler_params=params(),
        cost_estimate=cost_of(*args),
    )(*args, *extra)


def query_rows_kernel(count, source_ref, *refs):
    term_refs, out_refs = refs[:-count], refs[-count:]
    total = term_refs[0][...]
    rows, cols = total.shape
    for ref in term_refs[1:]:
        first = ref.shape[2] - cols
        total = total + (ref[0, :, first:].astype(F32) + ref[1, :, first:].astype(F32))
    place = lax.broadcasted_iota(jnp.int32, (rows, rows), 1) == source_ref[...]
    turned = jnp.dot(
        jnp.where(place, 1.0, 0.0).astype(BF16), total.astype(BF16), preferred_element_type=F32
    )
    each = rows // count
    for index, ref in enumerate(out_refs):
        ref[0] = turned[index * each : (index + 1) * each].astype(BF16)


def query_rows(source, terms, count):
    rows, cols = terms[0].shape
    return pl.pallas_call(
        functools.partial(query_rows_kernel, count),
        out_shape=[pltpu.VMEM((1, rows // count, cols), BF16)] * count,
        in_specs=[whole()] * (1 + len(terms)),
        out_specs=[whole()] * count,
        compiler_params=params(),
        cost_estimate=cost_of(*terms),
    )(source, *terms)


def gated_kernel(counts, ready, *refs):
    out_ref = refs[-1]
    local, wide, steps, _ = out_ref.shape
    taken, first = ready, 0
    for ref in refs[:ready]:
        out_ref[:, :, :, : ref.shape[3]] = ref[...]
        first = ref.shape[3]
    for count in counts:
        total = refs[taken][...]
        cols = total.shape[2]
        for ref in refs[taken + 1 : taken + count]:
            total = total + ref[:, :, :cols].astype(F32)
        taken += count
        gate, up = total[0], total[1]
        hidden = gate / (1.0 + jnp.exp(-gate)) * up
        for row in range(local * wide):
            piece = hidden[row * steps : (row + 1) * steps].astype(BF16)
            out_ref[row // wide, row % wide, :, first : first + cols] = piece
        first += cols


def gated(chunks, out_shape, ready=(), after=()):
    terms = [term for chunk in chunks for term in chunk]
    return pl.pallas_call(
        functools.partial(gated_kernel, [len(chunk) for chunk in chunks], len(ready)),
        out_shape=out_shape,
        in_specs=[whole()] * (len(ready) + len(terms)) + [whole(pl.ANY)] * len(after),
        out_specs=whole(),
        compiler_params=params(),
        cost_estimate=cost_of(*ready, *terms),
    )(*ready, *terms, *after)


def in_hbm(arrays):
    return [pltpu.with_memory_space_constraint(a, pltpu.HBM) for a in arrays]


def in_vmem(arrays):
    return [pltpu.with_memory_space_constraint(a, pltpu.VMEM) for a in arrays]


def tile_copies(w_refs, tile, ring, sems):
    columns = pl.ds(pl.multiple_of(tile * TILE, TILE), TILE)
    slot = lax.rem(tile, SLOTS)
    return [
        pltpu.make_async_copy(
            ref.at[:, columns], ring.at[slot, :, index * TILE : (index + 1) * TILE], sems.at[slot, index]
        )
        for index, ref in enumerate(w_refs)
    ]


def each_tile(first, last, action):
    def body(tile, carry):
        action(tile)
        return carry

    lax.fori_loop(first, last, body, 0)


def ring_shape(features):
    return pltpu.VMEM((SLOTS, features, 2 * TILE), BF16)


def load_kernel(first, last, wg_ref, wu_ref, *refs):
    ring, sems = refs[-2:]

    def start(tile):
        for copy in tile_copies((wg_ref, wu_ref), tile, ring, sems):
            copy.start()

    def wait(tile):
        for copy in tile_copies((wg_ref, wu_ref), tile, ring, sems):
            copy.wait()

    each_tile(first, last, start)
    each_tile(first, last, wait)


def load(weights, first, last, ring, after):
    features = weights[0].shape[0]
    rings = [] if ring is None else in_vmem((ring,))
    return pl.pallas_call(
        functools.partial(load_kernel, first, last),
        out_shape=ring_shape(features),
        in_specs=[whole(pltpu.HBM)] * 2 + [whole()] * len(rings) + [whole(pl.ANY)] * len(after),
        out_specs=whole(),
        scratch_shapes=[pltpu.SemaphoreType.DMA((SLOTS, 2))],
        input_output_aliases={2: 0} if rings else {},
        compiler_params=params(),
        cost_estimate=pl.CostEstimate(
            flops=0, bytes_accessed=4 * features * TILE * (last - first), transcendentals=0
        ),
    )(*in_hbm(weights), *rings, *after)


def store_split(ref, columns, value):
    high = value.astype(BF16)
    ref[0, :, columns] = high
    ref[1, :, columns] = (value - high.astype(F32)).astype(BF16)


def multiply_tiles(first, tiles, held, following, x_ref, w_refs, ring, sems, send_ref, keep_ref):
    loads = tiles + following - held
    early = min(6, SLOTS - held, loads)

    def start(index):
        for copy in tile_copies(w_refs, first + held + index, ring, sems):
            copy.start()

    def wait(index):
        for copy in tile_copies(w_refs, first + held + index, ring, sems):
            copy.wait()

    def multiply(index):
        if held < tiles:

            @pl.when(index >= held)
            def _():
                wait(index - held)

        place = ring.at[lax.rem(first + index, SLOTS)]
        part = jnp.dot(x_ref[...], place[...], preferred_element_type=F32)
        half = part.shape[0] // 2
        columns = pl.ds(pl.multiple_of(index * TILE, TILE), TILE)
        for which in range(2):
            lanes = slice(which * TILE, (which + 1) * TILE)
            send_ref[which, :, columns] = part[:half, lanes].astype(BF16)
            keep_ref[which, :, columns] = part[half:, lanes]
        if early < loads:

            @pl.when(index + early < loads)
            def _():
                start(index + early)

    each_tile(0, early, start)
    each_tile(0, tiles, multiply)
    return lambda: each_tile(tiles - held, loads, wait)


def first_kernel(tiles, following, x_ref, wg_ref, wu_ref, wq_ref, wkv_ref, _, *refs):
    send_ref, keep_ref, keep_q_ref, ring, q_ref, kv_ref, small_sems, sems = refs
    half = x_ref.shape[0] // 2
    smalls = [
        pltpu.make_async_copy(wq_ref, q_ref, small_sems.at[0]),
        pltpu.make_async_copy(wkv_ref, kv_ref, small_sems.at[1]),
    ]
    for copy in smalls:
        copy.start()
    finish = multiply_tiles(0, tiles, tiles, following, x_ref, (wg_ref, wu_ref), ring, sems, send_ref, keep_ref)
    for copy in smalls:
        copy.wait()
    q_cols, kv_cols, base = q_ref.shape[1], kv_ref.shape[1], tiles * TILE
    piece = q_cols // 3

    def queries(index):
        columns = pl.ds(pl.multiple_of(index * piece, piece), piece)
        part = jnp.dot(x_ref[...], q_ref[:, columns], preferred_element_type=F32)
        sent = pl.ds(pl.multiple_of(base + index * piece, TILE), piece)
        store_split(send_ref, sent, part[:half])
        keep_q_ref[:, columns] = part[half:]

    each_tile(0, 3, queries)
    part = jnp.dot(x_ref[...], kv_ref[...], preferred_element_type=F32)
    store_split(send_ref, slice(base + q_cols, base + q_cols + kv_cols), part[:half])
    keep_q_ref[:, q_cols:] = part[half:]
    finish()


def first_sums(x, weights, w_query, w_keyval, ring, tiles, following):
    rows, features = x.shape
    cols, small = tiles * TILE, w_query.shape[1] + w_keyval.shape[1]
    return pl.pallas_call(
        functools.partial(first_kernel, tiles, following),
        out_shape=[
            pltpu.VMEM((2, rows // 2, cols + small), BF16),
            pltpu.VMEM((2, rows // 2, cols), F32),
            pltpu.VMEM((rows // 2, small), F32),
            ring_shape(features),
        ],
        in_specs=[whole()] + [whole(pltpu.HBM)] * 4 + [whole()],
        out_specs=[whole()] * 4,
        scratch_shapes=[
            pltpu.VMEM(w_query.shape, BF16),
            pltpu.VMEM(w_keyval.shape, BF16),
            pltpu.SemaphoreType.DMA((2,)),
            pltpu.SemaphoreType.DMA((SLOTS, 2)),
        ],
        input_output_aliases={5: 3},
        compiler_params=params(),
        cost_estimate=pl.CostEstimate(
            flops=2 * rows * features * (2 * cols + small),
            bytes_accessed=4 * features * cols,
            transcendentals=0,
        ),
    )(x, *in_hbm((*weights, w_query, w_keyval)), *in_vmem((ring,)))


def wide_kernel(first, tiles, held, following, x_ref, wg_ref, wu_ref, _, *refs):
    send_ref, keep_ref, ring, sems = refs[-4:]
    multiply_tiles(
        first, tiles, held, following, x_ref, (wg_ref, wu_ref), ring, sems, send_ref, keep_ref
    )()


def wide_sums(x, weights, ring, first, tiles, held, following, after):
    rows, features = x.shape
    cols = tiles * TILE
    return pl.pallas_call(
        functools.partial(wide_kernel, first, tiles, held, following),
        out_shape=[
            pltpu.VMEM((2, rows // 2, cols), BF16),
            pltpu.VMEM((2, rows // 2, cols), F32),
            ring_shape(features),
        ],
        in_specs=[whole(), whole(pltpu.HBM), whole(pltpu.HBM), whole()]
        + [whole(pl.ANY)] * len(after),
        out_specs=[whole()] * 3,
        scratch_shapes=[pltpu.SemaphoreType.DMA((SLOTS, 2))],
        input_output_aliases={3: 2},
        compiler_params=params(),
        cost_estimate=pl.CostEstimate(
            flops=4 * rows * features * cols,
            bytes_accessed=4 * features * TILE * (tiles + following - held),
            transcendentals=0,
        ),
    )(x, *in_hbm(weights), *in_vmem((ring,)), *after)


def merge_kernel(kept_ref, came_ref, keep_ref, send_ref):
    half = keep_ref.shape[1]
    count = kept_ref.shape[0]
    for index in range(2 * count):
        both = (kept_ref[index] if index < count else came_ref[index - count]).astype(F32)
        keep_ref[index] = both[:half].astype(BF16)
        send_ref[index] = both[half:].astype(BF16)


def merge(kept, came):
    count, rows, cols = kept.shape
    out = pltpu.VMEM((2 * count, rows // 2, cols), BF16)
    return pl.pallas_call(
        merge_kernel,
        out_shape=(out, out),
        in_specs=[whole()] * 2,
        out_specs=(whole(), whole()),
        compiler_params=params(),
        cost_estimate=cost_of(kept, came),
    )(kept, came)


def attend_kernel(count, steps, query_cols, slot_ref, lengths_ref, cache_ref, *refs):
    part_refs, (out_ref, held, fresh) = refs[:count], refs[-3:]
    each = part_refs[0].shape[0]
    for index, ref in enumerate(part_refs):
        for source in range(each):
            held[slot_ref[index * each + source]] = ref[source].astype(F32)
    count = count * each
    pair_cols = held.shape[2] - query_cols
    heads = query_cols // HD
    scale = HD ** (-0.5)
    batch, positions = cache_ref.shape[0], cache_ref.shape[1]
    fresh[...] = jnp.zeros_like(fresh)
    for b in range(batch):
        rows = pl.ds(b * steps, steps)
        for c in range(count):
            fresh[b, :steps, c * pair_cols : (c + 1) * pair_cols] = held[c, rows, query_cols:]
        queries = jnp.concatenate(
            [held[c, rows, h * HD : (h + 1) * HD] for c in range(count) for h in range(heads)],
            axis=0,
        ).astype(BF16)
        pairs = fresh[b].astype(BF16)
        dims = (((1,), (1,)), ((), ()))
        old = lax.dot_general(
            queries, cache_ref[b, :, :HD], dims, preferred_element_type=F32
        ) * scale
        position = lax.broadcasted_iota(jnp.int32, old.shape, 1)
        old = jnp.where(position < lengths_ref[b], old, MASKED)
        new = lax.dot_general(queries, pairs[:, :HD], dims, preferred_element_type=F32) * scale
        step = lax.broadcasted_iota(jnp.int32, new.shape, 0) % steps
        new = jnp.where(lax.broadcasted_iota(jnp.int32, new.shape, 1) <= step, new, MASKED)
        highest = jnp.maximum(
            jnp.max(old, axis=-1, keepdims=True), jnp.max(new, axis=-1, keepdims=True)
        )
        old = jnp.exp(old - highest)
        new = jnp.exp(new - highest)
        total = jnp.sum(old, axis=-1, keepdims=True) + jnp.sum(new, axis=-1, keepdims=True)
        context = jnp.dot(
            (old / total).astype(BF16), cache_ref[b, :, HD:], preferred_element_type=F32
        ) + jnp.dot((new / total).astype(BF16), pairs[:, HD:], preferred_element_type=F32)
        for h in range(HEADS):
            piece = context[h * steps : (h + 1) * steps].astype(BF16)
            out_ref[b, 0, :, h * HD : (h + 1) * HD] = piece


def attend(slots, lengths, cache, parts, steps, query_cols, after):
    batch = cache.shape[0]
    count = len(parts)
    sources, rows, cols = parts[0].shape
    return pl.pallas_call(
        functools.partial(attend_kernel, count, steps, query_cols),
        out_shape=jax.ShapeDtypeStruct((batch, 1, steps, HEADS * HD), BF16),
        in_specs=[whole(pltpu.SMEM), whole(pltpu.SMEM)] + [whole()] * (1 + count) + [whole(pl.ANY)] * len(after),
        out_specs=whole(),
        scratch_shapes=[
            pltpu.VMEM((count * sources, rows, cols), F32),
            pltpu.VMEM((batch, 8, 2 * HD), F32),
        ],
        compiler_params=params(),
        cost_estimate=pl.CostEstimate(
            flops=4 * batch * steps * HEADS * HD * cache.shape[1],
            bytes_accessed=2 * cache.size,
            transcendentals=batch * steps * HEADS * cache.shape[1],
        ),
    )(slots, lengths, cache, *parts, *after)


def on_device(tokens, gain, w_query, w_keyval, w_gate, w_up, cache, lengths):
    size_x, size_y = lax.axis_size("gx"), lax.axis_size("gy")
    chips = size_y // 2
    me_x, me_y = lax.axis_index("gx"), lax.axis_index("gy")
    tall, _, steps, features = tokens.shape
    local = cache.shape[0]
    block = local * size_x * steps

    def shift_x(value, by):
        return lax.ppermute(value, "gx", [(i, (i + by) % size_x) for i in range(size_x)])

    def shift_y(value, by):
        return lax.ppermute(value, "gy", [(i, (i + by) % size_y) for i in range(size_y)])

    def swap_x(value, bit):
        return lax.ppermute(value, "gx", [(i, i ^ bit) for i in range(size_x)])

    def swap(value):
        return lax.ppermute(value, "gy", [(i, i ^ 1) for i in range(size_y)])

    row = jnp.arange(2 * chips * block, dtype=jnp.int32)
    core = jnp.where(row < chips * block, 1 - me_y % 2, me_y % 2)
    chip = (me_y // 2 + 1 + row // block % chips) % chips
    sequence = (chip * 2 + core) * local + row % block // (size_x * steps)
    column = row // steps % size_x
    source = (me_x - column) % size_x * (tall * steps) + sequence * steps + row % steps
    source = source[:, None]
    row = jnp.arange(block, dtype=jnp.int32)
    to = me_x ^ (row // (local * steps))
    order = row // steps % local * (size_x * steps) + to * steps + row % steps
    order = order[:, None]
    bits, offsets = [], [0]
    while len(offsets) < size_x:
        bits.append(size_x // (2 * len(offsets)))
        offsets = offsets + [offset ^ bits[-1] for offset in offsets]
    slots = jnp.array(offsets, jnp.int32) ^ me_x

    weights = (w_gate, w_up)
    tiles = w_gate.shape[1] // TILE
    before = [tiles * share // 36 for share in (4, 9)]
    bounds = [0, before[1]] + [tiles * share // 36 for share in (20, 29, 36)]
    ahead = [before[1]] + [max(1, tiles * share // 36) for share in (5, 4, 4)] + [0]
    gathered = [tokens] + [shift_x(tokens, by) for by in range(1, size_x)]
    ring = load(weights, 0, before[0], None, (source, order, slots))
    rows, stats = partial_stats(gathered, ring)
    every_stat = [stats] + [shift_y(stats, by) for by in range(1, size_y)]
    ring = load(weights, before[0], before[1], ring, (stats,))
    x = normed_rows(source, gain, rows, every_stat, ring)

    def chunk_sums(chunk, ring, after):
        first, count = bounds[chunk], bounds[chunk + 1] - bounds[chunk]
        return wide_sums(x, weights, ring, first, count, ahead[chunk], ahead[chunk + 1], after)

    def to_chips(parts):
        return [shift_y(part, 2 * by) for by, part in enumerate(parts[: chips - 1], 1)]

    send_0, keep_0, keep_q, ring = first_sums(
        x, weights, w_query, w_keyval, ring, bounds[1], ahead[1]
    )
    send_1, keep_1, ring = chunk_sums(1, ring, (send_0,))
    parts_0 = combine(chips, swap(send_0), keep_0, keep_q)
    from_0 = to_chips(parts_0)

    send_2, keep_2, ring = chunk_sums(2, ring, (parts_0[0], send_1))
    parts_1 = combine(chips, swap(send_1), keep_1)
    from_1 = to_chips(parts_1)
    kept, leaving = query_rows(order, [parts_0[-1]] + from_0, 2)
    came = swap_x(leaving, bits[0])

    send_3, keep_3, _ = chunk_sums(3, ring, (parts_1[0], kept, send_2))
    *parts_2, send_3 = combine(chips, swap(send_2), keep_2, None, send_3, (came, from_1[0]))
    from_2 = to_chips(parts_2)
    for bit in bits[1:]:
        kept, leaving = merge(kept, came)
        came = swap_x(leaving, bit)
    parts_3 = combine(chips, swap(send_3), keep_3)
    from_3 = to_chips(parts_3)
    half_done = gated(
        [[parts_0[chips - 1]] + from_0, [parts_1[-1]] + from_1],
        pltpu.VMEM((local, size_x, steps, bounds[2] * TILE), BF16),
        (),
        (parts_3[0],),
    )
    context = attend(
        slots,
        lengths.reshape(local),
        cache.reshape(local, cache.shape[2], cache.shape[3]),
        (kept, came),
        steps,
        w_query.shape[1],
        (parts_3[0],),
    )
    hidden = gated(
        [[parts_2[-1]] + from_2, [parts_3[-1]] + from_3],
        jax.ShapeDtypeStruct((local, size_x, steps, w_gate.shape[1]), BF16),
        (half_done,),
    )
    return (context, hidden)


def solution(mesh):
    return jax.shard_map(
        on_device,
        mesh=mesh,
        in_specs=(
            P("groups", "gx", None, "gy"),
            P("gy"),
            P("gy", "gx"),
            P("gy", "gx"),
            P("gy", "gx"),
            P("gy", "gx"),
            P(("groups", "gy"), "gx", None, None),
            P(("groups", "gy"), "gx"),
        ),
        out_specs=(P(("groups", "gy"), "gx", None, None), P(("groups", "gy"), None, None, "gx")),
        check_vma=False,
    )
```

```python
import functools

import jax
import jax.numpy as jnp
from jax import lax
from jax.experimental import pallas as pl
from jax.experimental.pallas import tpu as pltpu
from jax.sharding import PartitionSpec as P

D = 9216
HEADS = 24
HD = 256
EPSILON = 1e-05
MASKED = -1e30
MIB = 1024 * 1024
TILE = 256
SLOTS = 10
F32 = jnp.float32
BF16 = jnp.bfloat16


def whole(memory_space=pltpu.VMEM):
    return pl.BlockSpec(memory_space=memory_space)


def cost_of(*arrays):
    size = sum(a.size for a in arrays)
    return pl.CostEstimate(flops=size, bytes_accessed=size // 16, transcendentals=0)


def params():
    return pltpu.CompilerParams(vmem_limit_bytes=9 * MIB)


def stats_kernel(count, *refs):
    token_refs, (rows_ref, out_ref) = refs[:count], refs[-2:]
    tall, _, steps, features = token_refs[0].shape
    for index, ref in enumerate(token_refs):
        for t in range(tall):
            first = (index * tall + t) * steps
            rows_ref[first : first + steps] = ref[t, 0].astype(F32)
    floats = rows_ref[...]
    sums = jnp.sum(floats, axis=-1, keepdims=True)
    squares = jnp.sum(floats * floats, axis=-1, keepdims=True)
    lane = lax.broadcasted_iota(jnp.int32, out_ref.shape, 1)
    out_ref[...] = jnp.where(lane < 64, sums, squares)


def partial_stats(tokens, after):
    tall, _, steps, features = tokens[0].shape
    rows = len(tokens) * tall * steps
    return pl.pallas_call(
        functools.partial(stats_kernel, len(tokens)),
        out_shape=(pltpu.VMEM((rows, features), F32), pltpu.VMEM((rows, 128), F32)),
        in_specs=[whole()] * len(tokens) + [whole(pl.ANY)],
        out_specs=(whole(), whole()),
        compiler_params=params(),
        cost_estimate=cost_of(*tokens),
    )(*tokens, after)


def norm_kernel(source_ref, gain_ref, rows_ref, *refs):
    stat_refs, out_ref = refs[:-2], refs[-1]
    stats = stat_refs[0][...]
    for ref in stat_refs[1:]:
        stats = stats + ref[...]
    average = stats[:, 0:1] / D
    inverse_std = lax.rsqrt(stats[:, 64:65] / D - average * average + EPSILON)
    normed = ((rows_ref[...] - average) * inverse_std * gain_ref[...][None, :]).astype(BF16)
    rows = normed.shape[0]
    place = lax.broadcasted_iota(jnp.int32, (rows, rows), 1) == source_ref[...]
    out_ref[...] = jnp.dot(
        jnp.where(place, 1.0, 0.0).astype(BF16), normed, preferred_element_type=F32
    ).astype(BF16)


def normed_rows(source, gain, rows, stats, after):
    return pl.pallas_call(
        norm_kernel,
        out_shape=pltpu.VMEM(rows.shape, BF16),
        in_specs=[whole()] * (3 + len(stats)) + [whole(pl.ANY)],
        out_specs=whole(),
        compiler_params=params(),
        cost_estimate=cost_of(rows),
    )(source, gain, rows, *stats, after)


def combine_kernel(chips, small, skip, *refs):
    sent_ref, keep_ref = refs[:2]
    out_refs = refs[skip:]
    cols = keep_ref.shape[2]
    block = keep_ref.shape[1] // chips
    for index in range(chips):
        rows = slice(index * block, (index + 1) * block)
        total = keep_ref[:, rows] + sent_ref[:, rows, :cols].astype(F32)
        out_refs[index][:, :, :cols] = total.astype(out_refs[index].dtype)
        if small:
            sent = sent_ref[0, rows, cols:].astype(F32) + sent_ref[1, rows, cols:].astype(F32)
            total = refs[2][rows] + sent
            if index == chips - 1:
                out_refs[chips][...] = total
            else:
                store_split(out_refs[index], slice(cols, cols + small), total)


def combine(chips, sent, keep, keep_q=None, carry=None, after=()):
    small = 0 if keep_q is None else keep_q.shape[1]
    block = keep.shape[1] // chips
    out_shape = [pltpu.VMEM((2, block, sent.shape[2]), BF16)] * (chips - 1)
    out_shape.append(pltpu.VMEM((2, block, keep.shape[2]), F32))
    if small:
        out_shape.append(pltpu.VMEM((block, small), F32))
    args = (sent, keep, keep_q) if small else (sent, keep)
    extra = [*after] if carry is None else [*after, *in_vmem((carry,))]
    out_specs = [whole()] * len(out_shape)
    aliases = {}
    if carry is not None:
        aliases = {len(args) + len(after): len(out_shape)}
        out_shape.append(pltpu.VMEM(carry.shape, carry.dtype))
        out_specs.append(whole())
    return pl.pallas_call(
        functools.partial(combine_kernel, chips, small, len(args) + len(extra)),
        out_shape=out_shape,
        in_specs=[whole()] * len(args)
        + [whole(pl.ANY)] * len(after)
        + [whole()] * (len(extra) - len(after)),
        out_specs=out_specs,
        input_output_aliases=aliases,
        compiler_params=params(),
        cost_estimate=cost_of(*args),
    )(*args, *extra)


def query_rows_kernel(count, source_ref, *refs):
    term_refs, out_refs = refs[:-count], refs[-count:]
    total = term_refs[0][...]
    rows, cols = total.shape
    for ref in term_refs[1:]:
        first = ref.shape[2] - cols
        total = total + (ref[0, :, first:].astype(F32) + ref[1, :, first:].astype(F32))
    place = lax.broadcasted_iota(jnp.int32, (rows, rows), 1) == source_ref[...]
    turned = jnp.dot(
        jnp.where(place, 1.0, 0.0).astype(BF16), total.astype(BF16), preferred_element_type=F32
    )
    each = rows // count
    for index, ref in enumerate(out_refs):
        ref[0] = turned[index * each : (index + 1) * each].astype(BF16)


def query_rows(source, terms, count):
    rows, cols = terms[0].shape
    return pl.pallas_call(
        functools.partial(query_rows_kernel, count),
        out_shape=[pltpu.VMEM((1, rows // count, cols), BF16)] * count,
        in_specs=[whole()] * (1 + len(terms)),
        out_specs=[whole()] * count,
        compiler_params=params(),
        cost_estimate=cost_of(*terms),
    )(source, *terms)


def gated_kernel(counts, ready, *refs):
    out_ref = refs[-1]
    local, wide, steps, _ = out_ref.shape
    taken, first = ready, 0
    for ref in refs[:ready]:
        out_ref[:, :, :, : ref.shape[3]] = ref[...]
        first = ref.shape[3]
    for count in counts:
        total = refs[taken][...]
        cols = total.shape[2]
        for ref in refs[taken + 1 : taken + count]:
            total = total + ref[:, :, :cols].astype(F32)
        taken += count
        gate, up = total[0], total[1]
        hidden = gate / (1.0 + jnp.exp(-gate)) * up
        for row in range(local * wide):
            piece = hidden[row * steps : (row + 1) * steps].astype(BF16)
            out_ref[row // wide, row % wide, :, first : first + cols] = piece
        first += cols


def gated(chunks, out_shape, ready=(), after=()):
    terms = [term for chunk in chunks for term in chunk]
    return pl.pallas_call(
        functools.partial(gated_kernel, [len(chunk) for chunk in chunks], len(ready)),
        out_shape=out_shape,
        in_specs=[whole()] * (len(ready) + len(terms)) + [whole(pl.ANY)] * len(after),
        out_specs=whole(),
        compiler_params=params(),
        cost_estimate=cost_of(*ready, *terms),
    )(*ready, *terms, *after)


def in_hbm(arrays):
    return [pltpu.with_memory_space_constraint(a, pltpu.HBM) for a in arrays]


def in_vmem(arrays):
    return [pltpu.with_memory_space_constraint(a, pltpu.VMEM) for a in arrays]


def tile_copies(w_refs, tile, ring, sems):
    columns = pl.ds(pl.multiple_of(tile * TILE, TILE), TILE)
    slot = lax.rem(tile, SLOTS)
    return [
        pltpu.make_async_copy(
            ref.at[:, columns], ring.at[slot, :, index * TILE : (index + 1) * TILE], sems.at[slot, index]
        )
        for index, ref in enumerate(w_refs)
    ]


def each_tile(first, last, action):
    def body(tile, carry):
        action(tile)
        return carry

    lax.fori_loop(first, last, body, 0)


def ring_shape(features):
    return pltpu.VMEM((SLOTS, features, 2 * TILE), BF16)


def load_kernel(first, last, wg_ref, wu_ref, *refs):
    ring, sems = refs[-2:]

    def start(tile):
        for copy in tile_copies((wg_ref, wu_ref), tile, ring, sems):
            copy.start()

    def wait(tile):
        for copy in tile_copies((wg_ref, wu_ref), tile, ring, sems):
            copy.wait()

    each_tile(first, last, start)
    each_tile(first, last, wait)


def load(weights, first, last, ring, after):
    features = weights[0].shape[0]
    rings = [] if ring is None else in_vmem((ring,))
    return pl.pallas_call(
        functools.partial(load_kernel, first, last),
        out_shape=ring_shape(features),
        in_specs=[whole(pltpu.HBM)] * 2 + [whole()] * len(rings) + [whole(pl.ANY)] * len(after),
        out_specs=whole(),
        scratch_shapes=[pltpu.SemaphoreType.DMA((SLOTS, 2))],
        input_output_aliases={2: 0} if rings else {},
        compiler_params=params(),
        cost_estimate=pl.CostEstimate(
            flops=0, bytes_accessed=4 * features * TILE * (last - first), transcendentals=0
        ),
    )(*in_hbm(weights), *rings, *after)


def store_split(ref, columns, value):
    high = value.astype(BF16)
    ref[0, :, columns] = high
    ref[1, :, columns] = (value - high.astype(F32)).astype(BF16)


def multiply_tiles(first, tiles, held, following, x_ref, w_refs, ring, sems, send_ref, keep_ref):
    loads = tiles + following - held
    early = min(6, SLOTS - held, loads)

    def start(index):
        for copy in tile_copies(w_refs, first + held + index, ring, sems):
            copy.start()

    def wait(index):
        for copy in tile_copies(w_refs, first + held + index, ring, sems):
            copy.wait()

    def multiply(index):
        if held < tiles:

            @pl.when(index >= held)
            def _():
                wait(index - held)

        place = ring.at[lax.rem(first + index, SLOTS)]
        part = jnp.dot(x_ref[...], place[...], preferred_element_type=F32)
        half = part.shape[0] // 2
        columns = pl.ds(pl.multiple_of(index * TILE, TILE), TILE)
        for which in range(2):
            lanes = slice(which * TILE, (which + 1) * TILE)
            send_ref[which, :, columns] = part[:half, lanes].astype(BF16)
            keep_ref[which, :, columns] = part[half:, lanes]
        if early < loads:

            @pl.when(index + early < loads)
            def _():
                start(index + early)

    each_tile(0, early, start)
    each_tile(0, tiles, multiply)
    return lambda: each_tile(tiles - held, loads, wait)


def first_kernel(tiles, following, x_ref, wg_ref, wu_ref, wq_ref, wkv_ref, _, *refs):
    send_ref, keep_ref, keep_q_ref, ring, q_ref, kv_ref, small_sems, sems = refs
    half = x_ref.shape[0] // 2
    smalls = [
        pltpu.make_async_copy(wq_ref, q_ref, small_sems.at[0]),
        pltpu.make_async_copy(wkv_ref, kv_ref, small_sems.at[1]),
    ]
    for copy in smalls:
        copy.start()
    finish = multiply_tiles(0, tiles, tiles, following, x_ref, (wg_ref, wu_ref), ring, sems, send_ref, keep_ref)
    for copy in smalls:
        copy.wait()
    q_cols, kv_cols, base = q_ref.shape[1], kv_ref.shape[1], tiles * TILE
    piece = q_cols // 3

    def queries(index):
        columns = pl.ds(pl.multiple_of(index * piece, piece), piece)
        part = jnp.dot(x_ref[...], q_ref[:, columns], preferred_element_type=F32)
        sent = pl.ds(pl.multiple_of(base + index * piece, TILE), piece)
        store_split(send_ref, sent, part[:half])
        keep_q_ref[:, columns] = part[half:]

    each_tile(0, 3, queries)
    part = jnp.dot(x_ref[...], kv_ref[...], preferred_element_type=F32)
    store_split(send_ref, slice(base + q_cols, base + q_cols + kv_cols), part[:half])
    keep_q_ref[:, q_cols:] = part[half:]
    finish()


def first_sums(x, weights, w_query, w_keyval, ring, tiles, following):
    rows, features = x.shape
    cols, small = tiles * TILE, w_query.shape[1] + w_keyval.shape[1]
    return pl.pallas_call(
        functools.partial(first_kernel, tiles, following),
        out_shape=[
            pltpu.VMEM((2, rows // 2, cols + small), BF16),
            pltpu.VMEM((2, rows // 2, cols), F32),
            pltpu.VMEM((rows // 2, small), F32),
            ring_shape(features),
        ],
        in_specs=[whole()] + [whole(pltpu.HBM)] * 4 + [whole()],
        out_specs=[whole()] * 4,
        scratch_shapes=[
            pltpu.VMEM(w_query.shape, BF16),
            pltpu.VMEM(w_keyval.shape, BF16),
            pltpu.SemaphoreType.DMA((2,)),
            pltpu.SemaphoreType.DMA((SLOTS, 2)),
        ],
        input_output_aliases={5: 3},
        compiler_params=params(),
        cost_estimate=pl.CostEstimate(
            flops=2 * rows * features * (2 * cols + small),
            bytes_accessed=4 * features * cols,
            transcendentals=0,
        ),
    )(x, *in_hbm((*weights, w_query, w_keyval)), *in_vmem((ring,)))


def wide_kernel(first, tiles, held, following, x_ref, wg_ref, wu_ref, _, *refs):
    send_ref, keep_ref, ring, sems = refs[-4:]
    multiply_tiles(
        first, tiles, held, following, x_ref, (wg_ref, wu_ref), ring, sems, send_ref, keep_ref
    )()


def wide_sums(x, weights, ring, first, tiles, held, following, after):
    rows, features = x.shape
    cols = tiles * TILE
    return pl.pallas_call(
        functools.partial(wide_kernel, first, tiles, held, following),
        out_shape=[
            pltpu.VMEM((2, rows // 2, cols), BF16),
            pltpu.VMEM((2, rows // 2, cols), F32),
            ring_shape(features),
        ],
        in_specs=[whole(), whole(pltpu.HBM), whole(pltpu.HBM), whole()]
        + [whole(pl.ANY)] * len(after),
        out_specs=[whole()] * 3,
        scratch_shapes=[pltpu.SemaphoreType.DMA((SLOTS, 2))],
        input_output_aliases={3: 2},
        compiler_params=params(),
        cost_estimate=pl.CostEstimate(
            flops=4 * rows * features * cols,
            bytes_accessed=4 * features * TILE * (tiles + following - held),
            transcendentals=0,
        ),
    )(x, *in_hbm(weights), *in_vmem((ring,)), *after)


def merge_kernel(kept_ref, came_ref, keep_ref, send_ref):
    half = keep_ref.shape[1]
    count = kept_ref.shape[0]
    for index in range(2 * count):
        both = (kept_ref[index] if index < count else came_ref[index - count]).astype(F32)
        keep_ref[index] = both[:half].astype(BF16)
        send_ref[index] = both[half:].astype(BF16)


def merge(kept, came):
    count, rows, cols = kept.shape
    out = pltpu.VMEM((2 * count, rows // 2, cols), BF16)
    return pl.pallas_call(
        merge_kernel,
        out_shape=(out, out),
        in_specs=[whole()] * 2,
        out_specs=(whole(), whole()),
        compiler_params=params(),
        cost_estimate=cost_of(kept, came),
    )(kept, came)


def attend_kernel(count, steps, query_cols, slot_ref, lengths_ref, cache_ref, *refs):
    part_refs, (out_ref, held, fresh) = refs[:count], refs[-3:]
    each = part_refs[0].shape[0]
    for index, ref in enumerate(part_refs):
        for source in range(each):
            held[slot_ref[index * each + source]] = ref[source].astype(F32)
    count = count * each
    pair_cols = held.shape[2] - query_cols
    heads = query_cols // HD
    scale = HD ** (-0.5)
    batch, positions = cache_ref.shape[0], cache_ref.shape[1]
    fresh[...] = jnp.zeros_like(fresh)
    for b in range(batch):
        rows = pl.ds(b * steps, steps)
        for c in range(count):
            fresh[b, :steps, c * pair_cols : (c + 1) * pair_cols] = held[c, rows, query_cols:]
        queries = jnp.concatenate(
            [held[c, rows, h * HD : (h + 1) * HD] for c in range(count) for h in range(heads)],
            axis=0,
        ).astype(BF16)
        pairs = fresh[b].astype(BF16)
        dims = (((1,), (1,)), ((), ()))
        old = lax.dot_general(
            queries, cache_ref[b, :, :HD], dims, preferred_element_type=F32
        ) * scale
        position = lax.broadcasted_iota(jnp.int32, old.shape, 1)
        old = jnp.where(position < lengths_ref[b], old, MASKED)
        new = lax.dot_general(queries, pairs[:, :HD], dims, preferred_element_type=F32) * scale
        step = lax.broadcasted_iota(jnp.int32, new.shape, 0) % steps
        new = jnp.where(lax.broadcasted_iota(jnp.int32, new.shape, 1) <= step, new, MASKED)
        highest = jnp.maximum(
            jnp.max(old, axis=-1, keepdims=True), jnp.max(new, axis=-1, keepdims=True)
        )
        old = jnp.exp(old - highest)
        new = jnp.exp(new - highest)
        total = jnp.sum(old, axis=-1, keepdims=True) + jnp.sum(new, axis=-1, keepdims=True)
        context = jnp.dot(
            (old / total).astype(BF16), cache_ref[b, :, HD:], preferred_element_type=F32
        ) + jnp.dot((new / total).astype(BF16), pairs[:, HD:], preferred_element_type=F32)
        for h in range(HEADS):
            piece = context[h * steps : (h + 1) * steps].astype(BF16)
            out_ref[b, 0, :, h * HD : (h + 1) * HD] = piece


def attend(slots, lengths, cache, parts, steps, query_cols, after):
    batch = cache.shape[0]
    count = len(parts)
    sources, rows, cols = parts[0].shape
    return pl.pallas_call(
        functools.partial(attend_kernel, count, steps, query_cols),
        out_shape=jax.ShapeDtypeStruct((batch, 1, steps, HEADS * HD), BF16),
        in_specs=[whole(pltpu.SMEM), whole(pltpu.SMEM)] + [whole()] * (1 + count) + [whole(pl.ANY)] * len(after),
        out_specs=whole(),
        scratch_shapes=[
            pltpu.VMEM((count * sources, rows, cols), F32),
            pltpu.VMEM((batch, 8, 2 * HD), F32),
        ],
        compiler_params=params(),
        cost_estimate=pl.CostEstimate(
            flops=4 * batch * steps * HEADS * HD * cache.shape[1],
            bytes_accessed=2 * cache.size,
            transcendentals=batch * steps * HEADS * cache.shape[1],
        ),
    )(slots, lengths, cache, *parts, *after)


def on_device(tokens, gain, w_query, w_keyval, w_gate, w_up, cache, lengths):
    size_x, size_y = lax.axis_size("gx"), lax.axis_size("gy")
    chips = size_y // 2
    me_x, me_y = lax.axis_index("gx"), lax.axis_index("gy")
    tall, _, steps, features = tokens.shape
    local = cache.shape[0]
    block = local * size_x * steps

    def shift_y(value, by):
        return lax.ppermute(value, "gy", [(i, (i + by) % size_y) for i in range(size_y)])

    def swap_x(value, bits):
        return lax.ppermute(value, "gx", [(i, i ^ bits) for i in range(size_x)])

    def swap(value, bits=1):
        return lax.ppermute(value, "gy", [(i, i ^ bits) for i in range(size_y)])

    row = jnp.arange(2 * chips * block, dtype=jnp.int32)
    core = jnp.where(row < chips * block, 1 - me_y % 2, me_y % 2)
    chip = (me_y // 2 + 1 + row // block % chips) % chips
    sequence = (chip * 2 + core) * local + row % block // (size_x * steps)
    column = row // steps % size_x
    source = (me_x ^ column) * (tall * steps) + sequence * steps + row % steps
    source = source[:, None]
    row = jnp.arange(block, dtype=jnp.int32)
    to = me_x ^ (row // (local * steps))
    order = row // steps % local * (size_x * steps) + to * steps + row % steps
    order = order[:, None]
    bits, offsets = [], [0]
    while len(offsets) < size_x:
        bits.append(size_x // (2 * len(offsets)))
        offsets = offsets + [offset ^ bits[-1] for offset in offsets]
    number = jnp.arange(size_x, dtype=jnp.int32)
    slots = me_x ^ sum((number >> place & 1) * bit for place, bit in enumerate(bits))

    weights = (w_gate, w_up)
    tiles = w_gate.shape[1] // TILE
    before = [tiles * share // 36 for share in (4, 9)]
    bounds = [0, before[1]] + [tiles * share // 36 for share in (20, 29, 36)]
    ahead = [before[1]] + [max(1, tiles * share // 36) for share in (5, 4, 4)] + [0]
    gathered = [tokens] + [swap_x(tokens, bits) for bits in range(1, size_x)]
    ring = load(weights, 0, before[0], None, (source, order, slots))
    rows, stats = partial_stats(gathered, ring)
    every_stat = [stats] + [swap(stats, bits) for bits in range(1, size_y)]
    ring = load(weights, before[0], before[1], ring, (stats,))
    x = normed_rows(source, gain, rows, every_stat, ring)

    def chunk_sums(chunk, ring, after):
        first, count = bounds[chunk], bounds[chunk + 1] - bounds[chunk]
        return wide_sums(x, weights, ring, first, count, ahead[chunk], ahead[chunk + 1], after)

    def to_chips(parts):
        return [shift_y(part, 2 * by) for by, part in enumerate(parts[: chips - 1], 1)]

    send_0, keep_0, keep_q, ring = first_sums(
        x, weights, w_query, w_keyval, ring, bounds[1], ahead[1]
    )
    send_1, keep_1, ring = chunk_sums(1, ring, (send_0,))
    parts_0 = combine(chips, swap(send_0), keep_0, keep_q)
    from_0 = to_chips(parts_0)

    send_2, keep_2, ring = chunk_sums(2, ring, (parts_0[0], send_1))
    parts_1 = combine(chips, swap(send_1), keep_1)
    from_1 = to_chips(parts_1)
    kept, leaving = query_rows(order, [parts_0[-1]] + from_0, 2)
    came = swap_x(leaving, bits[0])

    send_3, keep_3, _ = chunk_sums(3, ring, (parts_1[0], kept, send_2))
    *parts_2, send_3 = combine(chips, swap(send_2), keep_2, None, send_3, (came, from_1[0]))
    from_2 = to_chips(parts_2)
    for bit in bits[1:]:
        kept, leaving = merge(kept, came)
        came = swap_x(leaving, bit)
    parts_3 = combine(chips, swap(send_3), keep_3)
    from_3 = to_chips(parts_3)
    half_done = gated(
        [[parts_0[chips - 1]] + from_0, [parts_1[-1]] + from_1],
        pltpu.VMEM((local, size_x, steps, bounds[2] * TILE), BF16),
        (),
        (parts_3[0],),
    )
    context = attend(
        slots,
        lengths.reshape(local),
        cache.reshape(local, cache.shape[2], cache.shape[3]),
        (kept, came),
        steps,
        w_query.shape[1],
        (parts_3[0],),
    )
    hidden = gated(
        [[parts_2[-1]] + from_2, [parts_3[-1]] + from_3],
        jax.ShapeDtypeStruct((local, size_x, steps, w_gate.shape[1]), BF16),
        (half_done,),
    )
    return (context, hidden)


def solution(mesh):
    return jax.shard_map(
        on_device,
        mesh=mesh,
        in_specs=(
            P("groups", "gx", None, "gy"),
            P("gy"),
            P("gy", "gx"),
            P("gy", "gx"),
            P("gy", "gx"),
            P("gy", "gx"),
            P(("groups", "gy"), "gx", None, None),
            P(("groups", "gy"), "gx"),
        ),
        out_specs=(P(("groups", "gy"), "gx", None, None), P(("groups", "gy"), None, None, "gx")),
        check_vma=False,
    )
```

```python
import functools

import jax
import jax.numpy as jnp
from jax import lax
from jax.experimental import pallas as pl
from jax.experimental.pallas import tpu as pltpu
from jax.sharding import PartitionSpec as P

D = 9216
HEADS = 24
HD = 256
EPSILON = 1e-05
MASKED = -1e30
MIB = 1024 * 1024
TILE = 256
SLOTS = 10
F32 = jnp.float32
BF16 = jnp.bfloat16


def whole(memory_space=pltpu.VMEM):
    return pl.BlockSpec(memory_space=memory_space)


def cost_of(*arrays):
    size = sum(a.size for a in arrays)
    return pl.CostEstimate(flops=size, bytes_accessed=size // 16, transcendentals=0)


def params():
    return pltpu.CompilerParams(vmem_limit_bytes=9 * MIB)


def stats_kernel(count, *refs):
    token_refs, (rows_ref, out_ref) = refs[:count], refs[-2:]
    tall, _, steps, features = token_refs[0].shape
    for index, ref in enumerate(token_refs):
        for t in range(tall):
            first = (index * tall + t) * steps
            rows_ref[first : first + steps] = ref[t, 0].astype(F32)
    floats = rows_ref[...]
    sums = jnp.sum(floats, axis=-1, keepdims=True)
    squares = jnp.sum(floats * floats, axis=-1, keepdims=True)
    lane = lax.broadcasted_iota(jnp.int32, out_ref.shape, 1)
    out_ref[...] = jnp.where(lane < 64, sums, squares)


def partial_stats(tokens, after):
    tall, _, steps, features = tokens[0].shape
    rows = len(tokens) * tall * steps
    return pl.pallas_call(
        functools.partial(stats_kernel, len(tokens)),
        out_shape=(pltpu.VMEM((rows, features), F32), pltpu.VMEM((rows, 128), F32)),
        in_specs=[whole()] * len(tokens) + [whole(pl.ANY)],
        out_specs=(whole(), whole()),
        compiler_params=params(),
        cost_estimate=cost_of(*tokens),
    )(*tokens, after)


def norm_kernel(source_ref, gain_ref, rows_ref, *refs):
    stat_refs, out_ref = refs[:-2], refs[-1]
    stats = stat_refs[0][...]
    for ref in stat_refs[1:]:
        stats = stats + ref[...]
    average = stats[:, 0:1] / D
    inverse_std = lax.rsqrt(stats[:, 64:65] / D - average * average + EPSILON)
    normed = ((rows_ref[...] - average) * inverse_std * gain_ref[...][None, :]).astype(BF16)
    rows = normed.shape[0]
    place = lax.broadcasted_iota(jnp.int32, (rows, rows), 1) == source_ref[...]
    out_ref[...] = jnp.dot(
        jnp.where(place, 1.0, 0.0).astype(BF16), normed, preferred_element_type=F32
    ).astype(BF16)


def normed_rows(source, gain, rows, stats, after):
    return pl.pallas_call(
        norm_kernel,
        out_shape=pltpu.VMEM(rows.shape, BF16),
        in_specs=[whole()] * (3 + len(stats)) + [whole(pl.ANY)],
        out_specs=whole(),
        compiler_params=params(),
        cost_estimate=cost_of(rows),
    )(source, gain, rows, *stats, after)


def combine_kernel(chips, small, skip, *refs):
    sent_ref, keep_ref = refs[:2]
    out_refs = refs[skip:]
    cols = keep_ref.shape[2]
    block = keep_ref.shape[1] // chips
    for index in range(chips):
        rows = slice(index * block, (index + 1) * block)
        total = keep_ref[:, rows] + sent_ref[:, rows, :cols].astype(F32)
        out_refs[index][:, :, :cols] = total.astype(out_refs[index].dtype)
        if small:
            sent = sent_ref[0, rows, cols:].astype(F32) + sent_ref[1, rows, cols:].astype(F32)
            total = refs[2][rows] + sent
            if index == chips - 1:
                out_refs[chips][...] = total
            else:
                store_split(out_refs[index], slice(cols, cols + small), total)


def combine(chips, sent, keep, keep_q=None, carry=None, after=()):
    small = 0 if keep_q is None else keep_q.shape[1]
    block = keep.shape[1] // chips
    out_shape = [pltpu.VMEM((2, block, sent.shape[2]), BF16)] * (chips - 1)
    out_shape.append(pltpu.VMEM((2, block, keep.shape[2]), F32))
    if small:
        out_shape.append(pltpu.VMEM((block, small), F32))
    args = (sent, keep, keep_q) if small else (sent, keep)
    extra = [*after] if carry is None else [*after, *in_vmem((carry,))]
    out_specs = [whole()] * len(out_shape)
    aliases = {}
    if carry is not None:
        aliases = {len(args) + len(after): len(out_shape)}
        out_shape.append(pltpu.VMEM(carry.shape, carry.dtype))
        out_specs.append(whole())
    return pl.pallas_call(
        functools.partial(combine_kernel, chips, small, len(args) + len(extra)),
        out_shape=out_shape,
        in_specs=[whole()] * len(args)
        + [whole(pl.ANY)] * len(after)
        + [whole()] * (len(extra) - len(after)),
        out_specs=out_specs,
        input_output_aliases=aliases,
        compiler_params=params(),
        cost_estimate=cost_of(*args),
    )(*args, *extra)


def query_rows_kernel(count, source_ref, *refs):
    term_refs, out_refs = refs[:-count], refs[-count:]
    total = term_refs[0][...]
    rows, cols = total.shape
    for ref in term_refs[1:]:
        first = ref.shape[2] - cols
        total = total + (ref[0, :, first:].astype(F32) + ref[1, :, first:].astype(F32))
    place = lax.broadcasted_iota(jnp.int32, (rows, rows), 1) == source_ref[...]
    turned = jnp.dot(
        jnp.where(place, 1.0, 0.0).astype(BF16), total.astype(BF16), preferred_element_type=F32
    )
    each = rows // count
    for index, ref in enumerate(out_refs):
        ref[...] = turned[index * each : (index + 1) * each].astype(BF16)


def query_rows(source, terms, count):
    rows, cols = terms[0].shape
    return pl.pallas_call(
        functools.partial(query_rows_kernel, count),
        out_shape=[pltpu.VMEM((rows // count, cols), BF16)] * count,
        in_specs=[whole()] * (1 + len(terms)),
        out_specs=[whole()] * count,
        compiler_params=params(),
        cost_estimate=cost_of(*terms),
    )(source, *terms)


def gated_kernel(counts, ready, *refs):
    out_ref = refs[-1]
    local, wide, steps, _ = out_ref.shape
    taken, first = ready, 0
    for ref in refs[:ready]:
        out_ref[:, :, :, : ref.shape[3]] = ref[...]
        first = ref.shape[3]
    for count in counts:
        total = refs[taken][...]
        cols = total.shape[2]
        for ref in refs[taken + 1 : taken + count]:
            total = total + ref[:, :, :cols].astype(F32)
        taken += count
        gate, up = total[0], total[1]
        hidden = gate / (1.0 + jnp.exp(-gate)) * up
        for row in range(local * wide):
            piece = hidden[row * steps : (row + 1) * steps].astype(BF16)
            out_ref[row // wide, row % wide, :, first : first + cols] = piece
        first += cols


def gated(chunks, out_shape, ready=(), after=()):
    terms = [term for chunk in chunks for term in chunk]
    return pl.pallas_call(
        functools.partial(gated_kernel, [len(chunk) for chunk in chunks], len(ready)),
        out_shape=out_shape,
        in_specs=[whole()] * (len(ready) + len(terms)) + [whole(pl.ANY)] * len(after),
        out_specs=whole(),
        compiler_params=params(),
        cost_estimate=cost_of(*ready, *terms),
    )(*ready, *terms, *after)


def in_hbm(arrays):
    return [pltpu.with_memory_space_constraint(a, pltpu.HBM) for a in arrays]


def in_vmem(arrays):
    return [pltpu.with_memory_space_constraint(a, pltpu.VMEM) for a in arrays]


def tile_copies(w_refs, tile, ring, sems):
    columns = pl.ds(pl.multiple_of(tile * TILE, TILE), TILE)
    slot = lax.rem(tile, SLOTS)
    return [
        pltpu.make_async_copy(
            ref.at[:, columns], ring.at[slot, :, index * TILE : (index + 1) * TILE], sems.at[slot, index]
        )
        for index, ref in enumerate(w_refs)
    ]


def each_tile(first, last, action):
    def body(tile, carry):
        action(tile)
        return carry

    lax.fori_loop(first, last, body, 0)


def ring_shape(features):
    return pltpu.VMEM((SLOTS, features, 2 * TILE), BF16)


def load_kernel(first, last, wg_ref, wu_ref, *refs):
    ring, sems = refs[-2:]

    def start(tile):
        for copy in tile_copies((wg_ref, wu_ref), tile, ring, sems):
            copy.start()

    def wait(tile):
        for copy in tile_copies((wg_ref, wu_ref), tile, ring, sems):
            copy.wait()

    each_tile(first, last, start)
    each_tile(first, last, wait)


def load(weights, first, last, ring, after):
    features = weights[0].shape[0]
    rings = [] if ring is None else in_vmem((ring,))
    return pl.pallas_call(
        functools.partial(load_kernel, first, last),
        out_shape=ring_shape(features),
        in_specs=[whole(pltpu.HBM)] * 2 + [whole()] * len(rings) + [whole(pl.ANY)] * len(after),
        out_specs=whole(),
        scratch_shapes=[pltpu.SemaphoreType.DMA((SLOTS, 2))],
        input_output_aliases={2: 0} if rings else {},
        compiler_params=params(),
        cost_estimate=pl.CostEstimate(
            flops=0, bytes_accessed=4 * features * TILE * (last - first), transcendentals=0
        ),
    )(*in_hbm(weights), *rings, *after)


def store_split(ref, columns, value):
    high = value.astype(BF16)
    ref[0, :, columns] = high
    ref[1, :, columns] = (value - high.astype(F32)).astype(BF16)


def multiply_tiles(first, tiles, held, following, x_ref, w_refs, ring, sems, send_ref, keep_ref):
    loads = tiles + following - held
    early = min(6, SLOTS - held, loads)

    def start(index):
        for copy in tile_copies(w_refs, first + held + index, ring, sems):
            copy.start()

    def wait(index):
        for copy in tile_copies(w_refs, first + held + index, ring, sems):
            copy.wait()

    def multiply(index):
        if held < tiles:

            @pl.when(index >= held)
            def _():
                wait(index - held)

        place = ring.at[lax.rem(first + index, SLOTS)]
        part = jnp.dot(x_ref[...], place[...], preferred_element_type=F32)
        half = part.shape[0] // 2
        columns = pl.ds(pl.multiple_of(index * TILE, TILE), TILE)
        for which in range(2):
            lanes = slice(which * TILE, (which + 1) * TILE)
            send_ref[which, :, columns] = part[:half, lanes].astype(BF16)
            keep_ref[which, :, columns] = part[half:, lanes]
        if early < loads:

            @pl.when(index + early < loads)
            def _():
                start(index + early)

    each_tile(0, early, start)
    each_tile(0, tiles, multiply)
    return lambda: each_tile(tiles - held, loads, wait)


def first_kernel(tiles, following, x_ref, wg_ref, wu_ref, wq_ref, wkv_ref, _, *refs):
    send_ref, keep_ref, keep_q_ref, ring, q_ref, kv_ref, small_sems, sems = refs
    half = x_ref.shape[0] // 2
    smalls = [
        pltpu.make_async_copy(wq_ref, q_ref, small_sems.at[0]),
        pltpu.make_async_copy(wkv_ref, kv_ref, small_sems.at[1]),
    ]
    for copy in smalls:
        copy.start()
    finish = multiply_tiles(0, tiles, tiles, following, x_ref, (wg_ref, wu_ref), ring, sems, send_ref, keep_ref)
    for copy in smalls:
        copy.wait()
    q_cols, kv_cols, base = q_ref.shape[1], kv_ref.shape[1], tiles * TILE
    piece = q_cols // 3

    def queries(index):
        columns = pl.ds(pl.multiple_of(index * piece, piece), piece)
        part = jnp.dot(x_ref[...], q_ref[:, columns], preferred_element_type=F32)
        sent = pl.ds(pl.multiple_of(base + index * piece, TILE), piece)
        store_split(send_ref, sent, part[:half])
        keep_q_ref[:, columns] = part[half:]

    each_tile(0, 3, queries)
    part = jnp.dot(x_ref[...], kv_ref[...], preferred_element_type=F32)
    store_split(send_ref, slice(base + q_cols, base + q_cols + kv_cols), part[:half])
    keep_q_ref[:, q_cols:] = part[half:]
    finish()


def first_sums(x, weights, w_query, w_keyval, ring, tiles, following):
    rows, features = x.shape
    cols, small = tiles * TILE, w_query.shape[1] + w_keyval.shape[1]
    return pl.pallas_call(
        functools.partial(first_kernel, tiles, following),
        out_shape=[
            pltpu.VMEM((2, rows // 2, cols + small), BF16),
            pltpu.VMEM((2, rows // 2, cols), F32),
            pltpu.VMEM((rows // 2, small), F32),
            ring_shape(features),
        ],
        in_specs=[whole()] + [whole(pltpu.HBM)] * 4 + [whole()],
        out_specs=[whole()] * 4,
        scratch_shapes=[
            pltpu.VMEM(w_query.shape, BF16),
            pltpu.VMEM(w_keyval.shape, BF16),
            pltpu.SemaphoreType.DMA((2,)),
            pltpu.SemaphoreType.DMA((SLOTS, 2)),
        ],
        input_output_aliases={5: 3},
        compiler_params=params(),
        cost_estimate=pl.CostEstimate(
            flops=2 * rows * features * (2 * cols + small),
            bytes_accessed=4 * features * cols,
            transcendentals=0,
        ),
    )(x, *in_hbm((*weights, w_query, w_keyval)), *in_vmem((ring,)))


def wide_kernel(first, tiles, held, following, x_ref, wg_ref, wu_ref, _, *refs):
    send_ref, keep_ref, ring, sems = refs[-4:]
    multiply_tiles(
        first, tiles, held, following, x_ref, (wg_ref, wu_ref), ring, sems, send_ref, keep_ref
    )()


def wide_sums(x, weights, ring, first, tiles, held, following, after):
    rows, features = x.shape
    cols = tiles * TILE
    return pl.pallas_call(
        functools.partial(wide_kernel, first, tiles, held, following),
        out_shape=[
            pltpu.VMEM((2, rows // 2, cols), BF16),
            pltpu.VMEM((2, rows // 2, cols), F32),
            ring_shape(features),
        ],
        in_specs=[whole(), whole(pltpu.HBM), whole(pltpu.HBM), whole()]
        + [whole(pl.ANY)] * len(after),
        out_specs=[whole()] * 3,
        scratch_shapes=[pltpu.SemaphoreType.DMA((SLOTS, 2))],
        input_output_aliases={3: 2},
        compiler_params=params(),
        cost_estimate=pl.CostEstimate(
            flops=4 * rows * features * cols,
            bytes_accessed=4 * features * TILE * (tiles + following - held),
            transcendentals=0,
        ),
    )(x, *in_hbm(weights), *in_vmem((ring,)), *after)


def attend_kernel(count, steps, query_cols, slot_ref, lengths_ref, cache_ref, *refs):
    part_refs, (out_ref, held, fresh) = refs[:count], refs[-3:]
    for index, ref in enumerate(part_refs):
        held[slot_ref[index]] = ref[...].astype(F32)
    pair_cols = held.shape[2] - query_cols
    heads = query_cols // HD
    scale = HD ** (-0.5)
    batch, positions = cache_ref.shape[0], cache_ref.shape[1]
    fresh[...] = jnp.zeros_like(fresh)
    for b in range(batch):
        rows = pl.ds(b * steps, steps)
        for c in range(count):
            fresh[b, :steps, c * pair_cols : (c + 1) * pair_cols] = held[c, rows, query_cols:]
        queries = jnp.concatenate(
            [held[c, rows, h * HD : (h + 1) * HD] for c in range(count) for h in range(heads)],
            axis=0,
        ).astype(BF16)
        pairs = fresh[b].astype(BF16)
        dims = (((1,), (1,)), ((), ()))
        old = lax.dot_general(
            queries, cache_ref[b, :, :HD], dims, preferred_element_type=F32
        ) * scale
        position = lax.broadcasted_iota(jnp.int32, old.shape, 1)
        old = jnp.where(position < lengths_ref[b], old, MASKED)
        new = lax.dot_general(queries, pairs[:, :HD], dims, preferred_element_type=F32) * scale
        step = lax.broadcasted_iota(jnp.int32, new.shape, 0) % steps
        new = jnp.where(lax.broadcasted_iota(jnp.int32, new.shape, 1) <= step, new, MASKED)
        highest = jnp.maximum(
            jnp.max(old, axis=-1, keepdims=True), jnp.max(new, axis=-1, keepdims=True)
        )
        old = jnp.exp(old - highest)
        new = jnp.exp(new - highest)
        total = jnp.sum(old, axis=-1, keepdims=True) + jnp.sum(new, axis=-1, keepdims=True)
        context = jnp.dot(
            (old / total).astype(BF16), cache_ref[b, :, HD:], preferred_element_type=F32
        ) + jnp.dot((new / total).astype(BF16), pairs[:, HD:], preferred_element_type=F32)
        for h in range(HEADS):
            piece = context[h * steps : (h + 1) * steps].astype(BF16)
            out_ref[b, 0, :, h * HD : (h + 1) * HD] = piece


def attend(slots, lengths, cache, parts, steps, query_cols, after):
    batch = cache.shape[0]
    count = len(parts)
    rows, cols = parts[0].shape
    return pl.pallas_call(
        functools.partial(attend_kernel, count, steps, query_cols),
        out_shape=jax.ShapeDtypeStruct((batch, 1, steps, HEADS * HD), BF16),
        in_specs=[whole(pltpu.SMEM), whole(pltpu.SMEM)] + [whole()] * (1 + count) + [whole(pl.ANY)] * len(after),
        out_specs=whole(),
        scratch_shapes=[
            pltpu.VMEM((count, rows, cols), F32),
            pltpu.VMEM((batch, 8, 2 * HD), F32),
        ],
        compiler_params=params(),
        cost_estimate=pl.CostEstimate(
            flops=4 * batch * steps * HEADS * HD * cache.shape[1],
            bytes_accessed=2 * cache.size,
            transcendentals=batch * steps * HEADS * cache.shape[1],
        ),
    )(slots, lengths, cache, *parts, *after)


def on_device(tokens, gain, w_query, w_keyval, w_gate, w_up, cache, lengths):
    size_x, size_y = lax.axis_size("gx"), lax.axis_size("gy")
    chips = size_y // 2
    me_x, me_y = lax.axis_index("gx"), lax.axis_index("gy")
    tall, _, steps, features = tokens.shape
    local = cache.shape[0]
    block = local * size_x * steps

    def shift_y(value, by):
        return lax.ppermute(value, "gy", [(i, (i + by) % size_y) for i in range(size_y)])

    def swap_x(value, bits):
        return lax.ppermute(value, "gx", [(i, i ^ bits) for i in range(size_x)])

    def swap(value, bits=1):
        return lax.ppermute(value, "gy", [(i, i ^ bits) for i in range(size_y)])

    row = jnp.arange(2 * chips * block, dtype=jnp.int32)
    core = jnp.where(row < chips * block, 1 - me_y % 2, me_y % 2)
    chip = (me_y // 2 + 1 + row // block % chips) % chips
    sequence = (chip * 2 + core) * local + row % block // (size_x * steps)
    column = row // steps % size_x
    source = (me_x ^ column) * (tall * steps) + sequence * steps + row % steps
    source = source[:, None]
    row = jnp.arange(block, dtype=jnp.int32)
    to = me_x ^ (row // (local * steps))
    order = row // steps % local * (size_x * steps) + to * steps + row % steps
    order = order[:, None]
    slots = me_x ^ jnp.arange(size_x, dtype=jnp.int32)

    weights = (w_gate, w_up)
    tiles = w_gate.shape[1] // TILE
    before = [tiles * share // 36 for share in (7, 9)]
    bounds = [0, before[1]] + [tiles * share // 36 for share in (20, 29, 36)]
    ahead = [before[1]] + [max(1, tiles * share // 36) for share in (5, 4, 4)] + [0]
    gathered = [tokens] + [swap_x(tokens, bits) for bits in range(1, size_x)]
    ring = load(weights, 0, before[0], None, (source, order, slots))
    rows, stats = partial_stats(gathered, ring)
    every_stat = [stats] + [swap(stats, bits) for bits in range(1, size_y)]
    ring = load(weights, before[0], before[1], ring, (stats,))
    x = normed_rows(source, gain, rows, every_stat, ring)

    def chunk_sums(chunk, ring, after):
        first, count = bounds[chunk], bounds[chunk + 1] - bounds[chunk]
        return wide_sums(x, weights, ring, first, count, ahead[chunk], ahead[chunk + 1], after)

    def to_chips(parts):
        return [shift_y(part, 2 * by) for by, part in enumerate(parts[: chips - 1], 1)]

    send_0, keep_0, keep_q, ring = first_sums(
        x, weights, w_query, w_keyval, ring, bounds[1], ahead[1]
    )
    send_1, keep_1, ring = chunk_sums(1, ring, (send_0,))
    parts_0 = combine(chips, swap(send_0), keep_0, keep_q)
    from_0 = to_chips(parts_0)

    send_2, keep_2, ring = chunk_sums(2, ring, (parts_0[0], send_1))
    parts_1 = combine(chips, swap(send_1), keep_1)
    from_1 = to_chips(parts_1)
    turned = query_rows(order, [parts_0[-1]] + from_0, size_x)
    new = [turned[0]] + [swap_x(turned[bits], bits) for bits in range(1, size_x)]

    send_3, keep_3, _ = chunk_sums(3, ring, (parts_1[0], turned[0], send_2))
    *parts_2, send_3 = combine(chips, swap(send_2), keep_2, None, send_3, (*new[1:], from_1[0]))
    from_2 = to_chips(parts_2)
    parts_3 = combine(chips, swap(send_3), keep_3)
    from_3 = to_chips(parts_3)
    half_done = gated(
        [[parts_0[chips - 1]] + from_0, [parts_1[-1]] + from_1],
        pltpu.VMEM((local, size_x, steps, bounds[2] * TILE), BF16),
        (),
        (parts_3[0],),
    )
    context = attend(
        slots,
        lengths.reshape(local),
        cache.reshape(local, cache.shape[2], cache.shape[3]),
        new,
        steps,
        w_query.shape[1],
        (parts_3[0],),
    )
    hidden = gated(
        [[parts_2[-1]] + from_2, [parts_3[-1]] + from_3],
        jax.ShapeDtypeStruct((local, size_x, steps, w_gate.shape[1]), BF16),
        (half_done,),
    )
    return (context, hidden)


def solution(mesh):
    return jax.shard_map(
        on_device,
        mesh=mesh,
        in_specs=(
            P("groups", "gx", None, "gy"),
            P("gy"),
            P("gy", "gx"),
            P("gy", "gx"),
            P("gy", "gx"),
            P("gy", "gx"),
            P(("groups", "gy"), "gx", None, None),
            P(("groups", "gy"), "gx"),
        ),
        out_specs=(P(("groups", "gy"), "gx", None, None), P(("groups", "gy"), None, None, "gx")),
        check_vma=False,
    )
```

```python
import functools

import jax
import jax.numpy as jnp
from jax import lax
from jax.experimental import pallas as pl
from jax.experimental.pallas import tpu as pltpu
from jax.sharding import PartitionSpec as P

D = 9216
HEADS = 24
HD = 256
EPSILON = 1e-05
MASKED = -1e30
MIB = 1024 * 1024
TILE = 256
SLOTS = 10
F32 = jnp.float32
BF16 = jnp.bfloat16


def whole(memory_space=pltpu.VMEM):
    return pl.BlockSpec(memory_space=memory_space)


def cost_of(*arrays):
    size = sum(a.size for a in arrays)
    return pl.CostEstimate(flops=size, bytes_accessed=size // 16, transcendentals=0)


def params():
    return pltpu.CompilerParams(vmem_limit_bytes=9 * MIB)


def stats_kernel(count, *refs):
    token_refs, (rows_ref, out_ref) = refs[:count], refs[-2:]
    tall, _, steps, features = token_refs[0].shape
    for index, ref in enumerate(token_refs):
        for t in range(tall):
            first = (index * tall + t) * steps
            rows_ref[first : first + steps] = ref[t, 0].astype(F32)
    floats = rows_ref[...]
    sums = jnp.sum(floats, axis=-1, keepdims=True)
    squares = jnp.sum(floats * floats, axis=-1, keepdims=True)
    lane = lax.broadcasted_iota(jnp.int32, out_ref.shape, 1)
    out_ref[...] = jnp.where(lane < 64, sums, squares)


def partial_stats(tokens, after):
    tall, _, steps, features = tokens[0].shape
    rows = len(tokens) * tall * steps
    return pl.pallas_call(
        functools.partial(stats_kernel, len(tokens)),
        out_shape=(pltpu.VMEM((rows, features), F32), pltpu.VMEM((rows, 128), F32)),
        in_specs=[whole()] * len(tokens) + [whole(pl.ANY)],
        out_specs=(whole(), whole()),
        compiler_params=params(),
        cost_estimate=cost_of(*tokens),
    )(*tokens, after)


def norm_kernel(source_ref, gain_ref, rows_ref, *refs):
    stat_refs, out_ref = refs[:-2], refs[-1]
    stats = stat_refs[0][...]
    for ref in stat_refs[1:]:
        stats = stats + ref[...]
    average = stats[:, 0:1] / D
    inverse_std = lax.rsqrt(stats[:, 64:65] / D - average * average + EPSILON)
    normed = ((rows_ref[...] - average) * inverse_std * gain_ref[...][None, :]).astype(BF16)
    rows = normed.shape[0]
    place = lax.broadcasted_iota(jnp.int32, (rows, rows), 1) == source_ref[...]
    out_ref[...] = jnp.dot(
        jnp.where(place, 1.0, 0.0).astype(BF16), normed, preferred_element_type=F32
    ).astype(BF16)


def normed_rows(source, gain, rows, stats, after):
    return pl.pallas_call(
        norm_kernel,
        out_shape=pltpu.VMEM(rows.shape, BF16),
        in_specs=[whole()] * (3 + len(stats)) + [whole(pl.ANY)],
        out_specs=whole(),
        compiler_params=params(),
        cost_estimate=cost_of(rows),
    )(source, gain, rows, *stats, after)


def combine_kernel(chips, small, skip, *refs):
    sent_ref, keep_ref = refs[:2]
    out_refs = refs[skip:]
    cols = keep_ref.shape[2]
    block = keep_ref.shape[1] // chips
    for index in range(chips):
        rows = slice(index * block, (index + 1) * block)
        total = keep_ref[:, rows] + sent_ref[:, rows, :cols].astype(F32)
        out_refs[index][:, :, :cols] = total.astype(out_refs[index].dtype)
        if small:
            sent = sent_ref[0, rows, cols:].astype(F32) + sent_ref[1, rows, cols:].astype(F32)
            total = refs[2][rows] + sent
            if index == chips - 1:
                out_refs[chips][...] = total
            else:
                store_split(out_refs[index], slice(cols, cols + small), total)


def combine(chips, sent, keep, keep_q=None, carry=None, after=()):
    small = 0 if keep_q is None else keep_q.shape[1]
    block = keep.shape[1] // chips
    out_shape = [pltpu.VMEM((2, block, sent.shape[2]), BF16)] * (chips - 1)
    out_shape.append(pltpu.VMEM((2, block, keep.shape[2]), F32))
    if small:
        out_shape.append(pltpu.VMEM((block, small), F32))
    args = (sent, keep, keep_q) if small else (sent, keep)
    extra = [*after] if carry is None else [*after, *in_vmem((carry,))]
    out_specs = [whole()] * len(out_shape)
    aliases = {}
    if carry is not None:
        aliases = {len(args) + len(after): len(out_shape)}
        out_shape.append(pltpu.VMEM(carry.shape, carry.dtype))
        out_specs.append(whole())
    return pl.pallas_call(
        functools.partial(combine_kernel, chips, small, len(args) + len(extra)),
        out_shape=out_shape,
        in_specs=[whole()] * len(args)
        + [whole(pl.ANY)] * len(after)
        + [whole()] * (len(extra) - len(after)),
        out_specs=out_specs,
        input_output_aliases=aliases,
        compiler_params=params(),
        cost_estimate=cost_of(*args),
    )(*args, *extra)


def query_rows_kernel(count, source_ref, *refs):
    term_refs, out_refs = refs[:-count], refs[-count:]
    total = term_refs[0][...]
    rows, cols = total.shape
    for ref in term_refs[1:]:
        first = ref.shape[2] - cols
        total = total + (ref[0, :, first:].astype(F32) + ref[1, :, first:].astype(F32))
    place = lax.broadcasted_iota(jnp.int32, (rows, rows), 1) == source_ref[...]
    turned = jnp.dot(
        jnp.where(place, 1.0, 0.0).astype(BF16), total.astype(BF16), preferred_element_type=F32
    )
    each = rows // count
    for index, ref in enumerate(out_refs):
        ref[...] = turned[index * each : (index + 1) * each].astype(BF16)


def query_rows(source, terms, count):
    rows, cols = terms[0].shape
    return pl.pallas_call(
        functools.partial(query_rows_kernel, count),
        out_shape=[pltpu.VMEM((rows // count, cols), BF16)] * count,
        in_specs=[whole()] * (1 + len(terms)),
        out_specs=[whole()] * count,
        compiler_params=params(),
        cost_estimate=cost_of(*terms),
    )(source, *terms)


def gated_kernel(counts, ready, *refs):
    out_ref = refs[-1]
    local, wide, steps, _ = out_ref.shape
    taken, first = ready, 0
    for ref in refs[:ready]:
        out_ref[:, :, :, : ref.shape[3]] = ref[...]
        first = ref.shape[3]
    for count in counts:
        total = refs[taken][...]
        cols = total.shape[2]
        for ref in refs[taken + 1 : taken + count]:
            total = total + ref[:, :, :cols].astype(F32)
        taken += count
        gate, up = total[0], total[1]
        hidden = gate / (1.0 + jnp.exp(-gate)) * up
        for row in range(local * wide):
            piece = hidden[row * steps : (row + 1) * steps].astype(BF16)
            out_ref[row // wide, row % wide, :, first : first + cols] = piece
        first += cols


def gated(chunks, out_shape, ready=(), after=()):
    terms = [term for chunk in chunks for term in chunk]
    return pl.pallas_call(
        functools.partial(gated_kernel, [len(chunk) for chunk in chunks], len(ready)),
        out_shape=out_shape,
        in_specs=[whole()] * (len(ready) + len(terms)) + [whole(pl.ANY)] * len(after),
        out_specs=whole(),
        compiler_params=params(),
        cost_estimate=cost_of(*ready, *terms),
    )(*ready, *terms, *after)


def in_hbm(arrays):
    return [pltpu.with_memory_space_constraint(a, pltpu.HBM) for a in arrays]


def in_vmem(arrays):
    return [pltpu.with_memory_space_constraint(a, pltpu.VMEM) for a in arrays]


def tile_copies(w_refs, tile, ring, sems):
    columns = pl.ds(pl.multiple_of(tile * TILE, TILE), TILE)
    slot = lax.rem(tile, SLOTS)
    return [
        pltpu.make_async_copy(
            ref.at[:, columns], ring.at[slot, :, index * TILE : (index + 1) * TILE], sems.at[slot, index]
        )
        for index, ref in enumerate(w_refs)
    ]


def each_tile(first, last, action):
    def body(tile, carry):
        action(tile)
        return carry

    lax.fori_loop(first, last, body, 0)


def ring_shape(features):
    return pltpu.VMEM((SLOTS, features, 2 * TILE), BF16)


def load_kernel(first, last, wg_ref, wu_ref, *refs):
    ring, sems = refs[-2:]

    def start(tile):
        for copy in tile_copies((wg_ref, wu_ref), tile, ring, sems):
            copy.start()

    def wait(tile):
        for copy in tile_copies((wg_ref, wu_ref), tile, ring, sems):
            copy.wait()

    each_tile(first, last, start)
    each_tile(first, last, wait)


def load(weights, first, last, ring, after):
    features = weights[0].shape[0]
    rings = [] if ring is None else in_vmem((ring,))
    return pl.pallas_call(
        functools.partial(load_kernel, first, last),
        out_shape=ring_shape(features),
        in_specs=[whole(pltpu.HBM)] * 2 + [whole()] * len(rings) + [whole(pl.ANY)] * len(after),
        out_specs=whole(),
        scratch_shapes=[pltpu.SemaphoreType.DMA((SLOTS, 2))],
        input_output_aliases={2: 0} if rings else {},
        compiler_params=params(),
        cost_estimate=pl.CostEstimate(
            flops=0, bytes_accessed=4 * features * TILE * (last - first), transcendentals=0
        ),
    )(*in_hbm(weights), *rings, *after)


def store_split(ref, columns, value):
    high = value.astype(BF16)
    ref[0, :, columns] = high
    ref[1, :, columns] = (value - high.astype(F32)).astype(BF16)


def multiply_tiles(first, tiles, held, following, x_ref, w_refs, ring, sems, send_ref, keep_ref):
    loads = tiles + following - held
    early = min(6, SLOTS - held, loads)

    def start(index):
        for copy in tile_copies(w_refs, first + held + index, ring, sems):
            copy.start()

    def wait(index):
        for copy in tile_copies(w_refs, first + held + index, ring, sems):
            copy.wait()

    def multiply(index):
        if held < tiles:

            @pl.when(index >= held)
            def _():
                wait(index - held)

        place = ring.at[lax.rem(first + index, SLOTS)]
        part = jnp.dot(x_ref[...], place[...], preferred_element_type=F32)
        half = part.shape[0] // 2
        columns = pl.ds(pl.multiple_of(index * TILE, TILE), TILE)
        for which in range(2):
            lanes = slice(which * TILE, (which + 1) * TILE)
            send_ref[which, :, columns] = part[:half, lanes].astype(BF16)
            keep_ref[which, :, columns] = part[half:, lanes]
        if early < loads:

            @pl.when(index + early < loads)
            def _():
                start(index + early)

    each_tile(0, early, start)
    each_tile(0, tiles, multiply)
    return lambda: each_tile(tiles - held, loads, wait)


def first_kernel(tiles, following, x_ref, wg_ref, wu_ref, wq_ref, wkv_ref, _, *refs):
    send_ref, keep_ref, keep_q_ref, ring, q_ref, kv_ref, small_sems, sems = refs
    half = x_ref.shape[0] // 2
    smalls = [
        pltpu.make_async_copy(wq_ref, q_ref, small_sems.at[0]),
        pltpu.make_async_copy(wkv_ref, kv_ref, small_sems.at[1]),
    ]
    for copy in smalls:
        copy.start()
    finish = multiply_tiles(0, tiles, tiles, following, x_ref, (wg_ref, wu_ref), ring, sems, send_ref, keep_ref)
    for copy in smalls:
        copy.wait()
    q_cols, kv_cols, base = q_ref.shape[1], kv_ref.shape[1], tiles * TILE
    piece = q_cols // 3

    def queries(index):
        columns = pl.ds(pl.multiple_of(index * piece, piece), piece)
        part = jnp.dot(x_ref[...], q_ref[:, columns], preferred_element_type=F32)
        sent = pl.ds(pl.multiple_of(base + index * piece, TILE), piece)
        store_split(send_ref, sent, part[:half])
        keep_q_ref[:, columns] = part[half:]

    each_tile(0, 3, queries)
    part = jnp.dot(x_ref[...], kv_ref[...], preferred_element_type=F32)
    store_split(send_ref, slice(base + q_cols, base + q_cols + kv_cols), part[:half])
    keep_q_ref[:, q_cols:] = part[half:]
    finish()


def first_sums(x, weights, w_query, w_keyval, ring, tiles, following):
    rows, features = x.shape
    cols, small = tiles * TILE, w_query.shape[1] + w_keyval.shape[1]
    return pl.pallas_call(
        functools.partial(first_kernel, tiles, following),
        out_shape=[
            pltpu.VMEM((2, rows // 2, cols + small), BF16),
            pltpu.VMEM((2, rows // 2, cols), F32),
            pltpu.VMEM((rows // 2, small), F32),
            ring_shape(features),
        ],
        in_specs=[whole()] + [whole(pltpu.HBM)] * 4 + [whole()],
        out_specs=[whole()] * 4,
        scratch_shapes=[
            pltpu.VMEM(w_query.shape, BF16),
            pltpu.VMEM(w_keyval.shape, BF16),
            pltpu.SemaphoreType.DMA((2,)),
            pltpu.SemaphoreType.DMA((SLOTS, 2)),
        ],
        input_output_aliases={5: 3},
        compiler_params=params(),
        cost_estimate=pl.CostEstimate(
            flops=2 * rows * features * (2 * cols + small),
            bytes_accessed=4 * features * cols,
            transcendentals=0,
        ),
    )(x, *in_hbm((*weights, w_query, w_keyval)), *in_vmem((ring,)))


def wide_kernel(first, tiles, held, following, x_ref, wg_ref, wu_ref, _, *refs):
    send_ref, keep_ref, ring, sems = refs[-4:]
    multiply_tiles(
        first, tiles, held, following, x_ref, (wg_ref, wu_ref), ring, sems, send_ref, keep_ref
    )()


def wide_sums(x, weights, ring, first, tiles, held, following, after):
    rows, features = x.shape
    cols = tiles * TILE
    return pl.pallas_call(
        functools.partial(wide_kernel, first, tiles, held, following),
        out_shape=[
            pltpu.VMEM((2, rows // 2, cols), BF16),
            pltpu.VMEM((2, rows // 2, cols), F32),
            ring_shape(features),
        ],
        in_specs=[whole(), whole(pltpu.HBM), whole(pltpu.HBM), whole()]
        + [whole(pl.ANY)] * len(after),
        out_specs=[whole()] * 3,
        scratch_shapes=[pltpu.SemaphoreType.DMA((SLOTS, 2))],
        input_output_aliases={3: 2},
        compiler_params=params(),
        cost_estimate=pl.CostEstimate(
            flops=4 * rows * features * cols,
            bytes_accessed=4 * features * TILE * (tiles + following - held),
            transcendentals=0,
        ),
    )(x, *in_hbm(weights), *in_vmem((ring,)), *after)


def attend_kernel(count, steps, query_cols, slot_ref, lengths_ref, cache_ref, *refs):
    part_refs, (out_ref, held, fresh) = refs[:count], refs[-3:]
    for index, ref in enumerate(part_refs):
        held[slot_ref[index]] = ref[...].astype(F32)
    pair_cols = held.shape[2] - query_cols
    heads = query_cols // HD
    scale = HD ** (-0.5)
    batch, positions = cache_ref.shape[0], cache_ref.shape[1]
    fresh[...] = jnp.zeros_like(fresh)
    for b in range(batch):
        rows = pl.ds(b * steps, steps)
        for c in range(count):
            fresh[b, :steps, c * pair_cols : (c + 1) * pair_cols] = held[c, rows, query_cols:]
        queries = jnp.concatenate(
            [held[c, rows, h * HD : (h + 1) * HD] for c in range(count) for h in range(heads)],
            axis=0,
        ).astype(BF16)
        pairs = fresh[b].astype(BF16)
        dims = (((1,), (1,)), ((), ()))
        old = lax.dot_general(
            queries, cache_ref[b, :, :HD], dims, preferred_element_type=F32
        ) * scale
        position = lax.broadcasted_iota(jnp.int32, old.shape, 1)
        old = jnp.where(position < lengths_ref[b], old, MASKED)
        new = lax.dot_general(queries, pairs[:, :HD], dims, preferred_element_type=F32) * scale
        step = lax.broadcasted_iota(jnp.int32, new.shape, 0) % steps
        new = jnp.where(lax.broadcasted_iota(jnp.int32, new.shape, 1) <= step, new, MASKED)
        highest = jnp.maximum(
            jnp.max(old, axis=-1, keepdims=True), jnp.max(new, axis=-1, keepdims=True)
        )
        old = jnp.exp(old - highest)
        new = jnp.exp(new - highest)
        total = jnp.sum(old, axis=-1, keepdims=True) + jnp.sum(new, axis=-1, keepdims=True)
        context = jnp.dot(
            (old / total).astype(BF16), cache_ref[b, :, HD:], preferred_element_type=F32
        ) + jnp.dot((new / total).astype(BF16), pairs[:, HD:], preferred_element_type=F32)
        for h in range(HEADS):
            piece = context[h * steps : (h + 1) * steps].astype(BF16)
            out_ref[b, 0, :, h * HD : (h + 1) * HD] = piece


def attend(slots, lengths, cache, parts, steps, query_cols, after):
    batch = cache.shape[0]
    count = len(parts)
    rows, cols = parts[0].shape
    return pl.pallas_call(
        functools.partial(attend_kernel, count, steps, query_cols),
        out_shape=jax.ShapeDtypeStruct((batch, 1, steps, HEADS * HD), BF16),
        in_specs=[whole(pltpu.SMEM), whole(pltpu.SMEM)] + [whole()] * (1 + count) + [whole(pl.ANY)] * len(after),
        out_specs=whole(),
        scratch_shapes=[
            pltpu.VMEM((count, rows, cols), F32),
            pltpu.VMEM((batch, 8, 2 * HD), F32),
        ],
        compiler_params=params(),
        cost_estimate=pl.CostEstimate(
            flops=4 * batch * steps * HEADS * HD * cache.shape[1],
            bytes_accessed=2 * cache.size,
            transcendentals=batch * steps * HEADS * cache.shape[1],
        ),
    )(slots, lengths, cache, *parts, *after)


def on_device(tokens, gain, w_query, w_keyval, w_gate, w_up, cache, lengths):
    size_x, size_y = lax.axis_size("gx"), lax.axis_size("gy")
    chips = size_y // 2
    me_x, me_y = lax.axis_index("gx"), lax.axis_index("gy")
    tall, _, steps, features = tokens.shape
    local = cache.shape[0]
    block = local * size_x * steps

    def shift_y(value, by):
        return lax.ppermute(value, "gy", [(i, (i + by) % size_y) for i in range(size_y)])

    def swap_x(value, bits):
        return lax.ppermute(value, "gx", [(i, i ^ bits) for i in range(size_x)])

    def swap(value, bits=1):
        return lax.ppermute(value, "gy", [(i, i ^ bits) for i in range(size_y)])

    row = jnp.arange(2 * chips * block, dtype=jnp.int32)
    core = jnp.where(row < chips * block, 1 - me_y % 2, me_y % 2)
    chip = (me_y // 2 + 1 + row // block % chips) % chips
    sequence = (chip * 2 + core) * local + row % block // (size_x * steps)
    column = row // steps % size_x
    source = (me_x ^ column) * (tall * steps) + sequence * steps + row % steps
    source = source[:, None]
    row = jnp.arange(block, dtype=jnp.int32)
    to = me_x ^ (row // (local * steps))
    order = row // steps % local * (size_x * steps) + to * steps + row % steps
    order = order[:, None]
    slots = me_x ^ jnp.arange(size_x, dtype=jnp.int32)

    weights = (w_gate, w_up)
    tiles = w_gate.shape[1] // TILE
    before = [tiles * share // 36 for share in (7, 9)]
    bounds = [0, before[1]] + [tiles * share // 36 for share in (23, 31, 36)]
    ahead = [before[1]] + [max(1, tiles * share // 36) for share in (5, 4, 4)] + [0]
    gathered = [tokens] + [swap_x(tokens, bits) for bits in range(1, size_x)]
    ring = load(weights, 0, before[0], None, (source, order, slots))
    rows, stats = partial_stats(gathered, ring)
    every_stat = [stats] + [swap(stats, bits) for bits in range(1, size_y)]
    ring = load(weights, before[0], before[1], ring, (stats,))
    x = normed_rows(source, gain, rows, every_stat, ring)

    def chunk_sums(chunk, ring, after):
        first, count = bounds[chunk], bounds[chunk + 1] - bounds[chunk]
        return wide_sums(x, weights, ring, first, count, ahead[chunk], ahead[chunk + 1], after)

    def to_chips(parts):
        return [shift_y(part, 2 * by) for by, part in enumerate(parts[: chips - 1], 1)]

    send_0, keep_0, keep_q, ring = first_sums(
        x, weights, w_query, w_keyval, ring, bounds[1], ahead[1]
    )
    send_1, keep_1, ring = chunk_sums(1, ring, (send_0,))
    parts_0 = combine(chips, swap(send_0), keep_0, keep_q)
    from_0 = to_chips(parts_0)

    send_2, keep_2, ring = chunk_sums(2, ring, (parts_0[0], send_1))
    parts_1 = combine(chips, swap(send_1), keep_1)
    from_1 = to_chips(parts_1)
    turned = query_rows(order, [parts_0[-1]] + from_0, size_x)
    new = [turned[0]] + [swap_x(turned[bits], bits) for bits in range(1, size_x)]

    send_3, keep_3, _ = chunk_sums(3, ring, (parts_1[0], turned[0], send_2))
    *parts_2, send_3 = combine(chips, swap(send_2), keep_2, None, send_3, (*new[1:], from_1[0]))
    from_2 = to_chips(parts_2)
    parts_3 = combine(chips, swap(send_3), keep_3)
    from_3 = to_chips(parts_3)
    half_done = gated(
        [[parts_0[chips - 1]] + from_0, [parts_1[-1]] + from_1],
        pltpu.VMEM((local, size_x, steps, bounds[2] * TILE), BF16),
        (),
        (parts_3[0],),
    )
    context = attend(
        slots,
        lengths.reshape(local),
        cache.reshape(local, cache.shape[2], cache.shape[3]),
        new,
        steps,
        w_query.shape[1],
        (parts_3[0],),
    )
    hidden = gated(
        [[parts_2[-1]] + from_2, [parts_3[-1]] + from_3],
        jax.ShapeDtypeStruct((local, size_x, steps, w_gate.shape[1]), BF16),
        (half_done,),
    )
    return (context, hidden)


def solution(mesh):
    return jax.shard_map(
        on_device,
        mesh=mesh,
        in_specs=(
            P("groups", "gx", None, "gy"),
            P("gy"),
            P("gy", "gx"),
            P("gy", "gx"),
            P("gy", "gx"),
            P("gy", "gx"),
            P(("groups", "gy"), "gx", None, None),
            P(("groups", "gy"), "gx"),
        ),
        out_specs=(P(("groups", "gy"), "gx", None, None), P(("groups", "gy"), None, None, "gx")),
        check_vma=False,
    )
```

```python
import functools

import jax
import jax.numpy as jnp
from jax import lax
from jax.experimental import pallas as pl
from jax.experimental.pallas import tpu as pltpu
from jax.sharding import PartitionSpec as P

D = 9216
HEADS = 24
HD = 256
EPSILON = 1e-05
MASKED = -1e30
MIB = 1024 * 1024
TILE = 256
SLOTS = 10
F32 = jnp.float32
BF16 = jnp.bfloat16


def whole(memory_space=pltpu.VMEM):
    return pl.BlockSpec(memory_space=memory_space)


def cost_of(*arrays):
    size = sum(a.size for a in arrays)
    return pl.CostEstimate(flops=size, bytes_accessed=size // 16, transcendentals=0)


def params():
    return pltpu.CompilerParams(vmem_limit_bytes=9 * MIB)


def stats_kernel(count, *refs):
    token_refs, (rows_ref, out_ref) = refs[:count], refs[-2:]
    tall, _, steps, features = token_refs[0].shape
    for index, ref in enumerate(token_refs):
        for t in range(tall):
            first = (index * tall + t) * steps
            rows_ref[first : first + steps] = ref[t, 0].astype(F32)
    floats = rows_ref[...]
    sums = jnp.sum(floats, axis=-1, keepdims=True)
    squares = jnp.sum(floats * floats, axis=-1, keepdims=True)
    lane = lax.broadcasted_iota(jnp.int32, out_ref.shape, 1)
    out_ref[...] = jnp.where(lane < 64, sums, squares)


def partial_stats(tokens, after):
    tall, _, steps, features = tokens[0].shape
    rows = len(tokens) * tall * steps
    return pl.pallas_call(
        functools.partial(stats_kernel, len(tokens)),
        out_shape=(pltpu.VMEM((rows, features), F32), pltpu.VMEM((rows, 128), F32)),
        in_specs=[whole()] * len(tokens) + [whole(pl.ANY)],
        out_specs=(whole(), whole()),
        compiler_params=params(),
        cost_estimate=cost_of(*tokens),
    )(*tokens, after)


def norm_kernel(source_ref, gain_ref, rows_ref, *refs):
    stat_refs, out_ref = refs[:-2], refs[-1]
    stats = stat_refs[0][...]
    for ref in stat_refs[1:]:
        stats = stats + ref[...]
    average = stats[:, 0:1] / D
    inverse_std = lax.rsqrt(stats[:, 64:65] / D - average * average + EPSILON)
    normed = ((rows_ref[...] - average) * inverse_std * gain_ref[...][None, :]).astype(BF16)
    rows = normed.shape[0]
    place = lax.broadcasted_iota(jnp.int32, (rows, rows), 1) == source_ref[...]
    out_ref[...] = jnp.dot(
        jnp.where(place, 1.0, 0.0).astype(BF16), normed, preferred_element_type=F32
    ).astype(BF16)


def normed_rows(source, gain, rows, stats, after):
    return pl.pallas_call(
        norm_kernel,
        out_shape=pltpu.VMEM(rows.shape, BF16),
        in_specs=[whole()] * (3 + len(stats)) + [whole(pl.ANY)],
        out_specs=whole(),
        compiler_params=params(),
        cost_estimate=cost_of(rows),
    )(source, gain, rows, *stats, after)


def combine_kernel(chips, small, skip, *refs):
    sent_ref, keep_ref = refs[:2]
    out_refs = refs[skip:]
    cols = keep_ref.shape[2]
    block = keep_ref.shape[1] // chips
    for index in range(chips):
        rows = slice(index * block, (index + 1) * block)
        total = keep_ref[:, rows] + sent_ref[:, rows, :cols].astype(F32)
        out_refs[index][:, :, :cols] = total.astype(out_refs[index].dtype)
        if small:
            sent = sent_ref[0, rows, cols:].astype(F32) + sent_ref[1, rows, cols:].astype(F32)
            total = refs[2][rows] + sent
            if index == chips - 1:
                out_refs[chips][...] = total
            else:
                store_split(out_refs[index], slice(cols, cols + small), total)


def combine(chips, sent, keep, keep_q=None, carry=None, after=()):
    small = 0 if keep_q is None else keep_q.shape[1]
    block = keep.shape[1] // chips
    out_shape = [pltpu.VMEM((2, block, sent.shape[2]), BF16)] * (chips - 1)
    out_shape.append(pltpu.VMEM((2, block, keep.shape[2]), F32))
    if small:
        out_shape.append(pltpu.VMEM((block, small), F32))
    args = (sent, keep, keep_q) if small else (sent, keep)
    extra = [*after] if carry is None else [*after, *in_vmem((carry,))]
    out_specs = [whole()] * len(out_shape)
    aliases = {}
    if carry is not None:
        aliases = {len(args) + len(after): len(out_shape)}
        out_shape.append(pltpu.VMEM(carry.shape, carry.dtype))
        out_specs.append(whole())
    return pl.pallas_call(
        functools.partial(combine_kernel, chips, small, len(args) + len(extra)),
        out_shape=out_shape,
        in_specs=[whole()] * len(args)
        + [whole(pl.ANY)] * len(after)
        + [whole()] * (len(extra) - len(after)),
        out_specs=out_specs,
        input_output_aliases=aliases,
        compiler_params=params(),
        cost_estimate=cost_of(*args),
    )(*args, *extra)


def query_rows_kernel(count, source_ref, *refs):
    term_refs, out_refs = refs[:-count], refs[-count:]
    total = term_refs[0][...]
    rows, cols = total.shape
    for ref in term_refs[1:]:
        first = ref.shape[2] - cols
        total = total + (ref[0, :, first:].astype(F32) + ref[1, :, first:].astype(F32))
    place = lax.broadcasted_iota(jnp.int32, (rows, rows), 1) == source_ref[...]
    turned = jnp.dot(
        jnp.where(place, 1.0, 0.0).astype(BF16), total.astype(BF16), preferred_element_type=F32
    )
    each = rows // count
    for index, ref in enumerate(out_refs):
        ref[0] = turned[index * each : (index + 1) * each].astype(BF16)


def query_rows(source, terms, count):
    rows, cols = terms[0].shape
    return pl.pallas_call(
        functools.partial(query_rows_kernel, count),
        out_shape=[pltpu.VMEM((1, rows // count, cols), BF16)] * count,
        in_specs=[whole()] * (1 + len(terms)),
        out_specs=[whole()] * count,
        compiler_params=params(),
        cost_estimate=cost_of(*terms),
    )(source, *terms)


def gated_kernel(counts, ready, *refs):
    out_ref = refs[-1]
    local, wide, steps, _ = out_ref.shape
    taken, first = ready, 0
    for ref in refs[:ready]:
        out_ref[:, :, :, : ref.shape[3]] = ref[...]
        first = ref.shape[3]
    for count in counts:
        total = refs[taken][...]
        cols = total.shape[2]
        for ref in refs[taken + 1 : taken + count]:
            total = total + ref[:, :, :cols].astype(F32)
        taken += count
        gate, up = total[0], total[1]
        hidden = gate / (1.0 + jnp.exp(-gate)) * up
        for row in range(local * wide):
            piece = hidden[row * steps : (row + 1) * steps].astype(BF16)
            out_ref[row // wide, row % wide, :, first : first + cols] = piece
        first += cols


def gated(chunks, out_shape, ready=(), after=()):
    terms = [term for chunk in chunks for term in chunk]
    return pl.pallas_call(
        functools.partial(gated_kernel, [len(chunk) for chunk in chunks], len(ready)),
        out_shape=out_shape,
        in_specs=[whole()] * (len(ready) + len(terms)) + [whole(pl.ANY)] * len(after),
        out_specs=whole(),
        compiler_params=params(),
        cost_estimate=cost_of(*ready, *terms),
    )(*ready, *terms, *after)


def in_hbm(arrays):
    return [pltpu.with_memory_space_constraint(a, pltpu.HBM) for a in arrays]


def in_vmem(arrays):
    return [pltpu.with_memory_space_constraint(a, pltpu.VMEM) for a in arrays]


def tile_copies(w_refs, tile, ring, sems):
    columns = pl.ds(pl.multiple_of(tile * TILE, TILE), TILE)
    slot = lax.rem(tile, SLOTS)
    return [
        pltpu.make_async_copy(
            ref.at[:, columns], ring.at[slot, :, index * TILE : (index + 1) * TILE], sems.at[slot, index]
        )
        for index, ref in enumerate(w_refs)
    ]


def each_tile(first, last, action):
    def body(tile, carry):
        action(tile)
        return carry

    lax.fori_loop(first, last, body, 0)


def ring_shape(features):
    return pltpu.VMEM((SLOTS, features, 2 * TILE), BF16)


def load_kernel(first, last, wg_ref, wu_ref, *refs):
    ring, sems = refs[-2:]

    def start(tile):
        for copy in tile_copies((wg_ref, wu_ref), tile, ring, sems):
            copy.start()

    def wait(tile):
        for copy in tile_copies((wg_ref, wu_ref), tile, ring, sems):
            copy.wait()

    each_tile(first, last, start)
    each_tile(first, last, wait)


def load(weights, first, last, ring, after):
    features = weights[0].shape[0]
    rings = [] if ring is None else in_vmem((ring,))
    return pl.pallas_call(
        functools.partial(load_kernel, first, last),
        out_shape=ring_shape(features),
        in_specs=[whole(pltpu.HBM)] * 2 + [whole()] * len(rings) + [whole(pl.ANY)] * len(after),
        out_specs=whole(),
        scratch_shapes=[pltpu.SemaphoreType.DMA((SLOTS, 2))],
        input_output_aliases={2: 0} if rings else {},
        compiler_params=params(),
        cost_estimate=pl.CostEstimate(
            flops=0, bytes_accessed=4 * features * TILE * (last - first), transcendentals=0
        ),
    )(*in_hbm(weights), *rings, *after)


def store_split(ref, columns, value):
    high = value.astype(BF16)
    ref[0, :, columns] = high
    ref[1, :, columns] = (value - high.astype(F32)).astype(BF16)


def multiply_tiles(first, tiles, held, following, x_ref, w_refs, ring, sems, send_ref, keep_ref):
    loads = tiles + following - held
    early = min(6, SLOTS - held, loads)

    def start(index):
        for copy in tile_copies(w_refs, first + held + index, ring, sems):
            copy.start()

    def wait(index):
        for copy in tile_copies(w_refs, first + held + index, ring, sems):
            copy.wait()

    def multiply(index):
        if held < tiles:

            @pl.when(index >= held)
            def _():
                wait(index - held)

        place = ring.at[lax.rem(first + index, SLOTS)]
        part = jnp.dot(x_ref[...], place[...], preferred_element_type=F32)
        half = part.shape[0] // 2
        columns = pl.ds(pl.multiple_of(index * TILE, TILE), TILE)
        for which in range(2):
            lanes = slice(which * TILE, (which + 1) * TILE)
            send_ref[which, :, columns] = part[:half, lanes].astype(BF16)
            keep_ref[which, :, columns] = part[half:, lanes]
        if early < loads:

            @pl.when(index + early < loads)
            def _():
                start(index + early)

    each_tile(0, early, start)
    each_tile(0, tiles, multiply)
    return lambda: each_tile(tiles - held, loads, wait)


def first_kernel(tiles, following, x_ref, wg_ref, wu_ref, wq_ref, wkv_ref, _, *refs):
    send_ref, keep_ref, keep_q_ref, ring, q_ref, kv_ref, small_sems, sems = refs
    half = x_ref.shape[0] // 2
    smalls = [
        pltpu.make_async_copy(wq_ref, q_ref, small_sems.at[0]),
        pltpu.make_async_copy(wkv_ref, kv_ref, small_sems.at[1]),
    ]
    for copy in smalls:
        copy.start()
    finish = multiply_tiles(0, tiles, tiles, following, x_ref, (wg_ref, wu_ref), ring, sems, send_ref, keep_ref)
    for copy in smalls:
        copy.wait()
    q_cols, kv_cols, base = q_ref.shape[1], kv_ref.shape[1], tiles * TILE
    piece = q_cols // 3

    def queries(index):
        columns = pl.ds(pl.multiple_of(index * piece, piece), piece)
        part = jnp.dot(x_ref[...], q_ref[:, columns], preferred_element_type=F32)
        sent = pl.ds(pl.multiple_of(base + index * piece, TILE), piece)
        store_split(send_ref, sent, part[:half])
        keep_q_ref[:, columns] = part[half:]

    each_tile(0, 3, queries)
    part = jnp.dot(x_ref[...], kv_ref[...], preferred_element_type=F32)
    store_split(send_ref, slice(base + q_cols, base + q_cols + kv_cols), part[:half])
    keep_q_ref[:, q_cols:] = part[half:]
    finish()


def first_sums(x, weights, w_query, w_keyval, ring, tiles, following):
    rows, features = x.shape
    cols, small = tiles * TILE, w_query.shape[1] + w_keyval.shape[1]
    return pl.pallas_call(
        functools.partial(first_kernel, tiles, following),
        out_shape=[
            pltpu.VMEM((2, rows // 2, cols + small), BF16),
            pltpu.VMEM((2, rows // 2, cols), F32),
            pltpu.VMEM((rows // 2, small), F32),
            ring_shape(features),
        ],
        in_specs=[whole()] + [whole(pltpu.HBM)] * 4 + [whole()],
        out_specs=[whole()] * 4,
        scratch_shapes=[
            pltpu.VMEM(w_query.shape, BF16),
            pltpu.VMEM(w_keyval.shape, BF16),
            pltpu.SemaphoreType.DMA((2,)),
            pltpu.SemaphoreType.DMA((SLOTS, 2)),
        ],
        input_output_aliases={5: 3},
        compiler_params=params(),
        cost_estimate=pl.CostEstimate(
            flops=2 * rows * features * (2 * cols + small),
            bytes_accessed=4 * features * cols,
            transcendentals=0,
        ),
    )(x, *in_hbm((*weights, w_query, w_keyval)), *in_vmem((ring,)))


def wide_kernel(first, tiles, held, following, x_ref, wg_ref, wu_ref, _, *refs):
    send_ref, keep_ref, ring, sems = refs[-4:]
    multiply_tiles(
        first, tiles, held, following, x_ref, (wg_ref, wu_ref), ring, sems, send_ref, keep_ref
    )()


def wide_sums(x, weights, ring, first, tiles, held, following, after):
    rows, features = x.shape
    cols = tiles * TILE
    return pl.pallas_call(
        functools.partial(wide_kernel, first, tiles, held, following),
        out_shape=[
            pltpu.VMEM((2, rows // 2, cols), BF16),
            pltpu.VMEM((2, rows // 2, cols), F32),
            ring_shape(features),
        ],
        in_specs=[whole(), whole(pltpu.HBM), whole(pltpu.HBM), whole()]
        + [whole(pl.ANY)] * len(after),
        out_specs=[whole()] * 3,
        scratch_shapes=[pltpu.SemaphoreType.DMA((SLOTS, 2))],
        input_output_aliases={3: 2},
        compiler_params=params(),
        cost_estimate=pl.CostEstimate(
            flops=4 * rows * features * cols,
            bytes_accessed=4 * features * TILE * (tiles + following - held),
            transcendentals=0,
        ),
    )(x, *in_hbm(weights), *in_vmem((ring,)), *after)


def merge_kernel(kept_ref, came_ref, keep_ref, send_ref):
    half = keep_ref.shape[1]
    count = kept_ref.shape[0]
    for index in range(2 * count):
        both = (kept_ref[index] if index < count else came_ref[index - count]).astype(F32)
        keep_ref[index] = both[:half].astype(BF16)
        send_ref[index] = both[half:].astype(BF16)


def merge(kept, came):
    count, rows, cols = kept.shape
    out = pltpu.VMEM((2 * count, rows // 2, cols), BF16)
    return pl.pallas_call(
        merge_kernel,
        out_shape=(out, out),
        in_specs=[whole()] * 2,
        out_specs=(whole(), whole()),
        compiler_params=params(),
        cost_estimate=cost_of(kept, came),
    )(kept, came)


def attend_kernel(count, steps, query_cols, slot_ref, lengths_ref, cache_ref, *refs):
    part_refs, (out_ref, held, fresh) = refs[:count], refs[-3:]
    each = part_refs[0].shape[0]
    for index, ref in enumerate(part_refs):
        for source in range(each):
            held[slot_ref[index * each + source]] = ref[source].astype(F32)
    count = count * each
    pair_cols = held.shape[2] - query_cols
    heads = query_cols // HD
    scale = HD ** (-0.5)
    batch, positions = cache_ref.shape[0], cache_ref.shape[1]
    fresh[...] = jnp.zeros_like(fresh)
    for b in range(batch):
        rows = pl.ds(b * steps, steps)
        for c in range(count):
            fresh[b, :steps, c * pair_cols : (c + 1) * pair_cols] = held[c, rows, query_cols:]
        queries = jnp.concatenate(
            [held[c, rows, h * HD : (h + 1) * HD] for c in range(count) for h in range(heads)],
            axis=0,
        ).astype(BF16)
        pairs = fresh[b].astype(BF16)
        dims = (((1,), (1,)), ((), ()))
        old = lax.dot_general(
            queries, cache_ref[b, :, :HD], dims, preferred_element_type=F32
        ) * scale
        position = lax.broadcasted_iota(jnp.int32, old.shape, 1)
        old = jnp.where(position < lengths_ref[b], old, MASKED)
        new = lax.dot_general(queries, pairs[:, :HD], dims, preferred_element_type=F32) * scale
        step = lax.broadcasted_iota(jnp.int32, new.shape, 0) % steps
        new = jnp.where(lax.broadcasted_iota(jnp.int32, new.shape, 1) <= step, new, MASKED)
        highest = jnp.maximum(
            jnp.max(old, axis=-1, keepdims=True), jnp.max(new, axis=-1, keepdims=True)
        )
        old = jnp.exp(old - highest)
        new = jnp.exp(new - highest)
        total = jnp.sum(old, axis=-1, keepdims=True) + jnp.sum(new, axis=-1, keepdims=True)
        context = jnp.dot(
            (old / total).astype(BF16), cache_ref[b, :, HD:], preferred_element_type=F32
        ) + jnp.dot((new / total).astype(BF16), pairs[:, HD:], preferred_element_type=F32)
        for h in range(HEADS):
            piece = context[h * steps : (h + 1) * steps].astype(BF16)
            out_ref[b, 0, :, h * HD : (h + 1) * HD] = piece


def attend(slots, lengths, cache, parts, steps, query_cols, after):
    batch = cache.shape[0]
    count = len(parts)
    sources, rows, cols = parts[0].shape
    return pl.pallas_call(
        functools.partial(attend_kernel, count, steps, query_cols),
        out_shape=jax.ShapeDtypeStruct((batch, 1, steps, HEADS * HD), BF16),
        in_specs=[whole(pltpu.SMEM), whole(pltpu.SMEM)] + [whole()] * (1 + count) + [whole(pl.ANY)] * len(after),
        out_specs=whole(),
        scratch_shapes=[
            pltpu.VMEM((count * sources, rows, cols), F32),
            pltpu.VMEM((batch, 8, 2 * HD), F32),
        ],
        compiler_params=params(),
        cost_estimate=pl.CostEstimate(
            flops=4 * batch * steps * HEADS * HD * cache.shape[1],
            bytes_accessed=2 * cache.size,
            transcendentals=batch * steps * HEADS * cache.shape[1],
        ),
    )(slots, lengths, cache, *parts, *after)


def on_device(tokens, gain, w_query, w_keyval, w_gate, w_up, cache, lengths):
    size_x, size_y = lax.axis_size("gx"), lax.axis_size("gy")
    chips = size_y // 2
    me_x, me_y = lax.axis_index("gx"), lax.axis_index("gy")
    tall, _, steps, features = tokens.shape
    local = cache.shape[0]
    block = local * size_x * steps

    def shift_y(value, by):
        return lax.ppermute(value, "gy", [(i, (i + by) % size_y) for i in range(size_y)])

    def swap_x(value, bits):
        return lax.ppermute(value, "gx", [(i, i ^ bits) for i in range(size_x)])

    def swap(value, bits=1):
        return lax.ppermute(value, "gy", [(i, i ^ bits) for i in range(size_y)])

    row = jnp.arange(2 * chips * block, dtype=jnp.int32)
    core = jnp.where(row < chips * block, 1 - me_y % 2, me_y % 2)
    chip = (me_y // 2 + 1 + row // block % chips) % chips
    sequence = (chip * 2 + core) * local + row % block // (size_x * steps)
    column = row // steps % size_x
    source = (me_x ^ column) * (tall * steps) + sequence * steps + row % steps
    source = source[:, None]
    row = jnp.arange(block, dtype=jnp.int32)
    to = me_x ^ (row // (local * steps))
    order = row // steps % local * (size_x * steps) + to * steps + row % steps
    order = order[:, None]
    bits, offsets = [], [0]
    while len(offsets) < size_x:
        bits.append(size_x // (2 * len(offsets)))
        offsets = offsets + [offset ^ bits[-1] for offset in offsets]
    number = jnp.arange(size_x, dtype=jnp.int32)
    slots = me_x ^ sum((number >> place & 1) * bit for place, bit in enumerate(bits))

    weights = (w_gate, w_up)
    tiles = w_gate.shape[1] // TILE
    before = [tiles * share // 36 for share in (7, 9)]
    bounds = [0, before[1]] + [tiles * share // 36 for share in (20, 29, 36)]
    ahead = [before[1]] + [max(1, tiles * share // 36) for share in (5, 4, 4)] + [0]
    gathered = [tokens] + [swap_x(tokens, bits) for bits in range(1, size_x)]
    ring = load(weights, 0, before[0], None, (source, order, slots))
    rows, stats = partial_stats(gathered, ring)
    every_stat = [stats] + [swap(stats, bits) for bits in range(1, size_y)]
    ring = load(weights, before[0], before[1], ring, (stats,))
    x = normed_rows(source, gain, rows, every_stat, ring)

    def chunk_sums(chunk, ring, after):
        first, count = bounds[chunk], bounds[chunk + 1] - bounds[chunk]
        return wide_sums(x, weights, ring, first, count, ahead[chunk], ahead[chunk + 1], after)

    def to_chips(parts):
        return [shift_y(part, 2 * by) for by, part in enumerate(parts[: chips - 1], 1)]

    send_0, keep_0, keep_q, ring = first_sums(
        x, weights, w_query, w_keyval, ring, bounds[1], ahead[1]
    )
    send_1, keep_1, ring = chunk_sums(1, ring, (send_0,))
    parts_0 = combine(chips, swap(send_0), keep_0, keep_q)
    from_0 = to_chips(parts_0)

    send_2, keep_2, ring = chunk_sums(2, ring, (parts_0[0], send_1))
    parts_1 = combine(chips, swap(send_1), keep_1)
    from_1 = to_chips(parts_1)
    kept, leaving = query_rows(order, [parts_0[-1]] + from_0, 2)
    came = swap_x(leaving, bits[0])

    send_3, keep_3, _ = chunk_sums(3, ring, (parts_1[0], kept, send_2))
    *parts_2, send_3 = combine(chips, swap(send_2), keep_2, None, send_3, (came, from_1[0]))
    from_2 = to_chips(parts_2)
    for bit in bits[1:]:
        kept, leaving = merge(kept, came)
        came = swap_x(leaving, bit)
    parts_3 = combine(chips, swap(send_3), keep_3)
    from_3 = to_chips(parts_3)
    half_done = gated(
        [[parts_0[chips - 1]] + from_0, [parts_1[-1]] + from_1],
        pltpu.VMEM((local, size_x, steps, bounds[2] * TILE), BF16),
        (),
        (parts_3[0],),
    )
    context = attend(
        slots,
        lengths.reshape(local),
        cache.reshape(local, cache.shape[2], cache.shape[3]),
        (kept, came),
        steps,
        w_query.shape[1],
        (parts_3[0],),
    )
    hidden = gated(
        [[parts_2[-1]] + from_2, [parts_3[-1]] + from_3],
        jax.ShapeDtypeStruct((local, size_x, steps, w_gate.shape[1]), BF16),
        (half_done,),
    )
    return (context, hidden)


def solution(mesh):
    return jax.shard_map(
        on_device,
        mesh=mesh,
        in_specs=(
            P("groups", "gx", None, "gy"),
            P("gy"),
            P("gy", "gx"),
            P("gy", "gx"),
            P("gy", "gx"),
            P("gy", "gx"),
            P(("groups", "gy"), "gx", None, None),
            P(("groups", "gy"), "gx"),
        ),
        out_specs=(P(("groups", "gy"), "gx", None, None), P(("groups", "gy"), None, None, "gx")),
        check_vma=False,
    )
```

```python
import functools

import jax
import jax.numpy as jnp
from jax import lax
from jax.experimental import pallas as pl
from jax.experimental.pallas import tpu as pltpu
from jax.sharding import PartitionSpec as P

D = 9216
HEADS = 24
HD = 256
EPSILON = 1e-05
MASKED = -1e30
MIB = 1024 * 1024
TILE = 256
SLOTS = 11
F32 = jnp.float32
BF16 = jnp.bfloat16


def whole(memory_space=pltpu.VMEM):
    return pl.BlockSpec(memory_space=memory_space)


def cost_of(*arrays):
    size = sum(a.size for a in arrays)
    return pl.CostEstimate(flops=size, bytes_accessed=size // 16, transcendentals=0)


def params():
    return pltpu.CompilerParams(vmem_limit_bytes=9 * MIB)


def stats_kernel(count, *refs):
    token_refs, (rows_ref, out_ref) = refs[:count], refs[-2:]
    tall, _, steps, features = token_refs[0].shape
    for index, ref in enumerate(token_refs):
        for t in range(tall):
            first = (index * tall + t) * steps
            rows_ref[first : first + steps] = ref[t, 0].astype(F32)
    floats = rows_ref[...]
    sums = jnp.sum(floats, axis=-1, keepdims=True)
    squares = jnp.sum(floats * floats, axis=-1, keepdims=True)
    lane = lax.broadcasted_iota(jnp.int32, out_ref.shape, 1)
    out_ref[...] = jnp.where(lane < 64, sums, squares)


def partial_stats(tokens, after):
    tall, _, steps, features = tokens[0].shape
    rows = len(tokens) * tall * steps
    return pl.pallas_call(
        functools.partial(stats_kernel, len(tokens)),
        out_shape=(pltpu.VMEM((rows, features), F32), pltpu.VMEM((rows, 128), F32)),
        in_specs=[whole()] * len(tokens) + [whole(pl.ANY)],
        out_specs=(whole(), whole()),
        compiler_params=params(),
        cost_estimate=cost_of(*tokens),
    )(*tokens, after)


def norm_kernel(source_ref, gain_ref, rows_ref, *refs):
    stat_refs, out_ref = refs[:-2], refs[-1]
    stats = stat_refs[0][...]
    for ref in stat_refs[1:]:
        stats = stats + ref[...]
    average = stats[:, 0:1] / D
    inverse_std = lax.rsqrt(stats[:, 64:65] / D - average * average + EPSILON)
    normed = ((rows_ref[...] - average) * inverse_std * gain_ref[...][None, :]).astype(BF16)
    rows = normed.shape[0]
    place = lax.broadcasted_iota(jnp.int32, (rows, rows), 1) == source_ref[...]
    out_ref[...] = jnp.dot(
        jnp.where(place, 1.0, 0.0).astype(BF16), normed, preferred_element_type=F32
    ).astype(BF16)


def normed_rows(source, gain, rows, stats, after):
    return pl.pallas_call(
        norm_kernel,
        out_shape=pltpu.VMEM(rows.shape, BF16),
        in_specs=[whole()] * (3 + len(stats)) + [whole(pl.ANY)],
        out_specs=whole(),
        compiler_params=params(),
        cost_estimate=cost_of(rows),
    )(source, gain, rows, *stats, after)


def combine_kernel(chips, small, skip, *refs):
    sent_ref, keep_ref = refs[:2]
    out_refs = refs[skip:]
    cols = keep_ref.shape[2]
    block = keep_ref.shape[1] // chips
    for index in range(chips):
        rows = slice(index * block, (index + 1) * block)
        total = keep_ref[:, rows] + sent_ref[:, rows, :cols].astype(F32)
        out_refs[index][:, :, :cols] = total.astype(out_refs[index].dtype)
        if small:
            sent = sent_ref[0, rows, cols:].astype(F32) + sent_ref[1, rows, cols:].astype(F32)
            total = refs[2][rows] + sent
            if index == chips - 1:
                out_refs[chips][...] = total
            else:
                store_split(out_refs[index], slice(cols, cols + small), total)


def combine(chips, sent, keep, keep_q=None, carry=None, after=()):
    small = 0 if keep_q is None else keep_q.shape[1]
    block = keep.shape[1] // chips
    out_shape = [pltpu.VMEM((2, block, sent.shape[2]), BF16)] * (chips - 1)
    out_shape.append(pltpu.VMEM((2, block, keep.shape[2]), F32))
    if small:
        out_shape.append(pltpu.VMEM((block, small), F32))
    args = (sent, keep, keep_q) if small else (sent, keep)
    extra = [*after] if carry is None else [*after, *in_vmem((carry,))]
    out_specs = [whole()] * len(out_shape)
    aliases = {}
    if carry is not None:
        aliases = {len(args) + len(after): len(out_shape)}
        out_shape.append(pltpu.VMEM(carry.shape, carry.dtype))
        out_specs.append(whole())
    return pl.pallas_call(
        functools.partial(combine_kernel, chips, small, len(args) + len(extra)),
        out_shape=out_shape,
        in_specs=[whole()] * len(args)
        + [whole(pl.ANY)] * len(after)
        + [whole()] * (len(extra) - len(after)),
        out_specs=out_specs,
        input_output_aliases=aliases,
        compiler_params=params(),
        cost_estimate=cost_of(*args),
    )(*args, *extra)


def query_rows_kernel(count, source_ref, *refs):
    term_refs, out_refs = refs[:-count], refs[-count:]
    total = term_refs[0][...]
    rows, cols = total.shape
    for ref in term_refs[1:]:
        first = ref.shape[2] - cols
        total = total + (ref[0, :, first:].astype(F32) + ref[1, :, first:].astype(F32))
    place = lax.broadcasted_iota(jnp.int32, (rows, rows), 1) == source_ref[...]
    turned = jnp.dot(
        jnp.where(place, 1.0, 0.0).astype(BF16), total.astype(BF16), preferred_element_type=F32
    )
    each = rows // count
    for index, ref in enumerate(out_refs):
        ref[0] = turned[index * each : (index + 1) * each].astype(BF16)


def query_rows(source, terms, count):
    rows, cols = terms[0].shape
    return pl.pallas_call(
        functools.partial(query_rows_kernel, count),
        out_shape=[pltpu.VMEM((1, rows // count, cols), BF16)] * count,
        in_specs=[whole()] * (1 + len(terms)),
        out_specs=[whole()] * count,
        compiler_params=params(),
        cost_estimate=cost_of(*terms),
    )(source, *terms)


def gated_kernel(counts, ready, *refs):
    out_ref = refs[-1]
    local, wide, steps, _ = out_ref.shape
    taken, first = ready, 0
    for ref in refs[:ready]:
        out_ref[:, :, :, : ref.shape[3]] = ref[...]
        first = ref.shape[3]
    for count in counts:
        total = refs[taken][...]
        cols = total.shape[2]
        for ref in refs[taken + 1 : taken + count]:
            total = total + ref[:, :, :cols].astype(F32)
        taken += count
        gate, up = total[0], total[1]
        hidden = gate / (1.0 + jnp.exp(-gate)) * up
        for row in range(local * wide):
            piece = hidden[row * steps : (row + 1) * steps].astype(BF16)
            out_ref[row // wide, row % wide, :, first : first + cols] = piece
        first += cols


def gated(chunks, out_shape, ready=(), after=()):
    terms = [term for chunk in chunks for term in chunk]
    return pl.pallas_call(
        functools.partial(gated_kernel, [len(chunk) for chunk in chunks], len(ready)),
        out_shape=out_shape,
        in_specs=[whole()] * (len(ready) + len(terms)) + [whole(pl.ANY)] * len(after),
        out_specs=whole(),
        compiler_params=params(),
        cost_estimate=cost_of(*ready, *terms),
    )(*ready, *terms, *after)


def in_hbm(arrays):
    return [pltpu.with_memory_space_constraint(a, pltpu.HBM) for a in arrays]


def in_vmem(arrays):
    return [pltpu.with_memory_space_constraint(a, pltpu.VMEM) for a in arrays]


def tile_copies(w_refs, tile, ring, sems):
    columns = pl.ds(pl.multiple_of(tile * TILE, TILE), TILE)
    slot = lax.rem(tile, SLOTS)
    return [
        pltpu.make_async_copy(
            ref.at[:, columns], ring.at[slot, :, index * TILE : (index + 1) * TILE], sems.at[slot, index]
        )
        for index, ref in enumerate(w_refs)
    ]


def each_tile(first, last, action):
    def body(tile, carry):
        action(tile)
        return carry

    lax.fori_loop(first, last, body, 0)


def ring_shape(features):
    return pltpu.VMEM((SLOTS, features, 2 * TILE), BF16)


def load_kernel(first, last, wg_ref, wu_ref, *refs):
    ring, sems = refs[-2:]

    def start(tile):
        for copy in tile_copies((wg_ref, wu_ref), tile, ring, sems):
            copy.start()

    def wait(tile):
        for copy in tile_copies((wg_ref, wu_ref), tile, ring, sems):
            copy.wait()

    each_tile(first, last, start)
    each_tile(first, last, wait)


def load(weights, first, last, ring, after):
    features = weights[0].shape[0]
    rings = [] if ring is None else in_vmem((ring,))
    return pl.pallas_call(
        functools.partial(load_kernel, first, last),
        out_shape=ring_shape(features),
        in_specs=[whole(pltpu.HBM)] * 2 + [whole()] * len(rings) + [whole(pl.ANY)] * len(after),
        out_specs=whole(),
        scratch_shapes=[pltpu.SemaphoreType.DMA((SLOTS, 2))],
        input_output_aliases={2: 0} if rings else {},
        compiler_params=params(),
        cost_estimate=pl.CostEstimate(
            flops=0, bytes_accessed=4 * features * TILE * (last - first), transcendentals=0
        ),
    )(*in_hbm(weights), *rings, *after)


def store_split(ref, columns, value):
    high = value.astype(BF16)
    ref[0, :, columns] = high
    ref[1, :, columns] = (value - high.astype(F32)).astype(BF16)


def multiply_tiles(first, tiles, held, following, x_ref, w_refs, ring, sems, send_ref, keep_ref):
    loads = tiles + following - held
    early = min(6, SLOTS - held, loads)

    def start(index):
        for copy in tile_copies(w_refs, first + held + index, ring, sems):
            copy.start()

    def wait(index):
        for copy in tile_copies(w_refs, first + held + index, ring, sems):
            copy.wait()

    def multiply(index):
        if held < tiles:

            @pl.when(index >= held)
            def _():
                wait(index - held)

        place = ring.at[lax.rem(first + index, SLOTS)]
        part = jnp.dot(x_ref[...], place[...], preferred_element_type=F32)
        half = part.shape[0] // 2
        columns = pl.ds(pl.multiple_of(index * TILE, TILE), TILE)
        for which in range(2):
            lanes = slice(which * TILE, (which + 1) * TILE)
            send_ref[which, :, columns] = part[:half, lanes].astype(BF16)
            keep_ref[which, :, columns] = part[half:, lanes]
        if early < loads:

            @pl.when(index + early < loads)
            def _():
                start(index + early)

    each_tile(0, early, start)
    each_tile(0, tiles, multiply)
    return lambda: each_tile(tiles - held, loads, wait)


def first_kernel(tiles, following, x_ref, wg_ref, wu_ref, wq_ref, wkv_ref, _, *refs):
    send_ref, keep_ref, keep_q_ref, ring, q_ref, kv_ref, small_sems, sems = refs
    half = x_ref.shape[0] // 2
    smalls = [
        pltpu.make_async_copy(wq_ref, q_ref, small_sems.at[0]),
        pltpu.make_async_copy(wkv_ref, kv_ref, small_sems.at[1]),
    ]
    for copy in smalls:
        copy.start()
    finish = multiply_tiles(0, tiles, tiles, following, x_ref, (wg_ref, wu_ref), ring, sems, send_ref, keep_ref)
    for copy in smalls:
        copy.wait()
    q_cols, kv_cols, base = q_ref.shape[1], kv_ref.shape[1], tiles * TILE
    piece = q_cols // 3

    def queries(index):
        columns = pl.ds(pl.multiple_of(index * piece, piece), piece)
        part = jnp.dot(x_ref[...], q_ref[:, columns], preferred_element_type=F32)
        sent = pl.ds(pl.multiple_of(base + index * piece, TILE), piece)
        store_split(send_ref, sent, part[:half])
        keep_q_ref[:, columns] = part[half:]

    each_tile(0, 3, queries)
    part = jnp.dot(x_ref[...], kv_ref[...], preferred_element_type=F32)
    store_split(send_ref, slice(base + q_cols, base + q_cols + kv_cols), part[:half])
    keep_q_ref[:, q_cols:] = part[half:]
    finish()


def first_sums(x, weights, w_query, w_keyval, ring, tiles, following):
    rows, features = x.shape
    cols, small = tiles * TILE, w_query.shape[1] + w_keyval.shape[1]
    return pl.pallas_call(
        functools.partial(first_kernel, tiles, following),
        out_shape=[
            pltpu.VMEM((2, rows // 2, cols + small), BF16),
            pltpu.VMEM((2, rows // 2, cols), F32),
            pltpu.VMEM((rows // 2, small), F32),
            ring_shape(features),
        ],
        in_specs=[whole()] + [whole(pltpu.HBM)] * 4 + [whole()],
        out_specs=[whole()] * 4,
        scratch_shapes=[
            pltpu.VMEM(w_query.shape, BF16),
            pltpu.VMEM(w_keyval.shape, BF16),
            pltpu.SemaphoreType.DMA((2,)),
            pltpu.SemaphoreType.DMA((SLOTS, 2)),
        ],
        input_output_aliases={5: 3},
        compiler_params=params(),
        cost_estimate=pl.CostEstimate(
            flops=2 * rows * features * (2 * cols + small),
            bytes_accessed=4 * features * cols,
            transcendentals=0,
        ),
    )(x, *in_hbm((*weights, w_query, w_keyval)), *in_vmem((ring,)))


def wide_kernel(first, tiles, held, following, x_ref, wg_ref, wu_ref, _, *refs):
    send_ref, keep_ref, ring, sems = refs[-4:]
    multiply_tiles(
        first, tiles, held, following, x_ref, (wg_ref, wu_ref), ring, sems, send_ref, keep_ref
    )()


def wide_sums(x, weights, ring, first, tiles, held, following, after):
    rows, features = x.shape
    cols = tiles * TILE
    return pl.pallas_call(
        functools.partial(wide_kernel, first, tiles, held, following),
        out_shape=[
            pltpu.VMEM((2, rows // 2, cols), BF16),
            pltpu.VMEM((2, rows // 2, cols), F32),
            ring_shape(features),
        ],
        in_specs=[whole(), whole(pltpu.HBM), whole(pltpu.HBM), whole()]
        + [whole(pl.ANY)] * len(after),
        out_specs=[whole()] * 3,
        scratch_shapes=[pltpu.SemaphoreType.DMA((SLOTS, 2))],
        input_output_aliases={3: 2},
        compiler_params=params(),
        cost_estimate=pl.CostEstimate(
            flops=4 * rows * features * cols,
            bytes_accessed=4 * features * TILE * (tiles + following - held),
            transcendentals=0,
        ),
    )(x, *in_hbm(weights), *in_vmem((ring,)), *after)


def merge_kernel(kept_ref, came_ref, keep_ref, send_ref):
    half = keep_ref.shape[1]
    count = kept_ref.shape[0]
    for index in range(2 * count):
        both = (kept_ref[index] if index < count else came_ref[index - count]).astype(F32)
        keep_ref[index] = both[:half].astype(BF16)
        send_ref[index] = both[half:].astype(BF16)


def merge(kept, came):
    count, rows, cols = kept.shape
    out = pltpu.VMEM((2 * count, rows // 2, cols), BF16)
    return pl.pallas_call(
        merge_kernel,
        out_shape=(out, out),
        in_specs=[whole()] * 2,
        out_specs=(whole(), whole()),
        compiler_params=params(),
        cost_estimate=cost_of(kept, came),
    )(kept, came)


def attend_kernel(count, steps, query_cols, slot_ref, lengths_ref, cache_ref, *refs):
    part_refs, (out_ref, held, fresh) = refs[:count], refs[-3:]
    each = part_refs[0].shape[0]
    for index, ref in enumerate(part_refs):
        for source in range(each):
            held[slot_ref[index * each + source]] = ref[source].astype(F32)
    count = count * each
    pair_cols = held.shape[2] - query_cols
    heads = query_cols // HD
    scale = HD ** (-0.5)
    batch, positions = cache_ref.shape[0], cache_ref.shape[1]
    fresh[...] = jnp.zeros_like(fresh)
    for b in range(batch):
        rows = pl.ds(b * steps, steps)
        for c in range(count):
            fresh[b, :steps, c * pair_cols : (c + 1) * pair_cols] = held[c, rows, query_cols:]
        queries = jnp.concatenate(
            [held[c, rows, h * HD : (h + 1) * HD] for c in range(count) for h in range(heads)],
            axis=0,
        ).astype(BF16)
        pairs = fresh[b].astype(BF16)
        dims = (((1,), (1,)), ((), ()))
        old = lax.dot_general(
            queries, cache_ref[b, :, :HD], dims, preferred_element_type=F32
        ) * scale
        position = lax.broadcasted_iota(jnp.int32, old.shape, 1)
        old = jnp.where(position < lengths_ref[b], old, MASKED)
        new = lax.dot_general(queries, pairs[:, :HD], dims, preferred_element_type=F32) * scale
        step = lax.broadcasted_iota(jnp.int32, new.shape, 0) % steps
        new = jnp.where(lax.broadcasted_iota(jnp.int32, new.shape, 1) <= step, new, MASKED)
        highest = jnp.maximum(
            jnp.max(old, axis=-1, keepdims=True), jnp.max(new, axis=-1, keepdims=True)
        )
        old = jnp.exp(old - highest)
        new = jnp.exp(new - highest)
        total = jnp.sum(old, axis=-1, keepdims=True) + jnp.sum(new, axis=-1, keepdims=True)
        context = jnp.dot(
            (old / total).astype(BF16), cache_ref[b, :, HD:], preferred_element_type=F32
        ) + jnp.dot((new / total).astype(BF16), pairs[:, HD:], preferred_element_type=F32)
        for h in range(HEADS):
            piece = context[h * steps : (h + 1) * steps].astype(BF16)
            out_ref[b, 0, :, h * HD : (h + 1) * HD] = piece


def attend(slots, lengths, cache, parts, steps, query_cols, after):
    batch = cache.shape[0]
    count = len(parts)
    sources, rows, cols = parts[0].shape
    return pl.pallas_call(
        functools.partial(attend_kernel, count, steps, query_cols),
        out_shape=jax.ShapeDtypeStruct((batch, 1, steps, HEADS * HD), BF16),
        in_specs=[whole(pltpu.SMEM), whole(pltpu.SMEM)] + [whole()] * (1 + count) + [whole(pl.ANY)] * len(after),
        out_specs=whole(),
        scratch_shapes=[
            pltpu.VMEM((count * sources, rows, cols), F32),
            pltpu.VMEM((batch, 8, 2 * HD), F32),
        ],
        compiler_params=params(),
        cost_estimate=pl.CostEstimate(
            flops=4 * batch * steps * HEADS * HD * cache.shape[1],
            bytes_accessed=2 * cache.size,
            transcendentals=batch * steps * HEADS * cache.shape[1],
        ),
    )(slots, lengths, cache, *parts, *after)


def on_device(tokens, gain, w_query, w_keyval, w_gate, w_up, cache, lengths):
    size_x, size_y = lax.axis_size("gx"), lax.axis_size("gy")
    chips = size_y // 2
    me_x, me_y = lax.axis_index("gx"), lax.axis_index("gy")
    tall, _, steps, features = tokens.shape
    local = cache.shape[0]
    block = local * size_x * steps

    def shift_y(value, by):
        return lax.ppermute(value, "gy", [(i, (i + by) % size_y) for i in range(size_y)])

    def swap_x(value, bits):
        return lax.ppermute(value, "gx", [(i, i ^ bits) for i in range(size_x)])

    def swap(value, bits=1):
        return lax.ppermute(value, "gy", [(i, i ^ bits) for i in range(size_y)])

    row = jnp.arange(2 * chips * block, dtype=jnp.int32)
    core = jnp.where(row < chips * block, 1 - me_y % 2, me_y % 2)
    chip = (me_y // 2 + 1 + row // block % chips) % chips
    sequence = (chip * 2 + core) * local + row % block // (size_x * steps)
    column = row // steps % size_x
    source = (me_x ^ column) * (tall * steps) + sequence * steps + row % steps
    source = source[:, None]
    row = jnp.arange(block, dtype=jnp.int32)
    to = me_x ^ (row // (local * steps))
    order = row // steps % local * (size_x * steps) + to * steps + row % steps
    order = order[:, None]
    bits, offsets = [], [0]
    while len(offsets) < size_x:
        bits.append(size_x // (2 * len(offsets)))
        offsets = offsets + [offset ^ bits[-1] for offset in offsets]
    number = jnp.arange(size_x, dtype=jnp.int32)
    slots = me_x ^ sum((number >> place & 1) * bit for place, bit in enumerate(bits))

    weights = (w_gate, w_up)
    tiles = w_gate.shape[1] // TILE
    before = [tiles * share // 36 for share in (7, 10)]
    bounds = [0, before[1]] + [tiles * share // 36 for share in (21, 29, 36)]
    ahead = [before[1]] + [max(1, tiles * share // 36) for share in (5, 4, 4)] + [0]
    gathered = [tokens] + [swap_x(tokens, bits) for bits in range(1, size_x)]
    ring = load(weights, 0, before[0], None, (source, order, slots))
    rows, stats = partial_stats(gathered, ring)
    every_stat = [stats] + [swap(stats, bits) for bits in range(1, size_y)]
    ring = load(weights, before[0], before[1], ring, (stats,))
    x = normed_rows(source, gain, rows, every_stat, ring)

    def chunk_sums(chunk, ring, after):
        first, count = bounds[chunk], bounds[chunk + 1] - bounds[chunk]
        return wide_sums(x, weights, ring, first, count, ahead[chunk], ahead[chunk + 1], after)

    def to_chips(parts):
        return [shift_y(part, 2 * by) for by, part in enumerate(parts[: chips - 1], 1)]

    send_0, keep_0, keep_q, ring = first_sums(
        x, weights, w_query, w_keyval, ring, bounds[1], ahead[1]
    )
    send_1, keep_1, ring = chunk_sums(1, ring, (send_0,))
    parts_0 = combine(chips, swap(send_0), keep_0, keep_q)
    from_0 = to_chips(parts_0)

    send_2, keep_2, ring = chunk_sums(2, ring, (parts_0[0], send_1))
    parts_1 = combine(chips, swap(send_1), keep_1)
    from_1 = to_chips(parts_1)
    kept, leaving = query_rows(order, [parts_0[-1]] + from_0, 2)
    came = swap_x(leaving, bits[0])

    send_3, keep_3, _ = chunk_sums(3, ring, (parts_1[0], kept, send_2))
    *parts_2, send_3 = combine(chips, swap(send_2), keep_2, None, send_3, (came, from_1[0]))
    from_2 = to_chips(parts_2)
    for bit in bits[1:]:
        kept, leaving = merge(kept, came)
        came = swap_x(leaving, bit)
    parts_3 = combine(chips, swap(send_3), keep_3)
    from_3 = to_chips(parts_3)
    half_done = gated(
        [[parts_0[chips - 1]] + from_0, [parts_1[-1]] + from_1],
        pltpu.VMEM((local, size_x, steps, bounds[2] * TILE), BF16),
        (),
        (parts_3[0],),
    )
    context = attend(
        slots,
        lengths.reshape(local),
        cache.reshape(local, cache.shape[2], cache.shape[3]),
        (kept, came),
        steps,
        w_query.shape[1],
        (parts_3[0],),
    )
    hidden = gated(
        [[parts_2[-1]] + from_2, [parts_3[-1]] + from_3],
        jax.ShapeDtypeStruct((local, size_x, steps, w_gate.shape[1]), BF16),
        (half_done,),
    )
    return (context, hidden)


def solution(mesh):
    return jax.shard_map(
        on_device,
        mesh=mesh,
        in_specs=(
            P("groups", "gx", None, "gy"),
            P("gy"),
            P("gy", "gx"),
            P("gy", "gx"),
            P("gy", "gx"),
            P("gy", "gx"),
            P(("groups", "gy"), "gx", None, None),
            P(("groups", "gy"), "gx"),
        ),
        out_specs=(P(("groups", "gy"), "gx", None, None), P(("groups", "gy"), None, None, "gx")),
        check_vma=False,
    )
```

```python
import functools

import jax
import jax.numpy as jnp
from jax import lax
from jax.experimental import pallas as pl
from jax.experimental.pallas import tpu as pltpu
from jax.sharding import PartitionSpec as P

D = 9216
HEADS = 24
HD = 256
EPSILON = 1e-05
MASKED = -1e30
MIB = 1024 * 1024
TILE = 256
SLOTS = 10
F32 = jnp.float32
BF16 = jnp.bfloat16


def whole(memory_space=pltpu.VMEM):
    return pl.BlockSpec(memory_space=memory_space)


def cost_of(*arrays):
    size = sum(a.size for a in arrays)
    return pl.CostEstimate(flops=size, bytes_accessed=size // 16, transcendentals=0)


def params():
    return pltpu.CompilerParams(vmem_limit_bytes=9 * MIB)


def stats_kernel(count, *refs):
    token_refs, (rows_ref, out_ref) = refs[:count], refs[-2:]
    tall, _, steps, features = token_refs[0].shape
    for index, ref in enumerate(token_refs):
        for t in range(tall):
            first = (index * tall + t) * steps
            rows_ref[first : first + steps] = ref[t, 0].astype(F32)
    floats = rows_ref[...]
    sums = jnp.sum(floats, axis=-1, keepdims=True)
    squares = jnp.sum(floats * floats, axis=-1, keepdims=True)
    lane = lax.broadcasted_iota(jnp.int32, out_ref.shape, 1)
    out_ref[...] = jnp.where(lane < 64, sums, squares)


def partial_stats(tokens, after):
    tall, _, steps, features = tokens[0].shape
    rows = len(tokens) * tall * steps
    return pl.pallas_call(
        functools.partial(stats_kernel, len(tokens)),
        out_shape=(pltpu.VMEM((rows, features), F32), pltpu.VMEM((rows, 128), F32)),
        in_specs=[whole()] * len(tokens) + [whole(pl.ANY)],
        out_specs=(whole(), whole()),
        compiler_params=params(),
        cost_estimate=cost_of(*tokens),
    )(*tokens, after)


def norm_kernel(source_ref, gain_ref, rows_ref, *refs):
    stat_refs, out_ref = refs[:-2], refs[-1]
    stats = stat_refs[0][...]
    for ref in stat_refs[1:]:
        stats = stats + ref[...]
    average = stats[:, 0:1] / D
    inverse_std = lax.rsqrt(stats[:, 64:65] / D - average * average + EPSILON)
    normed = ((rows_ref[...] - average) * inverse_std * gain_ref[...][None, :]).astype(BF16)
    rows = normed.shape[0]
    place = lax.broadcasted_iota(jnp.int32, (rows, rows), 1) == source_ref[...]
    out_ref[...] = jnp.dot(
        jnp.where(place, 1.0, 0.0).astype(BF16), normed, preferred_element_type=F32
    ).astype(BF16)


def normed_rows(source, gain, rows, stats, after):
    return pl.pallas_call(
        norm_kernel,
        out_shape=pltpu.VMEM(rows.shape, BF16),
        in_specs=[whole()] * (3 + len(stats)) + [whole(pl.ANY)],
        out_specs=whole(),
        compiler_params=params(),
        cost_estimate=cost_of(rows),
    )(source, gain, rows, *stats, after)


def combine_kernel(chips, small, skip, *refs):
    sent_ref, keep_ref = refs[:2]
    out_refs = refs[skip:]
    cols = keep_ref.shape[2]
    block = keep_ref.shape[1] // chips
    for index in range(chips):
        rows = slice(index * block, (index + 1) * block)
        total = keep_ref[:, rows] + sent_ref[:, rows, :cols].astype(F32)
        out_refs[index][:, :, :cols] = total.astype(out_refs[index].dtype)
        if small:
            sent = sent_ref[0, rows, cols:].astype(F32) + sent_ref[1, rows, cols:].astype(F32)
            total = refs[2][rows] + sent
            if index == chips - 1:
                out_refs[chips][...] = total
            else:
                store_split(out_refs[index], slice(cols, cols + small), total)


def combine(chips, sent, keep, keep_q=None, carry=None, after=()):
    small = 0 if keep_q is None else keep_q.shape[1]
    block = keep.shape[1] // chips
    out_shape = [pltpu.VMEM((2, block, sent.shape[2]), BF16)] * (chips - 1)
    out_shape.append(pltpu.VMEM((2, block, keep.shape[2]), F32))
    if small:
        out_shape.append(pltpu.VMEM((block, small), F32))
    args = (sent, keep, keep_q) if small else (sent, keep)
    extra = [*after] if carry is None else [*after, *in_vmem((carry,))]
    out_specs = [whole()] * len(out_shape)
    aliases = {}
    if carry is not None:
        aliases = {len(args) + len(after): len(out_shape)}
        out_shape.append(pltpu.VMEM(carry.shape, carry.dtype))
        out_specs.append(whole())
    return pl.pallas_call(
        functools.partial(combine_kernel, chips, small, len(args) + len(extra)),
        out_shape=out_shape,
        in_specs=[whole()] * len(args)
        + [whole(pl.ANY)] * len(after)
        + [whole()] * (len(extra) - len(after)),
        out_specs=out_specs,
        input_output_aliases=aliases,
        compiler_params=params(),
        cost_estimate=cost_of(*args),
    )(*args, *extra)


def query_rows_kernel(count, source_ref, *refs):
    term_refs, out_refs = refs[:-count], refs[-count:]
    total = term_refs[0][...]
    rows, cols = total.shape
    for ref in term_refs[1:]:
        first = ref.shape[2] - cols
        total = total + (ref[0, :, first:].astype(F32) + ref[1, :, first:].astype(F32))
    place = lax.broadcasted_iota(jnp.int32, (rows, rows), 1) == source_ref[...]
    turned = jnp.dot(
        jnp.where(place, 1.0, 0.0).astype(BF16), total.astype(BF16), preferred_element_type=F32
    )
    each = rows // count
    for index, ref in enumerate(out_refs):
        ref[0] = turned[index * each : (index + 1) * each].astype(BF16)


def query_rows(source, terms, count):
    rows, cols = terms[0].shape
    return pl.pallas_call(
        functools.partial(query_rows_kernel, count),
        out_shape=[pltpu.VMEM((1, rows // count, cols), BF16)] * count,
        in_specs=[whole()] * (1 + len(terms)),
        out_specs=[whole()] * count,
        compiler_params=params(),
        cost_estimate=cost_of(*terms),
    )(source, *terms)


def gated_kernel(counts, ready, *refs):
    out_ref = refs[-1]
    local, wide, steps, _ = out_ref.shape
    taken, first = ready, 0
    for ref in refs[:ready]:
        out_ref[:, :, :, : ref.shape[3]] = ref[...]
        first = ref.shape[3]
    for count in counts:
        total = refs[taken][...]
        cols = total.shape[2]
        for ref in refs[taken + 1 : taken + count]:
            total = total + ref[:, :, :cols].astype(F32)
        taken += count
        gate, up = total[0], total[1]
        hidden = gate / (1.0 + jnp.exp(-gate)) * up
        for row in range(local * wide):
            piece = hidden[row * steps : (row + 1) * steps].astype(BF16)
            out_ref[row // wide, row % wide, :, first : first + cols] = piece
        first += cols


def gated(chunks, out_shape, ready=(), after=()):
    terms = [term for chunk in chunks for term in chunk]
    return pl.pallas_call(
        functools.partial(gated_kernel, [len(chunk) for chunk in chunks], len(ready)),
        out_shape=out_shape,
        in_specs=[whole()] * (len(ready) + len(terms)) + [whole(pl.ANY)] * len(after),
        out_specs=whole(),
        compiler_params=params(),
        cost_estimate=cost_of(*ready, *terms),
    )(*ready, *terms, *after)


def in_hbm(arrays):
    return [pltpu.with_memory_space_constraint(a, pltpu.HBM) for a in arrays]


def in_vmem(arrays):
    return [pltpu.with_memory_space_constraint(a, pltpu.VMEM) for a in arrays]


def tile_copies(w_refs, tile, ring, sems):
    columns = pl.ds(pl.multiple_of(tile * TILE, TILE), TILE)
    slot = lax.rem(tile, SLOTS)
    return [
        pltpu.make_async_copy(
            ref.at[:, columns], ring.at[slot, :, index * TILE : (index + 1) * TILE], sems.at[slot, index]
        )
        for index, ref in enumerate(w_refs)
    ]


def each_tile(first, last, action):
    def body(tile, carry):
        action(tile)
        return carry

    lax.fori_loop(first, last, body, 0)


def ring_shape(features):
    return pltpu.VMEM((SLOTS, features, 2 * TILE), BF16)


def load_kernel(first, last, wg_ref, wu_ref, *refs):
    ring, sems = refs[-2:]

    def start(tile):
        for copy in tile_copies((wg_ref, wu_ref), tile, ring, sems):
            copy.start()

    def wait(tile):
        for copy in tile_copies((wg_ref, wu_ref), tile, ring, sems):
            copy.wait()

    each_tile(first, last, start)
    each_tile(first, last, wait)


def load(weights, first, last, ring, after):
    features = weights[0].shape[0]
    rings = [] if ring is None else in_vmem((ring,))
    return pl.pallas_call(
        functools.partial(load_kernel, first, last),
        out_shape=ring_shape(features),
        in_specs=[whole(pltpu.HBM)] * 2 + [whole()] * len(rings) + [whole(pl.ANY)] * len(after),
        out_specs=whole(),
        scratch_shapes=[pltpu.SemaphoreType.DMA((SLOTS, 2))],
        input_output_aliases={2: 0} if rings else {},
        compiler_params=params(),
        cost_estimate=pl.CostEstimate(
            flops=0, bytes_accessed=4 * features * TILE * (last - first), transcendentals=0
        ),
    )(*in_hbm(weights), *rings, *after)


def store_split(ref, columns, value):
    high = value.astype(BF16)
    ref[0, :, columns] = high
    ref[1, :, columns] = (value - high.astype(F32)).astype(BF16)


def multiply_tiles(first, tiles, held, following, x_ref, w_refs, ring, sems, send_ref, keep_ref):
    loads = tiles + following - held
    early = min(6, SLOTS - held, loads)

    def start(index):
        for copy in tile_copies(w_refs, first + held + index, ring, sems):
            copy.start()

    def wait(index):
        for copy in tile_copies(w_refs, first + held + index, ring, sems):
            copy.wait()

    def multiply(index):
        if held < tiles:

            @pl.when(index >= held)
            def _():
                wait(index - held)

        place = ring.at[lax.rem(first + index, SLOTS)]
        part = jnp.dot(x_ref[...], place[...], preferred_element_type=F32)
        half = part.shape[0] // 2
        columns = pl.ds(pl.multiple_of(index * TILE, TILE), TILE)
        for which in range(2):
            lanes = slice(which * TILE, (which + 1) * TILE)
            send_ref[which, :, columns] = part[:half, lanes].astype(BF16)
            keep_ref[which, :, columns] = part[half:, lanes]
        if early < loads:

            @pl.when(index + early < loads)
            def _():
                start(index + early)

    each_tile(0, early, start)
    each_tile(0, tiles, multiply)
    return lambda: each_tile(tiles - held, loads, wait)


def first_kernel(tiles, following, x_ref, wg_ref, wu_ref, wq_ref, wkv_ref, _, *refs):
    send_ref, keep_ref, keep_q_ref, ring, q_ref, kv_ref, small_sems, sems = refs
    half = x_ref.shape[0] // 2
    smalls = [
        pltpu.make_async_copy(wq_ref, q_ref, small_sems.at[0]),
        pltpu.make_async_copy(wkv_ref, kv_ref, small_sems.at[1]),
    ]
    for copy in smalls:
        copy.start()
    finish = multiply_tiles(0, tiles, tiles, following, x_ref, (wg_ref, wu_ref), ring, sems, send_ref, keep_ref)
    for copy in smalls:
        copy.wait()
    q_cols, kv_cols, base = q_ref.shape[1], kv_ref.shape[1], tiles * TILE
    piece = q_cols // 3

    def queries(index):
        columns = pl.ds(pl.multiple_of(index * piece, piece), piece)
        part = jnp.dot(x_ref[...], q_ref[:, columns], preferred_element_type=F32)
        sent = pl.ds(pl.multiple_of(base + index * piece, TILE), piece)
        store_split(send_ref, sent, part[:half])
        keep_q_ref[:, columns] = part[half:]

    each_tile(0, 3, queries)
    part = jnp.dot(x_ref[...], kv_ref[...], preferred_element_type=F32)
    store_split(send_ref, slice(base + q_cols, base + q_cols + kv_cols), part[:half])
    keep_q_ref[:, q_cols:] = part[half:]
    finish()


def first_sums(x, weights, w_query, w_keyval, ring, tiles, following):
    rows, features = x.shape
    cols, small = tiles * TILE, w_query.shape[1] + w_keyval.shape[1]
    return pl.pallas_call(
        functools.partial(first_kernel, tiles, following),
        out_shape=[
            pltpu.VMEM((2, rows // 2, cols + small), BF16),
            pltpu.VMEM((2, rows // 2, cols), F32),
            pltpu.VMEM((rows // 2, small), F32),
            ring_shape(features),
        ],
        in_specs=[whole()] + [whole(pltpu.HBM)] * 4 + [whole()],
        out_specs=[whole()] * 4,
        scratch_shapes=[
            pltpu.VMEM(w_query.shape, BF16),
            pltpu.VMEM(w_keyval.shape, BF16),
            pltpu.SemaphoreType.DMA((2,)),
            pltpu.SemaphoreType.DMA((SLOTS, 2)),
        ],
        input_output_aliases={5: 3},
        compiler_params=params(),
        cost_estimate=pl.CostEstimate(
            flops=2 * rows * features * (2 * cols + small),
            bytes_accessed=4 * features * cols,
            transcendentals=0,
        ),
    )(x, *in_hbm((*weights, w_query, w_keyval)), *in_vmem((ring,)))


def wide_kernel(first, tiles, held, following, x_ref, wg_ref, wu_ref, _, *refs):
    send_ref, keep_ref, ring, sems = refs[-4:]
    multiply_tiles(
        first, tiles, held, following, x_ref, (wg_ref, wu_ref), ring, sems, send_ref, keep_ref
    )()


def wide_sums(x, weights, ring, first, tiles, held, following, after):
    rows, features = x.shape
    cols = tiles * TILE
    return pl.pallas_call(
        functools.partial(wide_kernel, first, tiles, held, following),
        out_shape=[
            pltpu.VMEM((2, rows // 2, cols), BF16),
            pltpu.VMEM((2, rows // 2, cols), F32),
            ring_shape(features),
        ],
        in_specs=[whole(), whole(pltpu.HBM), whole(pltpu.HBM), whole()]
        + [whole(pl.ANY)] * len(after),
        out_specs=[whole()] * 3,
        scratch_shapes=[pltpu.SemaphoreType.DMA((SLOTS, 2))],
        input_output_aliases={3: 2},
        compiler_params=params(),
        cost_estimate=pl.CostEstimate(
            flops=4 * rows * features * cols,
            bytes_accessed=4 * features * TILE * (tiles + following - held),
            transcendentals=0,
        ),
    )(x, *in_hbm(weights), *in_vmem((ring,)), *after)


def merge_kernel(kept_ref, came_ref, keep_ref, send_ref):
    half = keep_ref.shape[1]
    count = kept_ref.shape[0]
    for index in range(2 * count):
        both = (kept_ref[index] if index < count else came_ref[index - count]).astype(F32)
        keep_ref[index] = both[:half].astype(BF16)
        send_ref[index] = both[half:].astype(BF16)


def merge(kept, came):
    count, rows, cols = kept.shape
    out = pltpu.VMEM((2 * count, rows // 2, cols), BF16)
    return pl.pallas_call(
        merge_kernel,
        out_shape=(out, out),
        in_specs=[whole()] * 2,
        out_specs=(whole(), whole()),
        compiler_params=params(),
        cost_estimate=cost_of(kept, came),
    )(kept, came)


def attend_kernel(count, steps, query_cols, slot_ref, lengths_ref, cache_ref, *refs):
    part_refs, (out_ref, held, fresh) = refs[:count], refs[-3:]
    each = part_refs[0].shape[0]
    for index, ref in enumerate(part_refs):
        for source in range(each):
            held[slot_ref[index * each + source]] = ref[source].astype(F32)
    count = count * each
    pair_cols = held.shape[2] - query_cols
    heads = query_cols // HD
    scale = HD ** (-0.5)
    batch, positions = cache_ref.shape[0], cache_ref.shape[1]
    fresh[...] = jnp.zeros_like(fresh)
    for b in range(batch):
        rows = pl.ds(b * steps, steps)
        for c in range(count):
            fresh[b, :steps, c * pair_cols : (c + 1) * pair_cols] = held[c, rows, query_cols:]
        queries = jnp.concatenate(
            [held[c, rows, h * HD : (h + 1) * HD] for c in range(count) for h in range(heads)],
            axis=0,
        ).astype(BF16)
        pairs = fresh[b].astype(BF16)
        dims = (((1,), (1,)), ((), ()))
        old = lax.dot_general(
            queries, cache_ref[b, :, :HD], dims, preferred_element_type=F32
        ) * scale
        position = lax.broadcasted_iota(jnp.int32, old.shape, 1)
        old = jnp.where(position < lengths_ref[b], old, MASKED)
        new = lax.dot_general(queries, pairs[:, :HD], dims, preferred_element_type=F32) * scale
        step = lax.broadcasted_iota(jnp.int32, new.shape, 0) % steps
        new = jnp.where(lax.broadcasted_iota(jnp.int32, new.shape, 1) <= step, new, MASKED)
        highest = jnp.maximum(
            jnp.max(old, axis=-1, keepdims=True), jnp.max(new, axis=-1, keepdims=True)
        )
        old = jnp.exp(old - highest)
        new = jnp.exp(new - highest)
        total = jnp.sum(old, axis=-1, keepdims=True) + jnp.sum(new, axis=-1, keepdims=True)
        context = jnp.dot(
            (old / total).astype(BF16), cache_ref[b, :, HD:], preferred_element_type=F32
        ) + jnp.dot((new / total).astype(BF16), pairs[:, HD:], preferred_element_type=F32)
        for h in range(HEADS):
            piece = context[h * steps : (h + 1) * steps].astype(BF16)
            out_ref[b, 0, :, h * HD : (h + 1) * HD] = piece


def attend(slots, lengths, cache, parts, steps, query_cols, after):
    batch = cache.shape[0]
    count = len(parts)
    sources, rows, cols = parts[0].shape
    return pl.pallas_call(
        functools.partial(attend_kernel, count, steps, query_cols),
        out_shape=jax.ShapeDtypeStruct((batch, 1, steps, HEADS * HD), BF16),
        in_specs=[whole(pltpu.SMEM), whole(pltpu.SMEM)] + [whole()] * (1 + count) + [whole(pl.ANY)] * len(after),
        out_specs=whole(),
        scratch_shapes=[
            pltpu.VMEM((count * sources, rows, cols), F32),
            pltpu.VMEM((batch, 8, 2 * HD), F32),
        ],
        compiler_params=params(),
        cost_estimate=pl.CostEstimate(
            flops=4 * batch * steps * HEADS * HD * cache.shape[1],
            bytes_accessed=2 * cache.size,
            transcendentals=batch * steps * HEADS * cache.shape[1],
        ),
    )(slots, lengths, cache, *parts, *after)


def on_device(tokens, gain, w_query, w_keyval, w_gate, w_up, cache, lengths):
    size_x, size_y = lax.axis_size("gx"), lax.axis_size("gy")
    chips = size_y // 2
    me_x, me_y = lax.axis_index("gx"), lax.axis_index("gy")
    tall, _, steps, features = tokens.shape
    local = cache.shape[0]
    block = local * size_x * steps

    def shift_y(value, by):
        return lax.ppermute(value, "gy", [(i, (i + by) % size_y) for i in range(size_y)])

    def swap_x(value, bits):
        return lax.ppermute(value, "gx", [(i, i ^ bits) for i in range(size_x)])

    def swap(value, bits=1):
        return lax.ppermute(value, "gy", [(i, i ^ bits) for i in range(size_y)])

    row = jnp.arange(2 * chips * block, dtype=jnp.int32)
    core = jnp.where(row < chips * block, 1 - me_y % 2, me_y % 2)
    chip = (me_y // 2 + 1 + row // block % chips) % chips
    sequence = (chip * 2 + core) * local + row % block // (size_x * steps)
    column = row // steps % size_x
    source = (me_x ^ column) * (tall * steps) + sequence * steps + row % steps
    source = source[:, None]
    row = jnp.arange(block, dtype=jnp.int32)
    to = me_x ^ (row // (local * steps))
    order = row // steps % local * (size_x * steps) + to * steps + row % steps
    order = order[:, None]
    bits, offsets = [], [0]
    while len(offsets) < size_x:
        bits.append(size_x // (2 * len(offsets)))
        offsets = offsets + [offset ^ bits[-1] for offset in offsets]
    number = jnp.arange(size_x, dtype=jnp.int32)
    slots = me_x ^ sum((number >> place & 1) * bit for place, bit in enumerate(bits))

    weights = (w_gate, w_up)
    tiles = w_gate.shape[1] // TILE
    before = [tiles * share // 36 for share in (7, 9)]
    bounds = [0, before[1]] + [tiles * share // 36 for share in (21, 30, 36)]
    ahead = [before[1]] + [max(1, tiles * share // 36) for share in (5, 4, 4)] + [0]
    gathered = [tokens] + [swap_x(tokens, bits) for bits in range(1, size_x)]
    ring = load(weights, 0, before[0], None, (source, order, slots))
    rows, stats = partial_stats(gathered, ring)
    every_stat = [stats] + [swap(stats, bits) for bits in range(1, size_y)]
    ring = load(weights, before[0], before[1], ring, (stats,))
    x = normed_rows(source, gain, rows, every_stat, ring)

    def chunk_sums(chunk, ring, after):
        first, count = bounds[chunk], bounds[chunk + 1] - bounds[chunk]
        return wide_sums(x, weights, ring, first, count, ahead[chunk], ahead[chunk + 1], after)

    def to_chips(parts):
        return [shift_y(part, 2 * by) for by, part in enumerate(parts[: chips - 1], 1)]

    send_0, keep_0, keep_q, ring = first_sums(
        x, weights, w_query, w_keyval, ring, bounds[1], ahead[1]
    )
    send_1, keep_1, ring = chunk_sums(1, ring, (send_0,))
    parts_0 = combine(chips, swap(send_0), keep_0, keep_q)
    from_0 = to_chips(parts_0)

    send_2, keep_2, ring = chunk_sums(2, ring, (parts_0[0], send_1))
    parts_1 = combine(chips, swap(send_1), keep_1)
    from_1 = to_chips(parts_1)
    kept, leaving = query_rows(order, [parts_0[-1]] + from_0, 2)
    came = swap_x(leaving, bits[0])

    send_3, keep_3, _ = chunk_sums(3, ring, (parts_1[0], kept, send_2))
    *parts_2, send_3 = combine(chips, swap(send_2), keep_2, None, send_3, (came, from_1[0]))
    from_2 = to_chips(parts_2)
    for bit in bits[1:]:
        kept, leaving = merge(kept, came)
        came = swap_x(leaving, bit)
    parts_3 = combine(chips, swap(send_3), keep_3)
    from_3 = to_chips(parts_3)
    half_done = gated(
        [[parts_0[chips - 1]] + from_0, [parts_1[-1]] + from_1],
        pltpu.VMEM((local, size_x, steps, bounds[2] * TILE), BF16),
        (),
        (parts_3[0],),
    )
    context = attend(
        slots,
        lengths.reshape(local),
        cache.reshape(local, cache.shape[2], cache.shape[3]),
        (kept, came),
        steps,
        w_query.shape[1],
        (parts_3[0],),
    )
    hidden = gated(
        [[parts_2[-1]] + from_2, [parts_3[-1]] + from_3],
        jax.ShapeDtypeStruct((local, size_x, steps, w_gate.shape[1]), BF16),
        (half_done,),
    )
    return (context, hidden)


def solution(mesh):
    return jax.shard_map(
        on_device,
        mesh=mesh,
        in_specs=(
            P("groups", "gx", None, "gy"),
            P("gy"),
            P("gy", "gx"),
            P("gy", "gx"),
            P("gy", "gx"),
            P("gy", "gx"),
            P(("groups", "gy"), "gx", None, None),
            P(("groups", "gy"), "gx"),
        ),
        out_specs=(P(("groups", "gy"), "gx", None, None), P(("groups", "gy"), None, None, "gx")),
        check_vma=False,
    )
```
